32 devices in a mesh: gx: 4 (over y, x), gy: 4 (over z), gz: 2 (over core).
Axes of the slice: x: 2, y: 2, z: 4, core: 2. Of those that a mesh axis runs over, the one named last changes fastest.
Arguments:
- features: bfloat16 [32, 16, 8, 512], P('gx', 'gy', 'gz'), may hold values from -31 to 31, as said below
- grad_y: bfloat16 [32, 16, 8, 512], P('gx', 'gy', 'gz'), may hold values from -6 to 6
- attn_out: bfloat16 [32, 16, 8, 512], P('gx', 'gy', 'gz'), may hold values from -3 to 3
- w_query: bfloat16 [512, 512], P('gz'), may hold values from -0.25 to 0.25
- w_key: bfloat16 [512, 512], P('gz'), may hold values from -0.25 to 0.25
- w_value: bfloat16 [512, 512], P('gz'), may hold values from -0.25 to 0.25
- w_out: bfloat16 [512, 512], P('gz'), may hold values from -0.25 to 0.25
Outputs:
- grad_x: bfloat16 [32, 16, 8, 512], P('gx', 'gy', 'gz')
- grad_query: float32 [512, 512], P('gz')
- grad_key: float32 [512, 512], P('gz')
- grad_value: float32 [512, 512], P('gz')
- grad_out: float32 [512, 512], P('gz')
The draws below stay inside these ranges and needn't reach their ends.
Inputs may be any that keep to these rules, and one draw needn't show every extreme that they name: features of the patch tokens.
All inputs are finite; a program needn't handle non-finite values.
Results may differ from the reference program's by a relative error of at most 0.018.
Values may be sent and summed in bfloat16 or wider, within the bound.
No kernel may reach another device: no remote copies, remote signals or barrier semaphores. Data moves between devices by JAX's collectives and lax.ppermute only.
A program may use at most 64 MiB of HBM per device.

```python
import math
import jax
import jax.numpy as jnp
from jax import lax

D = 512
HEADS = 8
B = 8
NX = 32
NY = 16
NZ = 8


def draw_features(key, part):
    first, second = jax.random.split(key, 2)
    field_shape = (NX, NY, NZ, D)
    token_scale = jnp.exp(jax.random.uniform(second, (NX, NY, NZ, 1), jnp.float32, math.log(0.3), math.log(3.0)))
    values = jax.random.truncated_normal(first, -4.0, 4.0, field_shape, jnp.float32) * token_scale
    return values.astype(jnp.bfloat16)


def levels(key, shape, cuts, least, largest):
    loudness = 1.0
    for axis_at, shards_of in cuts:
        draws = jax.random.uniform(jax.random.fold_in(jax.random.fold_in(key, 6), axis_at), (shards_of,), jnp.float32, least / len(cuts), largest / len(cuts))
        loudness = loudness * jnp.repeat(jnp.exp(draws), shape[axis_at] // shards_of).reshape((-1,) + (1,) * (len(shape) - 1 - axis_at))
    return loudness


def noise(stream_key, extent, scale, limit, shards=(), held_as=jnp.bfloat16):
    result = jax.random.normal(stream_key, extent, jnp.float32) * scale
    if len(shards) > 0:
        result = levels(stream_key, extent, shards, -0.22, 0.18) * result
    return jnp.clip(result, min=-limit, max=limit).astype(held_as)


def setup_inputs(seed: int = 0) -> dict:
    key_of = jax.random.split(jax.random.key(seed), 8)
    features = draw_features(jax.random.fold_in(key_of[7], 71), 0)
    grad_y = noise(key_of[1], (NX, NY, NZ, D), 1.0, 6.0, ((0, 4), (1, 4), (2, 2)))
    attn_out = noise(key_of[2], (NX, NY, NZ, D), 0.5, 3.0, ((0, 4), (1, 4), (2, 2)))
    w_query = noise(key_of[3], (D, D), D ** -0.5, 0.25, ((0, 2),))
    w_key = noise(key_of[4], (D, D), D ** -0.5, 0.25, ((0, 2),))
    w_value = noise(key_of[5], (D, D), D ** -0.5, 0.25, ((0, 2),))
    w_out = noise(key_of[6], (D, D), D ** -0.5, 0.25, ((0, 2),))
    return dict(features=features, grad_y=grad_y, attn_out=attn_out, w_query=w_query, w_key=w_key, w_value=w_value, w_out=w_out)


NEIGHBOURS = ((0, 0, 0), (-1, 0, 0), (1, 0, 0), (0, -1, 0), (0, 1, 0), (0, 0, -1), (0, 0, 1))

def to_blocks(field, block_edge):
    count_x = field.shape[0] // block_edge
    count_y = field.shape[1] // block_edge
    count_z = field.shape[2] // block_edge
    width = field.shape[3]
    split_field = field.reshape(count_x, block_edge, count_y, block_edge, count_z, block_edge, width)
    return split_field.transpose(0, 2, 4, 1, 3, 5, 6).reshape(count_x, count_y, count_z, block_edge ** 3, width)

def from_blocks(blocks, block_edge):
    count_x, count_y, count_z, unused, width = blocks.shape
    split_field = blocks.reshape(count_x, count_y, count_z, block_edge, block_edge, block_edge, width)
    return split_field.transpose(0, 3, 1, 4, 2, 5, 6).reshape(count_x * block_edge, count_y * block_edge, count_z * block_edge, width)

def reference(features, grad_y, attn_out, w_query, w_key, w_value, w_out):
    field_shape = features.shape
    width = field_shape[3]
    head_dim = width // HEADS
    score_scale = 1.0 / math.sqrt(head_dim)
    block_tokens = B ** 3
    feature_rows = features.reshape(-1, width)
    dy_rows = grad_y.reshape(-1, width)
    saved_rows = attn_out.reshape(-1, width)
    query = jnp.dot(feature_rows, w_query, preferred_element_type=jnp.float32).astype(jnp.bfloat16)
    key_rows = jnp.dot(feature_rows, w_key, preferred_element_type=jnp.float32).astype(jnp.bfloat16)
    value_rows = jnp.dot(feature_rows, w_value, preferred_element_type=jnp.float32).astype(jnp.bfloat16)
    out_grad = jnp.dot(dy_rows, w_out.T, preferred_element_type=jnp.float32).astype(jnp.bfloat16)
    query_blocks = to_blocks(query.reshape(field_shape), B)
    key_blocks = to_blocks(key_rows.reshape(field_shape), B)
    value_blocks = to_blocks(value_rows.reshape(field_shape), B)
    grad_blocks = to_blocks(out_grad.reshape(field_shape), B)
    saved_blocks = to_blocks(attn_out, B)
    count_x, count_y, count_z = query_blocks.shape[:3]

    def block_step(carry, index):
        key_total, value_total = carry
        place_x = index // (count_y * count_z)
        place_y = index // count_z % count_y
        place_z = index % count_z
        spots = []
        for step_x, step_y, step_z in NEIGHBOURS:
            spots.append(((place_x + step_x) % count_x, (place_y + step_y) % count_y, (place_z + step_z) % count_z))
        near_keys = jnp.concatenate([key_blocks[spot] for spot in spots])
        near_values = jnp.concatenate([value_blocks[spot] for spot in spots])
        key_heads = near_keys.astype(jnp.float32).reshape(7 * block_tokens, HEADS, head_dim)
        value_heads = near_values.astype(jnp.float32).reshape(7 * block_tokens, HEADS, head_dim)
        query_heads = query_blocks[place_x, place_y, place_z].astype(jnp.float32).reshape(block_tokens, HEADS, head_dim)
        grad_heads = grad_blocks[place_x, place_y, place_z].astype(jnp.float32).reshape(block_tokens, HEADS, head_dim)
        saved_heads = saved_blocks[place_x, place_y, place_z].astype(jnp.float32).reshape(block_tokens, HEADS, head_dim)
        scores = jnp.einsum('qhd,khd->hqk', query_heads, key_heads) * score_scale
        row_top = lax.optimization_barrier(jnp.max(scores, axis=2, keepdims=True))
        log_total = row_top + jnp.log(lax.optimization_barrier(jnp.sum(jnp.exp(scores - row_top), axis=2, keepdims=True)))
        attn_prob = jnp.exp(scores - log_total).astype(jnp.bfloat16)
        prob_grad = jnp.einsum('qhd,khd->hqk', grad_heads, value_heads)
        row_delta = lax.optimization_barrier(jnp.sum(grad_heads * saved_heads, axis=2)).T[:, :, None]
        score_grad = (attn_prob.astype(jnp.float32) * (prob_grad - row_delta) * score_scale).astype(jnp.bfloat16)
        query_grad = jnp.einsum('hqk,khd->qhd', score_grad.astype(jnp.float32), key_heads).reshape(block_tokens, width).astype(jnp.bfloat16)
        key_part = jnp.einsum('hqk,qhd->khd', score_grad.astype(jnp.float32), query_heads).astype(jnp.bfloat16).reshape(7, block_tokens, width)
        value_part = jnp.einsum('hqk,qhd->khd', attn_prob.astype(jnp.float32), grad_heads).astype(jnp.bfloat16).reshape(7, block_tokens, width)
        for slot_index in range(7):
            spot = spots[slot_index]
            key_total = key_total.at[spot].add(key_part[slot_index].astype(jnp.float32))
            value_total = value_total.at[spot].add(value_part[slot_index].astype(jnp.float32))
        return ((key_total, value_total), query_grad)
    zero_blocks = jnp.zeros(query_blocks.shape, jnp.float32)
    block_count = count_x * count_y * count_z
    totals, query_grads = lax.scan(block_step, (zero_blocks, zero_blocks), jnp.arange(block_count, dtype=jnp.int32))
    query_act_grad = from_blocks(query_grads.reshape(query_blocks.shape), B).reshape(-1, width)
    key_act_grad = from_blocks(totals[0].astype(jnp.bfloat16), B).reshape(-1, width)
    value_act_grad = from_blocks(totals[1].astype(jnp.bfloat16), B).reshape(-1, width)
    grad_x = jnp.dot(query_act_grad, w_query.T, preferred_element_type=jnp.float32)
    grad_x = grad_x + jnp.dot(key_act_grad, w_key.T, preferred_element_type=jnp.float32)
    grad_x = grad_x + jnp.dot(value_act_grad, w_value.T, preferred_element_type=jnp.float32)
    grad_x = grad_x.astype(jnp.bfloat16).reshape(field_shape)
    grad_query = jnp.dot(feature_rows.T, query_act_grad, preferred_element_type=jnp.float32)
    grad_key = jnp.dot(feature_rows.T, key_act_grad, preferred_element_type=jnp.float32)
    grad_value = jnp.dot(feature_rows.T, value_act_grad, preferred_element_type=jnp.float32)
    grad_out = jnp.dot(saved_rows.T, dy_rows, preferred_element_type=jnp.float32)
    return (grad_x, grad_query, grad_key, grad_value, grad_out)
```

```python
import functools
import math

import jax
import jax.numpy as jnp
from jax import lax
from jax.experimental import pallas as pl
from jax.experimental.pallas import tpu as pltpu
from jax.sharding import PartitionSpec as P

HEADS = 8
PART = 128
BF = jnp.bfloat16
F32 = jnp.float32
VMEM_BYTES = 52 * 1024 * 1024


def from_partner(block, axis):
    route = [(index, index ^ 1) for index in range(lax.axis_size(axis))]
    return lax.ppermute(block, axis, route)


def shifted(value, axis, steps):
    count = lax.axis_size(axis)
    return lax.ppermute(value, axis, [(source, (source + steps) % count) for source in range(count)])


def plane_swap(value, flip_x, flip_y):
    count_x, count_y = lax.axis_size("gx"), lax.axis_size("gy")
    route = []
    for at_x in range(count_x):
        for at_y in range(count_y):
            route.append((at_x * count_y + at_y, (at_x ^ flip_x) * count_y + (at_y ^ flip_y)))
    return lax.ppermute(value, ("gx", "gy"), route)


def dot_nn(left, right):
    return lax.dot_general(left, right, (((1,), (0,)), ((), ())), preferred_element_type=F32)


def dot_nt(left, right):
    return lax.dot_general(left, right, (((1,), (1,)), ((), ())), preferred_element_type=F32)


def dot_tn(left, right):
    return lax.dot_general(left, right, (((0,), (0,)), ((), ())), preferred_element_type=F32)


def columns(start):
    return pl.ds(pl.multiple_of(start, PART), PART)


def call(kernel, out_shape, args, scratch=(), flops=1e6, moved=1e6, exps=0):
    return pl.pallas_call(
        kernel,
        out_shape=out_shape,
        scratch_shapes=list(scratch),
        compiler_params=pltpu.CompilerParams(vmem_limit_bytes=VMEM_BYTES),
        cost_estimate=pl.CostEstimate(
            flops=int(flops), bytes_accessed=int(moved), transcendentals=int(exps)
        ),
    )(*args)


def shape_of(dims, dtype=BF):
    return jax.ShapeDtypeStruct(dims, dtype)


def pack_kernel(feat_ref, dy_ref, saved_ref, pair_ref, own_ref):
    y_bit = lax.axis_index("gy") % 2
    z_bit = lax.axis_index("gz") % 2
    tokens, width = feat_ref.shape
    last = 2 * width + PART
    for out in (pair_ref, own_ref):
        out[:, PART : PART + width] = feat_ref[...]
        out[:, PART + width : last] = dy_ref[...]
    pair_ref[:, 0:PART] = saved_ref[:, columns((z_bit * 2 + 1 - y_bit) * PART)]
    pair_ref[:, last:] = saved_ref[:, columns(((1 - z_bit) * 2 + 1 - y_bit) * PART)]
    own_ref[:, 0:PART] = saved_ref[:, columns(((1 - z_bit) * 2 + y_bit) * PART)]
    own_ref[:, last:] = saved_ref[:, columns((z_bit * 2 + y_bit) * PART)]


def project_kernel(
    own_half, own, core, pair, far, wq0, wq1, wk0, wk1, wv0, wv1, wout,
    q_ref, kv_ref, do_ref, w_cols,
):
    y_bit = lax.axis_index("gy") % 2
    z_bit = lax.axis_index("gz") % 2
    half = z_bit if own_half else z_bit * 0
    group = columns((z_bit * 2 + y_bit) * PART)
    half_rows = wq0.shape[0]
    width = 2 * half_rows
    for at, (first, second) in enumerate(((wq0, wq1), (wk0, wk1), (wv0, wv1))):
        spot = slice(at * PART, (at + 1) * PART)
        w_cols[pl.ds(pl.multiple_of(half * half_rows, half_rows), half_rows), spot] = first[:, group]
        w_cols[pl.ds(pl.multiple_of((1 - half) * half_rows, half_rows), half_rows), spot] = second[:, group]
    w_rows = wout[pl.ds(pl.multiple_of(y_bit * PART, PART), PART), :]
    for at, source in enumerate((own, core, pair, far)):
        rows = slice(at * PART, (at + 1) * PART)
        made = dot_nn(source[:, PART : PART + width], w_cols[...])
        q_ref[rows, :] = made[:, 0:PART].astype(BF) * jnp.asarray(1.0 / math.sqrt(width // HEADS), BF)
        kv_ref[rows, :] = made[:, PART:].astype(BF)
        do_ref[rows, :] = dot_nt(source[:, PART + width : PART + 2 * width], w_rows).astype(BF)


def early_kernel(own, core, pair, far, do_ref, delta_ref, feat_t_ref, o_ref, saved, dys):
    z_bit = lax.axis_index("gz") % 2
    width = (own.shape[1] - 2 * PART) // 2
    half = width // 2
    last = PART + 2 * width
    for at, (source, spot) in enumerate(((own, last), (core, 0), (pair, 0), (far, last))):
        rows = slice(at * PART, (at + 1) * PART)
        saved[rows, :] = source[:, spot : spot + PART]
        dys[rows, :] = source[:, PART + width : last]
        wanted = source[:, pl.ds(pl.multiple_of(PART + z_bit * half, PART), half)]
        feat_t_ref[:, rows] = wanted.astype(F32).T.astype(BF)
    head_dim = width // HEADS
    products = (do_ref[...].astype(F32) * saved[...].astype(F32)).T
    delta_ref[0:1, :] = jnp.sum(products[0:head_dim], axis=0, keepdims=True)
    delta_ref[1:2, :] = jnp.sum(products[head_dim:PART], axis=0, keepdims=True)
    out = dot_nn(saved[...].astype(F32).T.astype(BF), dys[...]).astype(BF)
    for at in range(8):
        low = out[at * 16 : (at + 1) * 16, :]
        o_ref[at * 32 : at * 32 + 16, :] = low[:, 0:half]
        o_ref[at * 32 + 16 : at * 32 + 32, :] = low[:, half:]


def attention_kernel(times, q_ref, do_ref, delta_ref, *refs):
    count = len(times)
    kvs = refs[:count]
    dq_ref = refs[count]
    dkvs = refs[count + 1 : 2 * count + 1]
    kv_s, e_s, top_s, total_s, f_s, fcol_s, dq_s, dkv_s = refs[2 * count + 1 :]
    tokens = q_ref.shape[0]
    head_dim = PART // 2
    for at in range(count):
        kv_s[at] = kvs[at][...]
    lane = lax.broadcasted_iota(jnp.int32, (tokens, PART), 1)
    low = lane < head_dim
    query = q_ref[...]
    grad = do_ref[...]
    none = jnp.zeros_like(query)
    q_heads = (jnp.where(low, query, none), jnp.where(low, none, query))
    g_heads = (jnp.where(low, grad, none), jnp.where(low, none, grad))

    def first(at, carry):
        keys = kv_s[at, :, 0:PART]
        for head in range(2):
            scores = dot_nt(keys, q_heads[head])
            top = jnp.max(scores, axis=0, keepdims=True)
            grown = jnp.exp(scores - top)
            e_s[2 * at + head] = grown.astype(BF)
            top_s[pl.ds(2 * at + head, 1), :] = top
            total_s[pl.ds(2 * at + head, 1), :] = jnp.sum(grown, axis=0, keepdims=True)
        return carry

    lax.fori_loop(0, count, first, 0)
    for head in range(2):
        tops = [top_s[2 * at + head : 2 * at + head + 1, :] for at in range(count)]
        most = functools.reduce(jnp.maximum, tops)
        lifts = [jnp.exp(top - most) for top in tops]
        total = functools.reduce(
            jnp.add,
            [
                times[at] * lifts[at] * total_s[2 * at + head : 2 * at + head + 1, :]
                for at in range(count)
            ],
        )
        for at in range(count):
            part = lifts[at] / total
            f_s[2 * at + head : 2 * at + head + 1, :] = part * times[at]
            top_s[2 * at + head : 2 * at + head + 1, :] = part
    turned = top_s[...].T
    for at in range(count):
        fcol_s[at] = jnp.where(low, turned[:, 2 * at : 2 * at + 1], turned[:, 2 * at + 1 : 2 * at + 2])
    dq_s[...] = jnp.zeros_like(dq_s)
    delta = delta_ref[...]

    def second(at, carry):
        keys = kv_s[at, :, 0:PART]
        values = kv_s[at, :, PART:]
        keys_t = keys.astype(F32).T.astype(BF)
        scale = fcol_s[at]
        query_f = (query.astype(F32) * scale).astype(BF)
        grad_f = (grad.astype(F32) * scale).astype(BF)
        dk = jnp.zeros((tokens, PART), F32)
        dv = jnp.zeros((tokens, PART), F32)
        for head in range(2):
            mine = low if head == 0 else jnp.logical_not(low)
            grown = e_s[2 * at + head]
            dprob = dot_nt(values, g_heads[head])
            dscore = (grown.astype(F32) * (dprob - delta[head : head + 1, :])).astype(BF)
            dv = dv + dot_nn(grown, jnp.where(mine, grad_f, none))
            dk = dk + dot_nn(dscore, jnp.where(mine, query_f, none))
            spot = slice(head * head_dim, (head + 1) * head_dim)
            dq_s[spot, :] = dq_s[spot, :] + dot_nn(keys_t[spot, :], dscore) * f_s[
                pl.ds(2 * at + head, 1), :
            ]
        dkv_s[at, :, 0:PART] = dk.astype(BF)
        dkv_s[at, :, PART:] = dv.astype(BF)
        return carry

    lax.fori_loop(0, count, second, 0)
    for at in range(count):
        dkvs[at][...] = dkv_s[at]
    dq_ref[...] = (dq_s[...].T * (1.0 / math.sqrt(head_dim))).astype(BF)


def collect_kernel(times, dq_ref, *refs):
    count = len(times)
    out = refs[count]
    total = times[0] * refs[0][...].astype(F32)
    for at in range(1, count):
        total = total + times[at] * refs[at][...].astype(F32)
    out[:, 0:PART] = dq_ref[...]
    out[:, PART:] = total.astype(BF)


def weight_kernel(chunks, own, core, feat_t, o_ref, pair_ref, mine_ref, *refs):
    outs, (grads, held) = refs[:chunks], refs[chunks:]
    z_bit = lax.axis_index("gz") % 2
    tokens = own.shape[0]
    for at in range(3):
        source = slice(at * PART, (at + 1) * PART)
        own_at = columns(at * 2 * PART + z_bit * PART)
        core_at = columns(at * 2 * PART + (1 - z_bit) * PART)
        grads[:, own_at] = own[:, source]
        for low in range(4):
            grads[low * PART : (low + 1) * PART, core_at] = core[
                (low ^ 1) * PART : ((low ^ 1) + 1) * PART, source
            ]
    mine_ref[...] = grads[0:PART, :]
    pair_ref[...] = grads[2 * PART : 3 * PART, :]
    wide = grads.shape[1]
    held[:, 0:wide] = dot_nn(feat_t[...], grads[...]).astype(BF)
    held[:, wide:] = o_ref[...]
    rows = held.shape[0] // chunks
    place = (lax.axis_index("gx") * 2 + lax.axis_index("gy") // 2) if chunks > 1 else 0
    for at in range(chunks):
        if chunks > 1:
            spot = (lax.axis_index("gx") ^ (at // 2)) * 2 + ((lax.axis_index("gy") // 2) ^ (at % 2))
            outs[at][...] = held[pl.ds(pl.multiple_of(spot * rows, rows), rows), :]
        else:
            outs[at][...] = held[...]


def grad_x_kernel(own_half, mine, pair, wq0, wq1, wk0, wk1, wv0, wv1, out, full):
    y_bit = lax.axis_index("gy") % 2
    z_bit = lax.axis_index("gz") % 2
    half = z_bit if own_half else z_bit * 0
    width = wq0.shape[1]
    half_rows = wq0.shape[0]
    for at in range(3):
        for side in range(2):
            spot = slice((at * 2 + side) * PART, (at * 2 + side + 1) * PART)
            base = at * width + side * 2 * PART
            full[:, columns(base + y_bit * PART)] = mine[:, spot]
            full[:, columns(base + (1 - y_bit) * PART)] = pair[:, spot]
    for at, sources in ((half, (wq0, wk0, wv0)), (1 - half, (wq1, wk1, wv1))):
        total = functools.reduce(
            jnp.add,
            [dot_nt(full[:, n * width : (n + 1) * width], sources[n][...]) for n in range(3)],
        )
        out[:, pl.ds(pl.multiple_of(at * half_rows, PART), half_rows)] = total.astype(BF)


def sum_kernel(*refs):
    total = refs[0][...].astype(F32)
    for ref in refs[1:-1]:
        total = total + ref[...].astype(F32)
    refs[-1][...] = total.astype(BF)


def spread_kernel(*refs):
    outs = refs[4:]
    at_x = lax.axis_index("gx")
    at_y = lax.axis_index("gy")
    rows, wide = refs[0].shape[1:]
    half = 2 * PART
    for flip_x in range(4):
        for flip_y in range(4):
            piece = refs[flip_x][flip_y].astype(F32)
            their_y = at_y ^ flip_y
            place = (at_x ^ flip_x) * 2 + their_y // 2
            bit = their_y % 2
            spot = pl.ds(pl.multiple_of(place * rows, rows), rows)
            for at in range(3):
                for side in range(2):
                    outs[at][spot, columns(side * half + bit * PART)] = piece[
                        :, (at * 2 + side) * PART : (at * 2 + side + 1) * PART
                    ]
            low = piece[:, 6 * PART :]
            spot = pl.ds(pl.multiple_of(bit * PART + place * (rows // 2), rows // 2), rows // 2)
            outs[3][spot, 0:half] = low[0 : rows // 2]
            outs[3][spot, half:] = low[rows // 2 :]


def on_device(features, grad_y, attn_out, w_query, w_key, w_value, w_out):
    width = features.shape[-1]
    half = width // 2
    tokens = features.shape[0] * features.shape[1] * features.shape[2]
    block_tokens = 4 * tokens
    count_x, count_y, count_z = lax.axis_size("gx"), lax.axis_size("gy"), lax.axis_size("gz")
    z_bit = lax.axis_index("gz") % 2
    y_bit = lax.axis_index("gy") % 2

    own_half = count_z == 2
    if own_half:
        pairs = []
        for weight in (w_query, w_key, w_value):
            pairs += [weight, from_partner(weight, "gz")]
        out_rows = w_out
    else:
        pairs = []
        for weight in (w_query, w_key, w_value):
            whole = lax.all_gather(weight, "gz", axis=0, tiled=True)
            pairs += [whole[:half], whole[half:]]
        whole = lax.all_gather(w_out, "gz", axis=0, tiled=True)
        out_rows = lax.dynamic_slice_in_dim(whole, z_bit * half, half, 0)

    message = shape_of((tokens, 2 * width + 2 * PART))
    pair_message, own = call(
        pack_kernel,
        (message, message),
        [value.reshape(tokens, width) for value in (features, grad_y, attn_out)],
    )
    pair = from_partner(pair_message, "gy")
    core = from_partner(own, "gz")
    far = from_partner(pair, "gz")
    query, own_kv, out_grad = call(
        functools.partial(project_kernel, own_half),
        (
            shape_of((block_tokens, PART)),
            shape_of((block_tokens, 2 * PART)),
            shape_of((block_tokens, PART)),
        ),
        [own, core, pair, far, *pairs, out_rows],
        scratch=[pltpu.VMEM((width, 3 * PART), BF)],
        flops=2 * block_tokens * width * 4 * PART,
    )

    times = [1]
    routes = []
    for axis, step, blocks in (("gx", 1, count_x), ("gy", 2, count_y // 2), ("gz", 2, count_z // 2)):
        if blocks == 1:
            times[0] += 2
        elif blocks == 2:
            routes.append((axis, step))
            times.append(2)
        else:
            routes += [(axis, step), (axis, -step)]
            times += [1, 1]
    near = [own_kv] + [shifted(own_kv, axis, step) for axis, step in routes]
    count = len(times)
    delta, feat_t, out_term = call(
        early_kernel,
        (
            shape_of((2, block_tokens), F32),
            shape_of((half, block_tokens)),
            shape_of((half, half)),
        ),
        [own, core, pair, far, out_grad],
        scratch=[pltpu.VMEM((block_tokens, PART), BF), pltpu.VMEM((block_tokens, width), BF)],
        flops=2 * block_tokens * width * PART,
    )
    rows = -(-2 * count // 8) * 8
    dq, *partials = call(
        functools.partial(attention_kernel, tuple(float(n) for n in times)),
        (
            shape_of((block_tokens, PART)),
            *[shape_of((block_tokens, 2 * PART)) for n in range(count)],
        ),
        [query, out_grad, delta, *near],
        scratch=[
            pltpu.VMEM((count, block_tokens, 2 * PART), BF),
            pltpu.VMEM((2 * count, block_tokens, block_tokens), BF),
            pltpu.VMEM((rows, block_tokens), F32),
            pltpu.VMEM((rows, block_tokens), F32),
            pltpu.VMEM((rows, block_tokens), F32),
            pltpu.VMEM((count, block_tokens, PART), F32),
            pltpu.VMEM((PART, block_tokens), F32),
            pltpu.VMEM((count, block_tokens, 2 * PART), BF),
        ],
        flops=2 * 2 * 5 * count * block_tokens * block_tokens * PART,
        exps=2 * count * block_tokens * block_tokens,
    )
    back = [partials[0]]
    for partial, (axis, step) in zip(partials[1:], routes):
        back.append(shifted(partial, axis, -step))
    grads = call(
        functools.partial(collect_kernel, tuple(float(n) for n in times)),
        shape_of((block_tokens, 3 * PART)),
        [dq, *back],
    )
    core_grads = from_partner(grads, "gz")
    planned = count_x == 4 and count_y == 4 and count_z == 2
    chunks = 8 if planned else 1
    piece = shape_of((half // chunks, 8 * PART))
    pair_out, mine, *pieces = call(
        functools.partial(weight_kernel, chunks),
        (shape_of((tokens, 6 * PART)), shape_of((tokens, 6 * PART)), *[piece] * chunks),
        [grads, core_grads, feat_t, out_term],
        scratch=[pltpu.VMEM((block_tokens, 6 * PART), BF), pltpu.VMEM((half, 8 * PART), BF)],
        flops=2 * block_tokens * half * 6 * PART,
    )
    pair_in = from_partner(pair_out, "gy")
    if planned:
        terms = [pieces[0]]
        for at in range(1, 8):
            terms.append(plane_swap(pieces[at], at // 2, 2 * (at % 2)))
        total = call(sum_kernel, piece, terms)
        line = jnp.stack([total] + [plane_swap(total, 0, flip) for flip in (1, 2, 3)])
        plane = [line] + [plane_swap(line, flip, 0) for flip in (1, 2, 3)]
        weights = call(spread_kernel, tuple([shape_of((half, width), F32)] * 4), plane)
    else:
        terms = pieces[0].astype(F32)
        stacked = jnp.zeros((4, width, width), F32)
        for at in range(3):
            for side in range(2):
                tile = terms[:, (at * 2 + side) * PART : (at * 2 + side + 1) * PART]
                stacked = lax.dynamic_update_slice(
                    stacked, tile[None], (at, z_bit * half, side * half + y_bit * PART)
                )
        tile = terms[:, 6 * PART :].reshape(8, 2, 16, half).transpose(0, 2, 1, 3).reshape(PART, width)
        stacked = lax.dynamic_update_slice(
            stacked, tile[None], (3, z_bit * half + y_bit * PART, 0)
        )
        stacked = lax.psum(stacked, ("gx", "gy", "gz"))
        held = w_query.shape[0]
        stacked = lax.dynamic_slice_in_dim(stacked, lax.axis_index("gz") * held, held, 1)
        weights = [stacked[at] for at in range(4)]
    grad_x = call(
        functools.partial(grad_x_kernel, own_half),
        shape_of((tokens, width)),
        [mine, pair_in, *pairs],
        scratch=[pltpu.VMEM((tokens, 3 * width), BF)],
        flops=2 * tokens * 3 * width * width,
    ).reshape(features.shape)
    return (grad_x, *weights)


def solution(mesh):
    return jax.shard_map(
        on_device,
        mesh=mesh,
        in_specs=(
            P("gx", "gy", "gz", None),
            P("gx", "gy", "gz", None),
            P("gx", "gy", "gz", None),
            P("gz", None),
            P("gz", None),
            P("gz", None),
            P("gz", None),
        ),
        out_specs=(
            P("gx", "gy", "gz", None),
            P("gz", None),
            P("gz", None),
            P("gz", None),
            P("gz", None),
        ),
        check_vma=False,
    )
```

```python
import functools
import math

import jax
import jax.numpy as jnp
from jax import lax
from jax.experimental import pallas as pl
from jax.experimental.pallas import tpu as pltpu
from jax.sharding import PartitionSpec as P

HEADS = 8
PART = 128
BF = jnp.bfloat16
F32 = jnp.float32
VMEM_BYTES = 32 * 1024 * 1024


def from_partner(block, axis):
    route = [(index, index ^ 1) for index in range(lax.axis_size(axis))]
    return lax.ppermute(block, axis, route)


def shifted(value, axis, steps):
    count = lax.axis_size(axis)
    return lax.ppermute(value, axis, [(source, (source + steps) % count) for source in range(count)])


def plane_swap(value, flip_x, flip_y):
    count_x, count_y = lax.axis_size("gx"), lax.axis_size("gy")
    route = []
    for at_x in range(count_x):
        for at_y in range(count_y):
            route.append((at_x * count_y + at_y, (at_x ^ flip_x) * count_y + (at_y ^ flip_y)))
    return lax.ppermute(value, ("gx", "gy"), route)


def dot_nn(left, right):
    return lax.dot_general(left, right, (((1,), (0,)), ((), ())), preferred_element_type=F32)


def dot_nt(left, right):
    return lax.dot_general(left, right, (((1,), (1,)), ((), ())), preferred_element_type=F32)


def dot_tn(left, right):
    return lax.dot_general(left, right, (((0,), (0,)), ((), ())), preferred_element_type=F32)


def columns(start):
    return pl.ds(pl.multiple_of(start, PART), PART)


def call(kernel, out_shape, args, scratch=(), flops=1e6, moved=1e6, exps=0):
    return pl.pallas_call(
        kernel,
        out_shape=out_shape,
        scratch_shapes=list(scratch),
        compiler_params=pltpu.CompilerParams(vmem_limit_bytes=VMEM_BYTES),
        cost_estimate=pl.CostEstimate(
            flops=int(flops), bytes_accessed=int(moved), transcendentals=int(exps)
        ),
    )(*args)


def shape_of(dims, dtype=BF):
    return jax.ShapeDtypeStruct(dims, dtype)


def pack_kernel(dy_ref, saved_ref, pair_ref, own_ref):
    y_bit = lax.axis_index("gy") % 2
    z_bit = lax.axis_index("gz") % 2
    last = PART + dy_ref.shape[1]
    for out in (pair_ref, own_ref):
        out[:, PART:last] = dy_ref[...]
    pair_ref[:, 0:PART] = saved_ref[:, columns((z_bit * 2 + 1 - y_bit) * PART)]
    pair_ref[:, last:] = saved_ref[:, columns(((1 - z_bit) * 2 + 1 - y_bit) * PART)]
    own_ref[:, 0:PART] = saved_ref[:, columns(((1 - z_bit) * 2 + y_bit) * PART)]
    own_ref[:, last:] = saved_ref[:, columns((z_bit * 2 + y_bit) * PART)]


def project_kernel(
    own_half, own, core, pair, far, wq0, wq1, wk0, wk1, wv0, wv1, q_ref, k_ref, v_ref, w_cols
):
    y_bit = lax.axis_index("gy") % 2
    z_bit = lax.axis_index("gz") % 2
    half = z_bit if own_half else z_bit * 0
    group = columns((z_bit * 2 + y_bit) * PART)
    half_rows = wq0.shape[0]
    width = 2 * half_rows
    for at, (first, second) in enumerate(((wq0, wq1), (wk0, wk1), (wv0, wv1))):
        spot = slice(at * PART, (at + 1) * PART)
        w_cols[pl.ds(pl.multiple_of(half * half_rows, half_rows), half_rows), spot] = first[:, group]
        w_cols[pl.ds(pl.multiple_of((1 - half) * half_rows, half_rows), half_rows), spot] = second[:, group]
    for at, source in enumerate((own, core, pair, far)):
        rows = slice(at * PART, (at + 1) * PART)
        made = dot_nn(source[...], w_cols[...])
        q_ref[rows, :] = made[:, 0:PART].astype(BF) * jnp.asarray(1.0 / math.sqrt(width // HEADS), BF)
        k_ref[rows, :] = made[:, PART : 2 * PART].astype(BF)
        v_ref[rows, :] = made[:, 2 * PART :].astype(BF)


def early_kernel(
    f_own, f_core, f_pair, f_far, own, core, pair, far, wout,
    do_ref, delta_ref, feat_t_ref, o_ref, saved, dys,
):
    y_bit = lax.axis_index("gy") % 2
    z_bit = lax.axis_index("gz") % 2
    width = f_own.shape[1]
    half = width // 2
    last = PART + width
    for at, (source, spot) in enumerate(((own, last), (core, 0), (pair, 0), (far, last))):
        rows = slice(at * PART, (at + 1) * PART)
        saved[rows, :] = source[:, spot : spot + PART]
        dys[rows, :] = source[:, PART:last]
    for at, source in enumerate((f_own, f_core, f_pair, f_far)):
        wanted = source[:, pl.ds(pl.multiple_of(z_bit * half, PART), half)]
        feat_t_ref[:, at * PART : (at + 1) * PART] = wanted.astype(F32).T.astype(BF)
    w_rows = wout[pl.ds(pl.multiple_of(y_bit * PART, PART), PART), :]
    out_grad = dot_nt(dys[...], w_rows).astype(BF)
    do_ref[...] = out_grad
    head_dim = width // HEADS
    products = (out_grad.astype(F32) * saved[...].astype(F32)).T
    delta_ref[0:1, :] = jnp.sum(products[0:head_dim], axis=0, keepdims=True)
    delta_ref[1:2, :] = jnp.sum(products[head_dim:PART], axis=0, keepdims=True)
    out = dot_nn(saved[...].astype(F32).T.astype(BF), dys[...]).astype(BF)
    for at in range(4):
        low = out[at * 32 : (at + 1) * 32, :]
        o_ref[at * 64 : at * 64 + 32, :] = low[:, 0:half]
        o_ref[at * 64 + 32 : at * 64 + 64, :] = low[:, half:]


def by_head(value):
    low = lax.broadcasted_iota(jnp.int32, value.shape, 1) < PART // 2
    none = jnp.zeros_like(value)
    return (jnp.where(low, value, none), jnp.where(low, none, value))


def row_scale(table, at, tokens):
    low = lax.broadcasted_iota(jnp.int32, (tokens, PART), 1) < PART // 2
    return jnp.where(low, table[:, 2 * at : 2 * at + 1], table[:, 2 * at + 1 : 2 * at + 2])


def score_kernel(times, q_ref, do_ref, *refs):
    count = len(times)
    keys_in = refs[:count]
    e_ref, part_ref = refs[count : count + 2]
    dvs = refs[count + 2 : 2 * count + 2]
    keys_s, top_s, total_s, fcol_s, dv_s = refs[2 * count + 2 :]
    tokens = q_ref.shape[0]
    for at in range(count):
        keys_s[at] = keys_in[at][...]
    q_heads = by_head(q_ref[...])

    def first(at, carry):
        keys = keys_s[at]
        for head in range(2):
            scores = dot_nt(keys, q_heads[head])
            top = jnp.max(scores, axis=0, keepdims=True)
            grown = jnp.exp(scores - top)
            e_ref[2 * at + head] = grown.astype(BF)
            top_s[pl.ds(2 * at + head, 1), :] = top
            total_s[pl.ds(2 * at + head, 1), :] = jnp.sum(grown, axis=0, keepdims=True)
        return carry

    lax.fori_loop(0, count, first, 0)
    for head in range(2):
        tops = [top_s[2 * at + head : 2 * at + head + 1, :] for at in range(count)]
        most = functools.reduce(jnp.maximum, tops)
        lifts = [jnp.exp(top - most) for top in tops]
        total = functools.reduce(
            jnp.add,
            [
                times[at] * lifts[at] * total_s[2 * at + head : 2 * at + head + 1, :]
                for at in range(count)
            ],
        )
        for at in range(count):
            part_ref[2 * at + head : 2 * at + head + 1, :] = lifts[at] / total
    if part_ref.shape[0] > 2 * count:
        part_ref[2 * count :, :] = jnp.zeros((part_ref.shape[0] - 2 * count, tokens), F32)
    turned = part_ref[...].T
    for at in range(count):
        fcol_s[at] = row_scale(turned, at, tokens)
    grad = do_ref[...].astype(F32)

    def second(at, carry):
        g_heads = by_head((grad * fcol_s[at]).astype(BF))
        dv_s[at] = (dot_nn(e_ref[2 * at], g_heads[0]) + dot_nn(e_ref[2 * at + 1], g_heads[1])).astype(BF)
        return carry

    lax.fori_loop(0, count, second, 0)
    for at in range(count):
        dvs[at][...] = dv_s[at]


def gradient_kernel(times, q_ref, do_ref, delta_ref, e_ref, part_ref, *refs):
    count = len(times)
    keys_in, values_in = refs[:count], refs[count : 2 * count]
    dq_ref = refs[2 * count]
    dks = refs[2 * count + 1 : 3 * count + 1]
    keys_s, values_s, f_s, fcol_s, dq_s, dk_s = refs[3 * count + 1 :]
    tokens = q_ref.shape[0]
    head_dim = PART // 2
    turned = part_ref[...].T
    for at in range(count):
        keys_s[at] = keys_in[at][...]
        values_s[at] = values_in[at][...]
        fcol_s[at] = row_scale(turned, at, tokens)
        f_s[2 * at : 2 * at + 2, :] = part_ref[2 * at : 2 * at + 2, :] * times[at]
    g_heads = by_head(do_ref[...])
    query = q_ref[...].astype(F32)
    delta = delta_ref[...]
    dq_s[...] = jnp.zeros_like(dq_s)

    def step(at, carry):
        keys_t = keys_s[at].astype(F32).T.astype(BF)
        values = values_s[at]
        q_heads = by_head((query * fcol_s[at]).astype(BF))
        dk = jnp.zeros((tokens, PART), F32)
        for head in range(2):
            dprob = dot_nt(values, g_heads[head])
            dscore = (e_ref[2 * at + head].astype(F32) * (dprob - delta[head : head + 1, :])).astype(BF)
            dk = dk + dot_nn(dscore, q_heads[head])
            spot = slice(head * head_dim, (head + 1) * head_dim)
            dq_s[spot, :] = dq_s[spot, :] + dot_nn(keys_t[spot, :], dscore) * f_s[
                pl.ds(2 * at + head, 1), :
            ]
        dk_s[at] = dk.astype(BF)
        return carry

    lax.fori_loop(0, count, step, 0)
    for at in range(count):
        dks[at][...] = dk_s[at]
    dq_ref[...] = (dq_s[...].T * (1.0 / math.sqrt(head_dim))).astype(BF)


def combined(times, refs):
    total = times[0] * refs[0][...].astype(F32)
    for time, ref in zip(times[1:], refs[1:]):
        total = total + time * ref[...].astype(F32)
    return total.astype(BF)


def collect_values_kernel(times, dq_ref, *refs):
    refs[-1][:, 0:PART] = dq_ref[...]
    refs[-1][:, PART:] = combined(times, refs[:-1])


def collect_keys_kernel(times, *refs):
    refs[-1][...] = combined(times, refs[:-1])


def place_grads(grads, own, core, count):
    z_bit = lax.axis_index("gz") % 2
    for at in range(count):
        source = slice(at * PART, (at + 1) * PART)
        grads[:, columns(at * 2 * PART + z_bit * PART)] = own[:, source]
        core_at = columns(at * 2 * PART + (1 - z_bit) * PART)
        for low in range(4):
            grads[low * PART : (low + 1) * PART, core_at] = core[
                (low ^ 1) * PART : ((low ^ 1) + 1) * PART, source
            ]


def weight_early_kernel(own, core, feat_t, o_ref, held_ref, rows_ref, grads):
    place_grads(grads, own, core, 2)
    wide = grads.shape[1]
    held_ref[:, 0:wide] = dot_nn(feat_t[...], grads[...]).astype(BF)
    held_ref[:, wide:] = o_ref[...]
    rows_ref[0] = grads[0:PART, :]
    rows_ref[1] = grads[2 * PART : 3 * PART, :]


def weight_late_kernel(chunks, own, core, feat_t, held_ref, rows_ref, pair_ref, mine_ref, *refs):
    outs, (grads, made) = refs[:chunks], refs[chunks:]
    place_grads(grads, own, core, 1)
    early = rows_ref.shape[2]
    mine_ref[:, 0:early] = rows_ref[0]
    mine_ref[:, early:] = grads[0:PART, :]
    pair_ref[:, 0:early] = rows_ref[1]
    pair_ref[:, early:] = grads[2 * PART : 3 * PART, :]
    made[...] = dot_nn(feat_t[...], grads[...]).astype(BF)
    rows = made.shape[0] // chunks
    wide = held_ref.shape[1]
    for at in range(chunks):
        spot = pl.ds(0, rows)
        if chunks > 1:
            spot = pl.ds(pl.multiple_of((lax.axis_index("gx") ^ at) * rows, rows), rows)
        outs[at][:, 0:wide] = held_ref[spot, :]
        outs[at][:, wide:] = made[spot, :]


def grad_x_kernel(own_half, mine, pair, wq0, wq1, wk0, wk1, wv0, wv1, out, full):
    y_bit = lax.axis_index("gy") % 2
    z_bit = lax.axis_index("gz") % 2
    half = z_bit if own_half else z_bit * 0
    width = wq0.shape[1]
    half_rows = wq0.shape[0]
    for at in range(3):
        for side in range(2):
            spot = slice((at * 2 + side) * PART, (at * 2 + side + 1) * PART)
            base = at * width + side * 2 * PART
            full[:, columns(base + y_bit * PART)] = mine[:, spot]
            full[:, columns(base + (1 - y_bit) * PART)] = pair[:, spot]
    for at, sources in ((half, (wq0, wv0, wk0)), (1 - half, (wq1, wv1, wk1))):
        total = functools.reduce(
            jnp.add,
            [dot_nt(full[:, n * width : (n + 1) * width], sources[n][...]) for n in range(3)],
        )
        out[:, pl.ds(pl.multiple_of(at * half_rows, PART), half_rows)] = total.astype(BF)


def sum_kernel(*refs):
    total = refs[0][...].astype(F32)
    for ref in refs[1:-1]:
        total = total + ref[...].astype(F32)
    refs[-1][...] = total.astype(BF)


def spread_kernel(*refs):
    pieces, outs = refs[:8], refs[8:]
    half = 2 * PART
    rows = pieces[0].shape[0]
    for at, piece in enumerate(pieces):
        place = lax.axis_index("gx") ^ (at // 2)
        bit = (lax.axis_index("gy") % 2) ^ (at % 2)
        spot = pl.ds(pl.multiple_of(place * rows, rows), rows)
        for base, out in ((0, outs[0]), (3, outs[1]), (1, outs[2])):
            for side in range(2):
                source = slice((base * 2 + side) * PART, (base * 2 + side + 1) * PART)
                out[spot, columns(side * half + bit * PART)] = piece[:, source].astype(F32)
        spot = pl.ds(pl.multiple_of(bit * PART + place * (rows // 2), rows // 2), rows // 2)
        outs[3][spot, 0:half] = piece[0 : rows // 2, 2 * half : 3 * half].astype(F32)
        outs[3][spot, half:] = piece[rows // 2 :, 2 * half : 3 * half].astype(F32)


def on_device(features, grad_y, attn_out, w_query, w_key, w_value, w_out):
    width = features.shape[-1]
    half = width // 2
    tokens = features.shape[0] * features.shape[1] * features.shape[2]
    block_tokens = 4 * tokens
    count_x, count_y, count_z = lax.axis_size("gx"), lax.axis_size("gy"), lax.axis_size("gz")
    z_bit = lax.axis_index("gz") % 2
    y_bit = lax.axis_index("gy") % 2

    own_half = count_z == 2
    if own_half:
        pairs = []
        for weight in (w_query, w_key, w_value):
            pairs += [weight, from_partner(weight, "gz")]
        out_rows = w_out
    else:
        pairs = []
        for weight in (w_query, w_key, w_value):
            whole = lax.all_gather(weight, "gz", axis=0, tiled=True)
            pairs += [whole[:half], whole[half:]]
        whole = lax.all_gather(w_out, "gz", axis=0, tiled=True)
        out_rows = lax.dynamic_slice_in_dim(whole, z_bit * half, half, 0)

    message = shape_of((tokens, width + 2 * PART))
    feat = features.reshape(tokens, width)
    feat_pair = from_partner(feat, "gy")
    feat_core = from_partner(feat, "gz")
    feat_pair, feat_core, *pairs = lax.optimization_barrier((feat_pair, feat_core, *pairs))
    feat_far = from_partner(feat_pair, "gz")
    feats = [feat, feat_core, feat_pair, feat_far]
    column = shape_of((block_tokens, PART))
    query, own_keys, own_values = call(
        functools.partial(project_kernel, own_half),
        (column, column, column),
        [*feats, *pairs],
        scratch=[pltpu.VMEM((width, 3 * PART), BF)],
        flops=2 * block_tokens * width * 3 * PART,
    )
    pair_message, own = call(
        pack_kernel,
        (message, message),
        [value.reshape(tokens, width) for value in (grad_y, attn_out)],
    )
    pair = from_partner(pair_message, "gy")
    core = from_partner(own, "gz")
    far = from_partner(pair, "gz")

    times = [1.0]
    routes = []
    for axis, step, blocks in (("gx", 1, count_x), ("gy", 2, count_y // 2), ("gz", 2, count_z // 2)):
        if blocks == 1:
            times[0] += 2.0
        elif blocks == 2:
            routes.append((axis, step))
            times.append(2.0)
        else:
            routes += [(axis, step), (axis, -step)]
            times += [1.0, 1.0]
    times = tuple(times)
    count = len(times)
    keys = [own_keys] + [shifted(own_keys, axis, step) for axis, step in routes]
    values = [own_values] + [shifted(own_values, axis, step) for axis, step in routes]
    out_grad, delta, feat_t, out_term = call(
        early_kernel,
        (
            column,
            shape_of((2, block_tokens), F32),
            shape_of((half, block_tokens)),
            shape_of((half, half)),
        ),
        [*feats, own, core, pair, far, out_rows],
        scratch=[pltpu.VMEM((block_tokens, PART), BF), pltpu.VMEM((block_tokens, width), BF)],
        flops=4 * block_tokens * width * PART,
    )
    rows = -(-2 * count // 8) * 8
    pixels = 2 * count * block_tokens * block_tokens
    grown, parts, *dvs = call(
        functools.partial(score_kernel, times),
        (
            shape_of((2 * count, block_tokens, block_tokens)),
            shape_of((rows, block_tokens), F32),
            *[column] * count,
        ),
        [query, out_grad, *keys],
        scratch=[
            pltpu.VMEM((count, block_tokens, PART), BF),
            pltpu.VMEM((rows, block_tokens), F32),
            pltpu.VMEM((rows, block_tokens), F32),
            pltpu.VMEM((count, block_tokens, PART), F32),
            pltpu.VMEM((count, block_tokens, PART), BF),
        ],
        flops=4 * pixels * PART,
        moved=2 * pixels,
        exps=pixels,
    )
    dv_back = [dvs[0]]
    for partial, (axis, step) in zip(dvs[1:], routes):
        dv_back.append(shifted(partial, axis, -step))
    dq, *dks = call(
        functools.partial(gradient_kernel, times),
        (column, *[column] * count),
        [query, out_grad, delta, grown, parts, *keys, *values],
        scratch=[
            pltpu.VMEM((count, block_tokens, PART), BF),
            pltpu.VMEM((count, block_tokens, PART), BF),
            pltpu.VMEM((rows, block_tokens), F32),
            pltpu.VMEM((count, block_tokens, PART), F32),
            pltpu.VMEM((PART, block_tokens), F32),
            pltpu.VMEM((count, block_tokens, PART), BF),
        ],
        flops=6 * pixels * PART,
        moved=2 * pixels,
    )
    dk_back = [dks[0]]
    for partial, (axis, step) in zip(dks[1:], routes):
        dk_back.append(shifted(partial, axis, -step))
    early = call(
        functools.partial(collect_values_kernel, times),
        shape_of((block_tokens, 2 * PART)),
        [dq, *dv_back],
    )
    early_core = from_partner(early, "gz")
    planned = count_x == 4 and count_y == 4 and count_z == 2
    chunks = 4 if planned else 1
    piece = shape_of((half // chunks, 8 * PART))
    held, early_rows = call(
        weight_early_kernel,
        (shape_of((half, 6 * PART)), shape_of((2, tokens, 4 * PART))),
        [early, early_core, feat_t, out_term],
        scratch=[pltpu.VMEM((block_tokens, 4 * PART), BF)],
        flops=2 * block_tokens * half * 4 * PART,
    )
    late = call(functools.partial(collect_keys_kernel, times), column, dk_back)
    late_core = from_partner(late, "gz")
    pair_out, mine, *pieces = call(
        functools.partial(weight_late_kernel, chunks),
        (shape_of((tokens, 6 * PART)), shape_of((tokens, 6 * PART)), *[piece] * chunks),
        [late, late_core, feat_t, held, early_rows],
        scratch=[pltpu.VMEM((block_tokens, 2 * PART), BF), pltpu.VMEM((half, 2 * PART), BF)],
        flops=2 * block_tokens * half * 2 * PART,
    )
    pair_in = from_partner(pair_out, "gy")
    if planned:
        terms = [pieces[0]] + [plane_swap(pieces[at], at, 0) for at in (1, 2, 3)]
        total = call(sum_kernel, piece, terms)
        total = call(sum_kernel, piece, [total, plane_swap(total, 0, 2)])
        by_x, by_y, by_z = plane_swap(total, 1, 0), plane_swap(total, 2, 0), plane_swap(total, 0, 1)
        by_xy, by_xz = plane_swap(by_y, 1, 0), plane_swap(by_x, 0, 1)
        by_yz, by_xyz = plane_swap(by_z, 2, 0), plane_swap(by_z, 3, 0)
        weights = call(
            spread_kernel,
            tuple([shape_of((half, width), F32)] * 4),
            [total, by_z, by_x, by_xz, by_y, by_yz, by_xy, by_xyz],
        )
    else:
        terms = pieces[0].astype(F32)
        stacked = jnp.zeros((4, width, width), F32)
        for base, at in ((0, 0), (3, 1), (1, 2)):
            for side in range(2):
                tile = terms[:, (base * 2 + side) * PART : (base * 2 + side + 1) * PART]
                stacked = lax.dynamic_update_slice(
                    stacked, tile[None], (at, z_bit * half, side * half + y_bit * PART)
                )
        tile = terms[:, 4 * PART : 6 * PART].reshape(4, 2, 32, half)
        tile = tile.transpose(0, 2, 1, 3).reshape(PART, width)
        stacked = lax.dynamic_update_slice(
            stacked, tile[None], (3, z_bit * half + y_bit * PART, 0)
        )
        stacked = lax.psum(stacked, ("gx", "gy", "gz"))
        held_rows = w_query.shape[0]
        stacked = lax.dynamic_slice_in_dim(stacked, lax.axis_index("gz") * held_rows, held_rows, 1)
        weights = [stacked[at] for at in range(4)]
    grad_x = call(
        functools.partial(grad_x_kernel, own_half),
        shape_of((tokens, width)),
        [mine, pair_in, *pairs],
        scratch=[pltpu.VMEM((tokens, 3 * width), BF)],
        flops=2 * tokens * 3 * width * width,
    ).reshape(features.shape)
    return (grad_x, *weights)


def solution(mesh):
    return jax.shard_map(
        on_device,
        mesh=mesh,
        in_specs=(
            P("gx", "gy", "gz", None),
            P("gx", "gy", "gz", None),
            P("gx", "gy", "gz", None),
            P("gz", None),
            P("gz", None),
            P("gz", None),
            P("gz", None),
        ),
        out_specs=(
            P("gx", "gy", "gz", None),
            P("gz", None),
            P("gz", None),
            P("gz", None),
            P("gz", None),
        ),
        check_vma=False,
    )
```

```python
import functools
import math

import jax
import jax.numpy as jnp
from jax import lax
from jax.experimental import pallas as pl
from jax.experimental.pallas import tpu as pltpu
from jax.sharding import PartitionSpec as P

HEADS = 8
PART = 128
BF = jnp.bfloat16
F32 = jnp.float32
VMEM_BYTES = 32 * 1024 * 1024


def from_partner(block, axis):
    route = [(index, index ^ 1) for index in range(lax.axis_size(axis))]
    return lax.ppermute(block, axis, route)


def shifted(value, axis, steps):
    count = lax.axis_size(axis)
    return lax.ppermute(value, axis, [(source, (source + steps) % count) for source in range(count)])


def plane_swap(value, flip_x, flip_y):
    count_x, count_y = lax.axis_size("gx"), lax.axis_size("gy")
    route = []
    for at_x in range(count_x):
        for at_y in range(count_y):
            route.append((at_x * count_y + at_y, (at_x ^ flip_x) * count_y + (at_y ^ flip_y)))
    return lax.ppermute(value, ("gx", "gy"), route)


def dot_nn(left, right):
    return lax.dot_general(left, right, (((1,), (0,)), ((), ())), preferred_element_type=F32)


def dot_nt(left, right):
    return lax.dot_general(left, right, (((1,), (1,)), ((), ())), preferred_element_type=F32)


def dot_tn(left, right):
    return lax.dot_general(left, right, (((0,), (0,)), ((), ())), preferred_element_type=F32)


def columns(start):
    return pl.ds(pl.multiple_of(start, PART), PART)


def call(kernel, out_shape, args, scratch=(), flops=1e6, moved=1e6, exps=0):
    return pl.pallas_call(
        kernel,
        out_shape=out_shape,
        scratch_shapes=list(scratch),
        compiler_params=pltpu.CompilerParams(vmem_limit_bytes=VMEM_BYTES),
        cost_estimate=pl.CostEstimate(
            flops=int(flops), bytes_accessed=int(moved), transcendentals=int(exps)
        ),
    )(*args)


def shape_of(dims, dtype=BF):
    return jax.ShapeDtypeStruct(dims, dtype)


def pack_kernel(dy_ref, saved_ref, pair_ref, own_ref):
    y_bit = lax.axis_index("gy") % 2
    z_bit = lax.axis_index("gz") % 2
    last = PART + dy_ref.shape[1]
    for out in (pair_ref, own_ref):
        out[:, PART:last] = dy_ref[...]
    pair_ref[:, 0:PART] = saved_ref[:, columns((z_bit * 2 + 1 - y_bit) * PART)]
    pair_ref[:, last:] = saved_ref[:, columns(((1 - z_bit) * 2 + 1 - y_bit) * PART)]
    own_ref[:, 0:PART] = saved_ref[:, columns(((1 - z_bit) * 2 + y_bit) * PART)]
    own_ref[:, last:] = saved_ref[:, columns((z_bit * 2 + y_bit) * PART)]


def columns_kernel(own_half, wq0, wq1, wk0, wk1, wv0, wv1, w_cols):
    y_bit = lax.axis_index("gy") % 2
    z_bit = lax.axis_index("gz") % 2
    half = z_bit if own_half else z_bit * 0
    group = columns((z_bit * 2 + y_bit) * PART)
    half_rows = wq0.shape[0]
    for at, (first, second) in enumerate(((wq0, wq1), (wk0, wk1), (wv0, wv1))):
        spot = slice(at * PART, (at + 1) * PART)
        w_cols[pl.ds(pl.multiple_of(half * half_rows, half_rows), half_rows), spot] = first[:, group]
        w_cols[pl.ds(pl.multiple_of((1 - half) * half_rows, half_rows), half_rows), spot] = second[:, group]


def project_kernel(own, core, pair, far, w_cols, q_ref, *refs):
    width = own.shape[1]
    for at, source in enumerate((own, core, pair, far)):
        rows = slice(at * PART, (at + 1) * PART)
        made = dot_nn(source[...], w_cols[...])
        q_ref[rows, :] = made[:, 0:PART].astype(BF) * jnp.asarray(1.0 / math.sqrt(width // HEADS), BF)
        for spot, outs in ((slice(PART, 2 * PART), refs[:2]), (slice(2 * PART, 3 * PART), refs[2:])):
            part = made[:, spot].astype(BF)
            outs[0][rows, :] = part
            for copy in range(outs[1].shape[0]):
                outs[1][copy, rows, :] = part


def early_kernel(
    f_own, f_core, f_pair, f_far, own, core, pair, far, wout,
    do_ref, delta_ref, feat_t_ref, o_ref, saved, dys,
):
    y_bit = lax.axis_index("gy") % 2
    z_bit = lax.axis_index("gz") % 2
    width = f_own.shape[1]
    half = width // 2
    last = PART + width
    for at, (source, spot) in enumerate(((own, last), (core, 0), (pair, 0), (far, last))):
        rows = slice(at * PART, (at + 1) * PART)
        saved[rows, :] = source[:, spot : spot + PART]
        dys[rows, :] = source[:, PART:last]
    for at, source in enumerate((f_own, f_core, f_pair, f_far)):
        wanted = source[:, pl.ds(pl.multiple_of(z_bit * half, PART), half)]
        feat_t_ref[:, at * PART : (at + 1) * PART] = wanted.astype(F32).T.astype(BF)
    w_rows = wout[pl.ds(pl.multiple_of(y_bit * PART, PART), PART), :]
    out_grad = dot_nt(dys[...], w_rows).astype(BF)
    do_ref[...] = out_grad
    head_dim = width // HEADS
    products = (out_grad.astype(F32) * saved[...].astype(F32)).T
    delta_ref[0:1, :] = jnp.sum(products[0:head_dim], axis=0, keepdims=True)
    delta_ref[1:2, :] = jnp.sum(products[head_dim:PART], axis=0, keepdims=True)
    out = dot_nn(saved[...].astype(F32).T.astype(BF), dys[...]).astype(BF)
    for at in range(4):
        low = out[at * 32 : (at + 1) * 32, :]
        o_ref[at * 64 : at * 64 + 32, :] = low[:, 0:half]
        o_ref[at * 64 + 32 : at * 64 + 64, :] = low[:, half:]


def ring_places(count):
    at_x = lax.axis_index("gx")
    return (lax.rem(at_x + count - 1, count), lax.rem(at_x + 1, count))


def load_blocks(store, ring, refs):
    store[0] = refs[0][...]
    if ring:
        for at, place in enumerate(ring_places(ring)):
            store[1 + at] = refs[1][place]
    first = 3 if ring else 1
    for at, ref in enumerate(refs[2 if ring else 1 :]):
        store[first + at] = ref[...]


def store_blocks(store, ring, refs):
    refs[0][...] = store[0]
    if ring:
        before, after = ring_places(ring)
        refs[1][lax.rem(before + ring - 1, ring)] = store[0]
        refs[1][lax.axis_index("gx")] = store[0]
        refs[1][before] = store[1]
        refs[1][after] = store[2]
    first = 3 if ring else 1
    for at, ref in enumerate(refs[2 if ring else 1 :]):
        ref[...] = store[first + at]


def by_head(value):
    low = lax.broadcasted_iota(jnp.int32, value.shape, 1) < PART // 2
    none = jnp.zeros_like(value)
    return (jnp.where(low, value, none), jnp.where(low, none, value))


def row_scale(table, at, tokens):
    low = lax.broadcasted_iota(jnp.int32, (tokens, PART), 1) < PART // 2
    return jnp.where(low, table[:, 2 * at : 2 * at + 1], table[:, 2 * at + 1 : 2 * at + 2])


def score_kernel(times, ring, q_ref, do_ref, *refs):
    count = len(times)
    arrays = count - 1 if ring else count
    e_ref, part_ref = refs[arrays : arrays + 2]
    keys_s, top_s, total_s, fcol_s, dv_s = refs[2 * arrays + 2 :]
    tokens = q_ref.shape[0]
    load_blocks(keys_s, ring, refs[:arrays])
    q_heads = by_head(q_ref[...])

    def first(at, carry):
        keys = keys_s[at]
        for head in range(2):
            scores = dot_nt(keys, q_heads[head])
            top = jnp.max(scores, axis=0, keepdims=True)
            grown = jnp.exp(scores - top)
            e_ref[2 * at + head] = grown.astype(BF)
            top_s[pl.ds(2 * at + head, 1), :] = top
            total_s[pl.ds(2 * at + head, 1), :] = jnp.sum(grown, axis=0, keepdims=True)
        return carry

    lax.fori_loop(0, count, first, 0)
    for head in range(2):
        tops = [top_s[2 * at + head : 2 * at + head + 1, :] for at in range(count)]
        most = functools.reduce(jnp.maximum, tops)
        lifts = [jnp.exp(top - most) for top in tops]
        total = functools.reduce(
            jnp.add,
            [
                times[at] * lifts[at] * total_s[2 * at + head : 2 * at + head + 1, :]
                for at in range(count)
            ],
        )
        for at in range(count):
            part_ref[2 * at + head : 2 * at + head + 1, :] = lifts[at] / total
    if part_ref.shape[0] > 2 * count:
        part_ref[2 * count :, :] = jnp.zeros((part_ref.shape[0] - 2 * count, tokens), F32)
    turned = part_ref[...].T
    for at in range(count):
        fcol_s[at] = row_scale(turned, at, tokens)
    grad = do_ref[...].astype(F32)

    def second(at, carry):
        g_heads = by_head((grad * fcol_s[at]).astype(BF))
        dv_s[at] = (dot_nn(e_ref[2 * at], g_heads[0]) + dot_nn(e_ref[2 * at + 1], g_heads[1])).astype(BF)
        return carry

    lax.fori_loop(0, count, second, 0)
    store_blocks(dv_s, ring, refs[arrays + 2 : 2 * arrays + 2])


def gradient_kernel(times, ring, q_ref, do_ref, delta_ref, e_ref, part_ref, *refs):
    count = len(times)
    arrays = count - 1 if ring else count
    dq_ref = refs[2 * arrays]
    keys_s, values_s, f_s, fcol_s, dq_s, dk_s = refs[3 * arrays + 1 :]
    tokens = q_ref.shape[0]
    head_dim = PART // 2
    turned = part_ref[...].T
    load_blocks(keys_s, ring, refs[:arrays])
    load_blocks(values_s, ring, refs[arrays : 2 * arrays])
    for at in range(count):
        fcol_s[at] = row_scale(turned, at, tokens)
        f_s[2 * at : 2 * at + 2, :] = part_ref[2 * at : 2 * at + 2, :] * times[at]
    g_heads = by_head(do_ref[...])
    query = q_ref[...].astype(F32)
    delta = delta_ref[...]
    dq_s[...] = jnp.zeros_like(dq_s)

    def step(at, carry):
        keys_t = keys_s[at].astype(F32).T.astype(BF)
        values = values_s[at]
        q_heads = by_head((query * fcol_s[at]).astype(BF))
        dk = jnp.zeros((tokens, PART), F32)
        for head in range(2):
            dprob = dot_nt(values, g_heads[head])
            dscore = (e_ref[2 * at + head].astype(F32) * (dprob - delta[head : head + 1, :])).astype(BF)
            dk = dk + dot_nn(dscore, q_heads[head])
            spot = slice(head * head_dim, (head + 1) * head_dim)
            dq_s[spot, :] = dq_s[spot, :] + dot_nn(keys_t[spot, :], dscore) * f_s[
                pl.ds(2 * at + head, 1), :
            ]
        dk_s[at] = dk.astype(BF)
        return carry

    lax.fori_loop(0, count, step, 0)
    store_blocks(dk_s, ring, refs[2 * arrays + 1 : 3 * arrays + 1])
    dq_ref[...] = (dq_s[...].T * (1.0 / math.sqrt(head_dim))).astype(BF)


def combined(times, ring, refs):
    total = times[0] * refs[0][...].astype(F32)
    if ring:
        for at, place in enumerate(ring_places(ring)):
            total = total + times[1 + at] * refs[1][place].astype(F32)
    first = 3 if ring else 1
    for time, ref in zip(times[first:], refs[2 if ring else 1 :]):
        total = total + time * ref[...].astype(F32)
    return total.astype(BF)


def collect_values_kernel(times, ring, dq_ref, *refs):
    refs[-1][:, 0:PART] = dq_ref[...]
    refs[-1][:, PART:] = combined(times, ring, refs[:-1])


def collect_keys_kernel(times, ring, *refs):
    refs[-1][...] = combined(times, ring, refs[:-1])


def place_grads(grads, own, core, count):
    z_bit = lax.axis_index("gz") % 2
    for at in range(count):
        source = slice(at * PART, (at + 1) * PART)
        grads[:, columns(at * 2 * PART + z_bit * PART)] = own[:, source]
        core_at = columns(at * 2 * PART + (1 - z_bit) * PART)
        for low in range(4):
            grads[low * PART : (low + 1) * PART, core_at] = core[
                (low ^ 1) * PART : ((low ^ 1) + 1) * PART, source
            ]


def weight_early_kernel(own, core, feat_t, o_ref, held_ref, rows_ref, grads):
    place_grads(grads, own, core, 2)
    wide = grads.shape[1]
    held_ref[:, 0:wide] = dot_nn(feat_t[...], grads[...]).astype(BF)
    held_ref[:, wide:] = o_ref[...]
    rows_ref[0] = grads[0:PART, :]
    rows_ref[1] = grads[2 * PART : 3 * PART, :]


def weight_late_kernel(own, core, feat_t, held_ref, rows_ref, pair_ref, mine_ref, out_ref, grads):
    place_grads(grads, own, core, 1)
    early = rows_ref.shape[2]
    mine_ref[:, 0:early] = rows_ref[0]
    mine_ref[:, early:] = grads[0:PART, :]
    pair_ref[:, 0:early] = rows_ref[1]
    pair_ref[:, early:] = grads[2 * PART : 3 * PART, :]
    wide = held_ref.shape[1]
    out_ref[:, 0:wide] = held_ref[...]
    out_ref[:, wide:] = dot_nn(feat_t[...], grads[...]).astype(BF)


def grad_x_kernel(own_half, mine, pair, wq0, wq1, wk0, wk1, wv0, wv1, out, full):
    y_bit = lax.axis_index("gy") % 2
    z_bit = lax.axis_index("gz") % 2
    half = z_bit if own_half else z_bit * 0
    width = wq0.shape[1]
    half_rows = wq0.shape[0]
    for at in range(3):
        for side in range(2):
            spot = slice((at * 2 + side) * PART, (at * 2 + side + 1) * PART)
            base = at * width + side * 2 * PART
            full[:, columns(base + y_bit * PART)] = mine[:, spot]
            full[:, columns(base + (1 - y_bit) * PART)] = pair[:, spot]
    for at, sources in ((half, (wq0, wv0, wk0)), (1 - half, (wq1, wv1, wk1))):
        total = functools.reduce(
            jnp.add,
            [dot_nt(full[:, n * width : (n + 1) * width], sources[n][...]) for n in range(3)],
        )
        out[:, pl.ds(pl.multiple_of(at * half_rows, PART), half_rows)] = total.astype(BF)


def sum_kernel(in_ref, out_ref):
    rows = out_ref.shape[0]
    total = in_ref[0:rows, :].astype(F32)
    for at in range(1, in_ref.shape[0] // rows):
        total = total + in_ref[at * rows : (at + 1) * rows, :].astype(F32)
    out_ref[...] = total.astype(BF)


def pair_sum_kernel(left, right, out_ref):
    out_ref[...] = (left[...].astype(F32) + right[...].astype(F32)).astype(BF)


def spread_kernel(pieces, *outs):
    half = 2 * PART
    rows = pieces.shape[2]
    for place in range(pieces.shape[0]):
        for other in range(2):
            piece = pieces[place, other]
            bit = (lax.axis_index("gy") % 2) ^ other
            spot = slice(place * rows, (place + 1) * rows)
            for base, out in ((0, outs[0]), (3, outs[1]), (1, outs[2])):
                for side in range(2):
                    source = slice((base * 2 + side) * PART, (base * 2 + side + 1) * PART)
                    out[spot, columns(side * half + bit * PART)] = piece[:, source].astype(F32)
            spot = pl.ds(pl.multiple_of(bit * PART + place * (rows // 2), rows // 2), rows // 2)
            outs[3][spot, 0:half] = piece[0 : rows // 2, 2 * half : 3 * half].astype(F32)
            outs[3][spot, half:] = piece[rows // 2 :, 2 * half : 3 * half].astype(F32)


def on_device(features, grad_y, attn_out, w_query, w_key, w_value, w_out):
    width = features.shape[-1]
    half = width // 2
    tokens = features.shape[0] * features.shape[1] * features.shape[2]
    block_tokens = 4 * tokens
    count_x, count_y, count_z = lax.axis_size("gx"), lax.axis_size("gy"), lax.axis_size("gz")
    z_bit = lax.axis_index("gz") % 2
    y_bit = lax.axis_index("gy") % 2

    own_half = count_z == 2
    if own_half:
        pairs = []
        for weight in (w_query, w_key, w_value):
            pairs += [weight, from_partner(weight, "gz")]
        out_rows = w_out
    else:
        pairs = []
        for weight in (w_query, w_key, w_value):
            whole = lax.all_gather(weight, "gz", axis=0, tiled=True)
            pairs += [whole[:half], whole[half:]]
        whole = lax.all_gather(w_out, "gz", axis=0, tiled=True)
        out_rows = lax.dynamic_slice_in_dim(whole, z_bit * half, half, 0)

    message = shape_of((tokens, width + 2 * PART))
    feat = features.reshape(tokens, width)
    feat_pair = from_partner(feat, "gy")
    feat_core = from_partner(feat, "gz")
    w_cols = call(
        functools.partial(columns_kernel, own_half), shape_of((width, 3 * PART)), pairs
    )
    feat_pair, feat_core, w_cols = lax.optimization_barrier((feat_pair, feat_core, w_cols))
    feat_far = from_partner(feat_pair, "gz")
    feats = [feat, feat_core, feat_pair, feat_far]
    column = shape_of((block_tokens, PART))
    ring = 4 if count_x == 4 else 0
    copies = shape_of((max(ring, 1), block_tokens, PART))
    query, own_keys, key_copies, own_values, value_copies = call(
        project_kernel,
        (column, column, copies, column, copies),
        [*feats, w_cols],
        flops=2 * block_tokens * width * 3 * PART,
    )
    pair_message, own = call(
        pack_kernel,
        (message, message),
        [value.reshape(tokens, width) for value in (grad_y, attn_out)],
    )
    pair = from_partner(pair_message, "gy")
    pair, query = lax.optimization_barrier((pair, query))
    core = from_partner(own, "gz")
    far = from_partner(pair, "gz")

    times = [1.0]
    routes = []
    for axis, step, blocks in (("gx", 1, count_x), ("gy", 2, count_y // 2), ("gz", 2, count_z // 2)):
        if blocks == 1:
            times[0] += 2.0
        elif blocks == 2:
            routes.append((axis, step))
            times.append(2.0)
        else:
            routes += [(axis, step), (axis, -step)]
            times += [1.0, 1.0]
    times = tuple(times)
    count = len(times)

    def across(value):
        return lax.all_to_all(value, "gx", 0, 0, tiled=True)

    def sent(own_part, copies_part):
        if not ring:
            return [own_part] + [shifted(own_part, axis, step) for axis, step in routes]
        others = [shifted(own_part, axis, step) for axis, step in routes[2:]]
        return [own_part, across(copies_part)] + others

    def returned(parts):
        if not ring:
            return [parts[0]] + [
                shifted(part, axis, -step) for part, (axis, step) in zip(parts[1:], routes)
            ]
        others = [shifted(part, axis, -step) for part, (axis, step) in zip(parts[2:], routes[2:])]
        return [parts[0], across(parts[1])] + others

    keys = sent(own_keys, key_copies)
    values = sent(own_values, value_copies)
    partial_shapes = [column] * count if not ring else [column, copies] + [column] * (count - 3)
    out_grad, delta, feat_t, out_term = call(
        early_kernel,
        (
            column,
            shape_of((2, block_tokens), F32),
            shape_of((half, block_tokens)),
            shape_of((half, half)),
        ),
        [*feats, own, core, pair, far, out_rows],
        scratch=[pltpu.VMEM((block_tokens, PART), BF), pltpu.VMEM((block_tokens, width), BF)],
        flops=4 * block_tokens * width * PART,
    )
    rows = -(-2 * count // 8) * 8
    pixels = 2 * count * block_tokens * block_tokens
    grown, parts, *dvs = call(
        functools.partial(score_kernel, times, ring),
        (
            shape_of((2 * count, block_tokens, block_tokens)),
            shape_of((rows, block_tokens), F32),
            *partial_shapes,
        ),
        [query, out_grad, *keys],
        scratch=[
            pltpu.VMEM((count, block_tokens, PART), BF),
            pltpu.VMEM((rows, block_tokens), F32),
            pltpu.VMEM((rows, block_tokens), F32),
            pltpu.VMEM((count, block_tokens, PART), F32),
            pltpu.VMEM((count, block_tokens, PART), BF),
        ],
        flops=4 * pixels * PART,
        moved=2 * pixels,
        exps=pixels,
    )
    dv_back = returned(dvs)
    dq, *dks = call(
        functools.partial(gradient_kernel, times, ring),
        (column, *partial_shapes),
        [query, out_grad, delta, grown, parts, *keys, *values],
        scratch=[
            pltpu.VMEM((count, block_tokens, PART), BF),
            pltpu.VMEM((count, block_tokens, PART), BF),
            pltpu.VMEM((rows, block_tokens), F32),
            pltpu.VMEM((count, block_tokens, PART), F32),
            pltpu.VMEM((PART, block_tokens), F32),
            pltpu.VMEM((count, block_tokens, PART), BF),
        ],
        flops=6 * pixels * PART,
        moved=2 * pixels,
    )
    dk_back = returned(dks)
    early = call(
        functools.partial(collect_values_kernel, times, ring),
        shape_of((block_tokens, 2 * PART)),
        [dq, *dv_back],
    )
    early_core = from_partner(early, "gz")
    planned = count_x == 4 and count_y == 4 and count_z == 2
    piece = shape_of((half // 4, 8 * PART))
    held, early_rows = call(
        weight_early_kernel,
        (shape_of((half, 6 * PART)), shape_of((2, tokens, 4 * PART))),
        [early, early_core, feat_t, out_term],
        scratch=[pltpu.VMEM((block_tokens, 4 * PART), BF)],
        flops=2 * block_tokens * half * 4 * PART,
    )
    late = call(functools.partial(collect_keys_kernel, times, ring), column, dk_back)
    late_core = from_partner(late, "gz")
    pair_out, mine, terms = call(
        weight_late_kernel,
        (shape_of((tokens, 6 * PART)), shape_of((tokens, 6 * PART)), shape_of((half, 8 * PART))),
        [late, late_core, feat_t, held, early_rows],
        scratch=[pltpu.VMEM((block_tokens, 2 * PART), BF)],
        flops=2 * block_tokens * half * 2 * PART,
    )
    pair_in = from_partner(pair_out, "gy")
    if planned:
        total = call(sum_kernel, piece, [across(terms)])
        total = call(pair_sum_kernel, piece, [total, plane_swap(total, 0, 2)])
        both = jnp.stack([total, plane_swap(total, 0, 1)])
        weights = call(
            spread_kernel,
            tuple([shape_of((half, width), F32)] * 4),
            [lax.all_gather(both, "gx")],
        )
    else:
        terms = terms.astype(F32)
        stacked = jnp.zeros((4, width, width), F32)
        for base, at in ((0, 0), (3, 1), (1, 2)):
            for side in range(2):
                tile = terms[:, (base * 2 + side) * PART : (base * 2 + side + 1) * PART]
                stacked = lax.dynamic_update_slice(
                    stacked, tile[None], (at, z_bit * half, side * half + y_bit * PART)
                )
        tile = terms[:, 4 * PART : 6 * PART].reshape(4, 2, 32, half)
        tile = tile.transpose(0, 2, 1, 3).reshape(PART, width)
        stacked = lax.dynamic_update_slice(
            stacked, tile[None], (3, z_bit * half + y_bit * PART, 0)
        )
        stacked = lax.psum(stacked, ("gx", "gy", "gz"))
        held_rows = w_query.shape[0]
        stacked = lax.dynamic_slice_in_dim(stacked, lax.axis_index("gz") * held_rows, held_rows, 1)
        weights = [stacked[at] for at in range(4)]
    grad_x = call(
        functools.partial(grad_x_kernel, own_half),
        shape_of((tokens, width)),
        [mine, pair_in, *pairs],
        scratch=[pltpu.VMEM((tokens, 3 * width), BF)],
        flops=2 * tokens * 3 * width * width,
    ).reshape(features.shape)
    return (grad_x, *weights)


def solution(mesh):
    return jax.shard_map(
        on_device,
        mesh=mesh,
        in_specs=(
            P("gx", "gy", "gz", None),
            P("gx", "gy", "gz", None),
            P("gx", "gy", "gz", None),
            P("gz", None),
            P("gz", None),
            P("gz", None),
            P("gz", None),
        ),
        out_specs=(
            P("gx", "gy", "gz", None),
            P("gz", None),
            P("gz", None),
            P("gz", None),
            P("gz", None),
        ),
        check_vma=False,
    )
```

```python
import functools
import math

import jax
import jax.numpy as jnp
from jax import lax
from jax.experimental import pallas as pl
from jax.experimental.pallas import tpu as pltpu
from jax.sharding import PartitionSpec as P

HEADS = 8
PART = 128
BF = jnp.bfloat16
F32 = jnp.float32
VMEM_BYTES = 32 * 1024 * 1024


def from_partner(block, axis):
    route = [(index, index ^ 1) for index in range(lax.axis_size(axis))]
    return lax.ppermute(block, axis, route)


def shifted(value, axis, steps):
    count = lax.axis_size(axis)
    return lax.ppermute(value, axis, [(source, (source + steps) % count) for source in range(count)])


def plane_swap(value, flip_x, flip_y):
    count_x, count_y = lax.axis_size("gx"), lax.axis_size("gy")
    route = []
    for at_x in range(count_x):
        for at_y in range(count_y):
            route.append((at_x * count_y + at_y, (at_x ^ flip_x) * count_y + (at_y ^ flip_y)))
    return lax.ppermute(value, ("gx", "gy"), route)


def dot_nn(left, right):
    return lax.dot_general(left, right, (((1,), (0,)), ((), ())), preferred_element_type=F32)


def dot_nt(left, right):
    return lax.dot_general(left, right, (((1,), (1,)), ((), ())), preferred_element_type=F32)


def dot_tn(left, right):
    return lax.dot_general(left, right, (((0,), (0,)), ((), ())), preferred_element_type=F32)


def columns(start):
    return pl.ds(pl.multiple_of(start, PART), PART)


def call(kernel, out_shape, args, scratch=(), flops=1e6, moved=1e6, exps=0):
    return pl.pallas_call(
        kernel,
        out_shape=out_shape,
        scratch_shapes=list(scratch),
        compiler_params=pltpu.CompilerParams(vmem_limit_bytes=VMEM_BYTES),
        cost_estimate=pl.CostEstimate(
            flops=int(flops), bytes_accessed=int(moved), transcendentals=int(exps)
        ),
    )(*args)


def shape_of(dims, dtype=BF):
    return jax.ShapeDtypeStruct(dims, dtype)


def pack_kernel(dy_ref, saved_ref, pair_ref, own_ref):
    y_bit = lax.axis_index("gy") % 2
    z_bit = lax.axis_index("gz") % 2
    last = PART + dy_ref.shape[1]
    for out in (pair_ref, own_ref):
        out[:, PART:last] = dy_ref[...]
    pair_ref[:, 0:PART] = saved_ref[:, columns((z_bit * 2 + 1 - y_bit) * PART)]
    pair_ref[:, last:] = saved_ref[:, columns(((1 - z_bit) * 2 + 1 - y_bit) * PART)]
    own_ref[:, 0:PART] = saved_ref[:, columns(((1 - z_bit) * 2 + y_bit) * PART)]
    own_ref[:, last:] = saved_ref[:, columns((z_bit * 2 + y_bit) * PART)]


def columns_kernel(own_half, wq0, wq1, wk0, wk1, wv0, wv1, w_cols):
    y_bit = lax.axis_index("gy") % 2
    z_bit = lax.axis_index("gz") % 2
    half = z_bit if own_half else z_bit * 0
    group = columns((z_bit * 2 + y_bit) * PART)
    half_rows = wq0.shape[0]
    for at, (first, second) in enumerate(((wq0, wq1), (wk0, wk1), (wv0, wv1))):
        spot = slice(at * PART, (at + 1) * PART)
        w_cols[pl.ds(pl.multiple_of(half * half_rows, half_rows), half_rows), spot] = first[:, group]
        w_cols[pl.ds(pl.multiple_of((1 - half) * half_rows, half_rows), half_rows), spot] = second[:, group]


def project_kernel(own, core, pair, far, w_cols, q_ref, k_ref, v_ref):
    width = own.shape[1]
    for at, source in enumerate((own, core, pair, far)):
        rows = slice(at * PART, (at + 1) * PART)
        made = dot_nn(source[...], w_cols[...])
        q_ref[rows, :] = made[:, 0:PART].astype(BF) * jnp.asarray(1.0 / math.sqrt(width // HEADS), BF)
        k_ref[rows, :] = made[:, PART : 2 * PART].astype(BF)
        v_ref[rows, :] = made[:, 2 * PART :].astype(BF)


def early_kernel(
    f_own, f_core, f_pair, f_far, own, core, pair, far, wout,
    do_ref, delta_ref, feat_t_ref, o_ref, saved, dys,
):
    y_bit = lax.axis_index("gy") % 2
    z_bit = lax.axis_index("gz") % 2
    width = f_own.shape[1]
    half = width // 2
    last = PART + width
    for at, (source, spot) in enumerate(((own, last), (core, 0), (pair, 0), (far, last))):
        rows = slice(at * PART, (at + 1) * PART)
        saved[rows, :] = source[:, spot : spot + PART]
        dys[rows, :] = source[:, PART:last]
    for at, source in enumerate((f_own, f_core, f_pair, f_far)):
        wanted = source[:, pl.ds(pl.multiple_of(z_bit * half, PART), half)]
        feat_t_ref[:, at * PART : (at + 1) * PART] = wanted.astype(F32).T.astype(BF)
    w_rows = wout[pl.ds(pl.multiple_of(y_bit * PART, PART), PART), :]
    out_grad = dot_nt(dys[...], w_rows).astype(BF)
    do_ref[...] = out_grad
    head_dim = width // HEADS
    products = (out_grad.astype(F32) * saved[...].astype(F32)).T
    delta_ref[0:1, :] = jnp.sum(products[0:head_dim], axis=0, keepdims=True)
    delta_ref[1:2, :] = jnp.sum(products[head_dim:PART], axis=0, keepdims=True)
    out = dot_nn(saved[...].astype(F32).T.astype(BF), dys[...]).astype(BF)
    for at in range(4):
        low = out[at * 32 : (at + 1) * 32, :]
        o_ref[at * 64 : at * 64 + 32, :] = low[:, 0:half]
        o_ref[at * 64 + 32 : at * 64 + 64, :] = low[:, half:]


def by_head(value):
    low = lax.broadcasted_iota(jnp.int32, value.shape, 1) < PART // 2
    none = jnp.zeros_like(value)
    return (jnp.where(low, value, none), jnp.where(low, none, value))


def row_scale(table, at, tokens):
    low = lax.broadcasted_iota(jnp.int32, (tokens, PART), 1) < PART // 2
    return jnp.where(low, table[:, 2 * at : 2 * at + 1], table[:, 2 * at + 1 : 2 * at + 2])


def score_kernel(times, q_ref, do_ref, *refs):
    count = len(times)
    keys_in = refs[:count]
    e_ref, part_ref = refs[count : count + 2]
    dvs = refs[count + 2 : 2 * count + 2]
    keys_s, top_s, total_s, fcol_s, dv_s = refs[2 * count + 2 :]
    tokens = q_ref.shape[0]
    for at in range(count):
        keys_s[at] = keys_in[at][...]
    q_heads = by_head(q_ref[...])

    def first(at, carry):
        keys = keys_s[at]
        for head in range(2):
            scores = dot_nt(keys, q_heads[head])
            top = jnp.max(scores, axis=0, keepdims=True)
            grown = jnp.exp(scores - top)
            e_ref[2 * at + head] = grown.astype(BF)
            top_s[pl.ds(2 * at + head, 1), :] = top
            total_s[pl.ds(2 * at + head, 1), :] = jnp.sum(grown, axis=0, keepdims=True)
        return carry

    lax.fori_loop(0, count, first, 0, unroll=True)
    for head in range(2):
        tops = [top_s[2 * at + head : 2 * at + head + 1, :] for at in range(count)]
        most = functools.reduce(jnp.maximum, tops)
        lifts = [jnp.exp(top - most) for top in tops]
        total = functools.reduce(
            jnp.add,
            [
                times[at] * lifts[at] * total_s[2 * at + head : 2 * at + head + 1, :]
                for at in range(count)
            ],
        )
        for at in range(count):
            part_ref[2 * at + head : 2 * at + head + 1, :] = lifts[at] / total
    if part_ref.shape[0] > 2 * count:
        part_ref[2 * count :, :] = jnp.zeros((part_ref.shape[0] - 2 * count, tokens), F32)
    turned = part_ref[...].T
    for at in range(count):
        fcol_s[at] = row_scale(turned, at, tokens)
    grad = do_ref[...].astype(F32)

    def second(at, carry):
        g_heads = by_head((grad * fcol_s[at]).astype(BF))
        dv_s[at] = (dot_nn(e_ref[2 * at], g_heads[0]) + dot_nn(e_ref[2 * at + 1], g_heads[1])).astype(BF)
        return carry

    lax.fori_loop(0, count, second, 0, unroll=True)
    for at in range(count):
        dvs[at][...] = dv_s[at]


def gradient_kernel(times, q_ref, do_ref, delta_ref, e_ref, part_ref, *refs):
    count = len(times)
    keys_in, values_in = refs[:count], refs[count : 2 * count]
    dq_ref = refs[2 * count]
    dks = refs[2 * count + 1 : 3 * count + 1]
    keys_s, values_s, f_s, fcol_s, dq_s, dk_s = refs[3 * count + 1 :]
    tokens = q_ref.shape[0]
    head_dim = PART // 2
    turned = part_ref[...].T
    for at in range(count):
        keys_s[at] = keys_in[at][...]
        values_s[at] = values_in[at][...]
        fcol_s[at] = row_scale(turned, at, tokens)
        f_s[2 * at : 2 * at + 2, :] = part_ref[2 * at : 2 * at + 2, :] * times[at]
    g_heads = by_head(do_ref[...])
    query = q_ref[...].astype(F32)
    delta = delta_ref[...]
    dq_s[...] = jnp.zeros_like(dq_s)

    def step(at, carry):
        keys_t = keys_s[at].astype(F32).T.astype(BF)
        values = values_s[at]
        q_heads = by_head((query * fcol_s[at]).astype(BF))
        dk = jnp.zeros((tokens, PART), F32)
        for head in range(2):
            dprob = dot_nt(values, g_heads[head])
            dscore = (e_ref[2 * at + head].astype(F32) * (dprob - delta[head : head + 1, :])).astype(BF)
            dk = dk + dot_nn(dscore, q_heads[head])
            spot = slice(head * head_dim, (head + 1) * head_dim)
            dq_s[spot, :] = dq_s[spot, :] + dot_nn(keys_t[spot, :], dscore) * f_s[
                pl.ds(2 * at + head, 1), :
            ]
        dk_s[at] = dk.astype(BF)
        return carry

    lax.fori_loop(0, count, step, 0, unroll=True)
    for at in range(count):
        dks[at][...] = dk_s[at]
    dq_ref[...] = (dq_s[...].T * (1.0 / math.sqrt(head_dim))).astype(BF)


def combined(times, refs):
    total = times[0] * refs[0][...].astype(F32)
    for time, ref in zip(times[1:], refs[1:]):
        total = total + time * ref[...].astype(F32)
    return total.astype(BF)


def collect_values_kernel(times, dq_ref, *refs):
    refs[-1][:, 0:PART] = dq_ref[...]
    refs[-1][:, PART:] = combined(times, refs[:-1])


def collect_keys_kernel(times, *refs):
    refs[-1][...] = combined(times, refs[:-1])


def place_grads(grads, own, core, count):
    z_bit = lax.axis_index("gz") % 2
    for at in range(count):
        source = slice(at * PART, (at + 1) * PART)
        grads[:, columns(at * 2 * PART + z_bit * PART)] = own[:, source]
        core_at = columns(at * 2 * PART + (1 - z_bit) * PART)
        for low in range(4):
            grads[low * PART : (low + 1) * PART, core_at] = core[
                (low ^ 1) * PART : ((low ^ 1) + 1) * PART, source
            ]


def weight_early_kernel(own, core, feat_t, o_ref, held_ref, rows_ref, grads):
    place_grads(grads, own, core, 2)
    wide = grads.shape[1]
    held_ref[:, 0:wide] = dot_nn(feat_t[...], grads[...]).astype(BF)
    held_ref[:, wide:] = o_ref[...]
    rows_ref[0] = grads[0:PART, :]
    rows_ref[1] = grads[2 * PART : 3 * PART, :]


def weight_late_kernel(chunks, own, core, feat_t, held_ref, rows_ref, pair_ref, mine_ref, *refs):
    outs, (grads, made) = refs[:chunks], refs[chunks:]
    place_grads(grads, own, core, 1)
    early = rows_ref.shape[2]
    mine_ref[:, 0:early] = rows_ref[0]
    mine_ref[:, early:] = grads[0:PART, :]
    pair_ref[:, 0:early] = rows_ref[1]
    pair_ref[:, early:] = grads[2 * PART : 3 * PART, :]
    made[...] = dot_nn(feat_t[...], grads[...]).astype(BF)
    rows = made.shape[0] // chunks
    wide = held_ref.shape[1]
    for at in range(chunks):
        spot = pl.ds(0, rows)
        if chunks > 1:
            spot = pl.ds(pl.multiple_of((lax.axis_index("gx") ^ at) * rows, rows), rows)
        outs[at][:, 0:wide] = held_ref[spot, :]
        outs[at][:, wide:] = made[spot, :]


def grad_x_kernel(own_half, mine, pair, wq0, wq1, wk0, wk1, wv0, wv1, out, full):
    y_bit = lax.axis_index("gy") % 2
    z_bit = lax.axis_index("gz") % 2
    half = z_bit if own_half else z_bit * 0
    width = wq0.shape[1]
    half_rows = wq0.shape[0]
    for at in range(3):
        for side in range(2):
            spot = slice((at * 2 + side) * PART, (at * 2 + side + 1) * PART)
            base = at * width + side * 2 * PART
            full[:, columns(base + y_bit * PART)] = mine[:, spot]
            full[:, columns(base + (1 - y_bit) * PART)] = pair[:, spot]
    for at, sources in ((half, (wq0, wv0, wk0)), (1 - half, (wq1, wv1, wk1))):
        total = functools.reduce(
            jnp.add,
            [dot_nt(full[:, n * width : (n + 1) * width], sources[n][...]) for n in range(3)],
        )
        out[:, pl.ds(pl.multiple_of(at * half_rows, PART), half_rows)] = total.astype(BF)


def sum_kernel(*refs):
    total = refs[0][...].astype(F32)
    for ref in refs[1:-1]:
        total = total + ref[...].astype(F32)
    refs[-1][...] = total.astype(BF)


def spread_kernel(*refs):
    pieces, outs = refs[:8], refs[8:]
    half = 2 * PART
    rows = pieces[0].shape[0]
    for at, piece in enumerate(pieces):
        place = lax.axis_index("gx") ^ (at // 2)
        bit = (lax.axis_index("gy") % 2) ^ (at % 2)
        spot = pl.ds(pl.multiple_of(place * rows, rows), rows)
        for base, out in ((0, outs[0]), (3, outs[1]), (1, outs[2])):
            for side in range(2):
                source = slice((base * 2 + side) * PART, (base * 2 + side + 1) * PART)
                out[spot, columns(side * half + bit * PART)] = piece[:, source].astype(F32)
        spot = pl.ds(pl.multiple_of(bit * PART + place * (rows // 2), rows // 2), rows // 2)
        outs[3][spot, 0:half] = piece[0 : rows // 2, 2 * half : 3 * half].astype(F32)
        outs[3][spot, half:] = piece[rows // 2 :, 2 * half : 3 * half].astype(F32)


def on_device(features, grad_y, attn_out, w_query, w_key, w_value, w_out):
    width = features.shape[-1]
    half = width // 2
    tokens = features.shape[0] * features.shape[1] * features.shape[2]
    block_tokens = 4 * tokens
    count_x, count_y, count_z = lax.axis_size("gx"), lax.axis_size("gy"), lax.axis_size("gz")
    z_bit = lax.axis_index("gz") % 2
    y_bit = lax.axis_index("gy") % 2

    own_half = count_z == 2
    if own_half:
        pairs = []
        for weight in (w_query, w_key, w_value):
            pairs += [weight, from_partner(weight, "gz")]
        out_rows = w_out
    else:
        pairs = []
        for weight in (w_query, w_key, w_value):
            whole = lax.all_gather(weight, "gz", axis=0, tiled=True)
            pairs += [whole[:half], whole[half:]]
        whole = lax.all_gather(w_out, "gz", axis=0, tiled=True)
        out_rows = lax.dynamic_slice_in_dim(whole, z_bit * half, half, 0)

    message = shape_of((tokens, width + 2 * PART))
    feat = features.reshape(tokens, width)
    feat_pair = from_partner(feat, "gy")
    feat_core = from_partner(feat, "gz")
    w_cols = call(
        functools.partial(columns_kernel, own_half), shape_of((width, 3 * PART)), pairs
    )
    pair_message, own = call(
        pack_kernel,
        (message, message),
        [value.reshape(tokens, width) for value in (grad_y, attn_out)],
    )
    feat_pair, feat_core, w_cols, own = lax.optimization_barrier(
        (feat_pair, feat_core, w_cols, own)
    )
    pair = from_partner(pair_message, "gy")
    feat_far = from_partner(feat_pair, "gz")
    feats = [feat, feat_core, feat_pair, feat_far]
    column = shape_of((block_tokens, PART))
    query, own_keys, own_values = call(
        project_kernel,
        (column, column, column),
        [*feats, w_cols],
        flops=2 * block_tokens * width * 3 * PART,
    )
    pair, query = lax.optimization_barrier((pair, query))
    core = from_partner(own, "gz")
    far = from_partner(pair, "gz")

    times = [1.0]
    routes = []
    for axis, step, blocks in (("gx", 1, count_x), ("gy", 2, count_y // 2), ("gz", 2, count_z // 2)):
        if blocks == 1:
            times[0] += 2.0
        elif blocks == 2:
            routes.append((axis, step))
            times.append(2.0)
        else:
            routes += [(axis, step), (axis, -step)]
            times += [1.0, 1.0]
    times = tuple(times)
    count = len(times)
    keys = [own_keys] + [shifted(own_keys, axis, step) for axis, step in routes]
    out_grad, delta, feat_t, out_term = call(
        early_kernel,
        (
            column,
            shape_of((2, block_tokens), F32),
            shape_of((half, block_tokens)),
            shape_of((half, half)),
        ),
        [*feats, own, core, pair, far, out_rows],
        scratch=[pltpu.VMEM((block_tokens, PART), BF), pltpu.VMEM((block_tokens, width), BF)],
        flops=4 * block_tokens * width * PART,
    )
    own_values, out_grad = lax.optimization_barrier((own_values, out_grad))
    values = [own_values] + [shifted(own_values, axis, step) for axis, step in routes]
    rows = -(-2 * count // 8) * 8
    pixels = 2 * count * block_tokens * block_tokens
    grown, parts, *dvs = call(
        functools.partial(score_kernel, times),
        (
            shape_of((2 * count, block_tokens, block_tokens)),
            shape_of((rows, block_tokens), F32),
            *[column] * count,
        ),
        [query, out_grad, *keys],
        scratch=[
            pltpu.VMEM((count, block_tokens, PART), BF),
            pltpu.VMEM((rows, block_tokens), F32),
            pltpu.VMEM((rows, block_tokens), F32),
            pltpu.VMEM((count, block_tokens, PART), F32),
            pltpu.VMEM((count, block_tokens, PART), BF),
        ],
        flops=4 * pixels * PART,
        moved=2 * pixels,
        exps=pixels,
    )
    dv_back = [dvs[0]]
    for partial, (axis, step) in zip(dvs[1:], routes):
        dv_back.append(shifted(partial, axis, -step))
    dq, *dks = call(
        functools.partial(gradient_kernel, times),
        (column, *[column] * count),
        [query, out_grad, delta, grown, parts, *keys, *values],
        scratch=[
            pltpu.VMEM((count, block_tokens, PART), BF),
            pltpu.VMEM((count, block_tokens, PART), BF),
            pltpu.VMEM((rows, block_tokens), F32),
            pltpu.VMEM((count, block_tokens, PART), F32),
            pltpu.VMEM((PART, block_tokens), F32),
            pltpu.VMEM((count, block_tokens, PART), BF),
        ],
        flops=6 * pixels * PART,
        moved=2 * pixels,
    )
    dks, dv_back = lax.optimization_barrier((dks, dv_back))
    dk_back = [dks[0]]
    for partial, (axis, step) in zip(dks[1:], routes):
        dk_back.append(shifted(partial, axis, -step))
    early = call(
        functools.partial(collect_values_kernel, times),
        shape_of((block_tokens, 2 * PART)),
        [dq, *dv_back],
    )
    early_core = from_partner(early, "gz")
    planned = count_x == 4 and count_y == 4 and count_z == 2
    chunks = 4 if planned else 1
    piece = shape_of((half // chunks, 8 * PART))
    held, early_rows = call(
        weight_early_kernel,
        (shape_of((half, 6 * PART)), shape_of((2, tokens, 4 * PART))),
        [early, early_core, feat_t, out_term],
        scratch=[pltpu.VMEM((block_tokens, 4 * PART), BF)],
        flops=2 * block_tokens * half * 4 * PART,
    )
    late = call(functools.partial(collect_keys_kernel, times), column, dk_back)
    late_core = from_partner(late, "gz")
    pair_out, mine, *pieces = call(
        functools.partial(weight_late_kernel, chunks),
        (shape_of((tokens, 6 * PART)), shape_of((tokens, 6 * PART)), *[piece] * chunks),
        [late, late_core, feat_t, held, early_rows],
        scratch=[pltpu.VMEM((block_tokens, 2 * PART), BF), pltpu.VMEM((half, 2 * PART), BF)],
        flops=2 * block_tokens * half * 2 * PART,
    )
    pair_in = from_partner(pair_out, "gy")

    def features_grad(pair_rows):
        return call(
            functools.partial(grad_x_kernel, own_half),
            shape_of((tokens, width)),
            [mine, pair_rows, *pairs],
            scratch=[pltpu.VMEM((tokens, 3 * width), BF)],
            flops=2 * tokens * 3 * width * width,
        ).reshape(features.shape)

    if planned:
        terms = [pieces[0]] + [plane_swap(pieces[at], at, 0) for at in (1, 2, 3)]
        total = call(sum_kernel, piece, terms)
        total, pair_in = lax.optimization_barrier((total, pair_in))
        other = plane_swap(total, 0, 2)
        grad_x = features_grad(pair_in)
        total, grad_x = lax.optimization_barrier((total, grad_x))
        total = call(sum_kernel, piece, [total, other])
        by_x, by_y, by_z = plane_swap(total, 1, 0), plane_swap(total, 2, 0), plane_swap(total, 0, 1)
        by_xy, by_xz = plane_swap(by_y, 1, 0), plane_swap(by_x, 0, 1)
        by_yz, by_xyz = plane_swap(by_z, 2, 0), plane_swap(by_z, 3, 0)
        weights = call(
            spread_kernel,
            tuple([shape_of((half, width), F32)] * 4),
            [total, by_z, by_x, by_xz, by_y, by_yz, by_xy, by_xyz],
        )
    else:
        grad_x = features_grad(pair_in)
        terms = pieces[0].astype(F32)
        stacked = jnp.zeros((4, width, width), F32)
        for base, at in ((0, 0), (3, 1), (1, 2)):
            for side in range(2):
                tile = terms[:, (base * 2 + side) * PART : (base * 2 + side + 1) * PART]
                stacked = lax.dynamic_update_slice(
                    stacked, tile[None], (at, z_bit * half, side * half + y_bit * PART)
                )
        tile = terms[:, 4 * PART : 6 * PART].reshape(4, 2, 32, half)
        tile = tile.transpose(0, 2, 1, 3).reshape(PART, width)
        stacked = lax.dynamic_update_slice(
            stacked, tile[None], (3, z_bit * half + y_bit * PART, 0)
        )
        stacked = lax.psum(stacked, ("gx", "gy", "gz"))
        held_rows = w_query.shape[0]
        stacked = lax.dynamic_slice_in_dim(stacked, lax.axis_index("gz") * held_rows, held_rows, 1)
        weights = [stacked[at] for at in range(4)]
    return (grad_x, *weights)


def solution(mesh):
    return jax.shard_map(
        on_device,
        mesh=mesh,
        in_specs=(
            P("gx", "gy", "gz", None),
            P("gx", "gy", "gz", None),
            P("gx", "gy", "gz", None),
            P("gz", None),
            P("gz", None),
            P("gz", None),
            P("gz", None),
        ),
        out_specs=(
            P("gx", "gy", "gz", None),
            P("gz", None),
            P("gz", None),
            P("gz", None),
            P("gz", None),
        ),
        check_vma=False,
    )
```

```python
import functools
import math

import jax
import jax.numpy as jnp
from jax import lax
from jax.experimental import pallas as pl
from jax.experimental.pallas import tpu as pltpu
from jax.sharding import PartitionSpec as P

HEADS = 8
PART = 128
BF = jnp.bfloat16
F32 = jnp.float32
VMEM_BYTES = 32 * 1024 * 1024


def from_partner(block, axis):
    route = [(index, index ^ 1) for index in range(lax.axis_size(axis))]
    return lax.ppermute(block, axis, route)


def shifted(value, axis, steps):
    count = lax.axis_size(axis)
    return lax.ppermute(value, axis, [(source, (source + steps) % count) for source in range(count)])


def plane_swap(value, flip_x, flip_y):
    count_x, count_y = lax.axis_size("gx"), lax.axis_size("gy")
    route = []
    for at_x in range(count_x):
        for at_y in range(count_y):
            route.append((at_x * count_y + at_y, (at_x ^ flip_x) * count_y + (at_y ^ flip_y)))
    return lax.ppermute(value, ("gx", "gy"), route)


def dot_nn(left, right):
    return lax.dot_general(left, right, (((1,), (0,)), ((), ())), preferred_element_type=F32)


def dot_nt(left, right):
    return lax.dot_general(left, right, (((1,), (1,)), ((), ())), preferred_element_type=F32)


def dot_tn(left, right):
    return lax.dot_general(left, right, (((0,), (0,)), ((), ())), preferred_element_type=F32)


def columns(start):
    return pl.ds(pl.multiple_of(start, PART), PART)


def call(kernel, out_shape, args, scratch=(), flops=1e6, moved=1e6, exps=0, spaces=None):
    specs = [pl.BlockSpec(memory_space=space or pltpu.VMEM) for space in spaces or [None] * len(args)]
    return pl.pallas_call(
        kernel,
        out_shape=out_shape,
        in_specs=specs,
        scratch_shapes=list(scratch),
        compiler_params=pltpu.CompilerParams(vmem_limit_bytes=VMEM_BYTES),
        cost_estimate=pl.CostEstimate(
            flops=int(flops), bytes_accessed=int(moved), transcendentals=int(exps)
        ),
    )(*args)


def shape_of(dims, dtype=BF):
    return jax.ShapeDtypeStruct(dims, dtype)


def pack_kernel(dy_ref, saved_ref, pair_ref, own_ref):
    y_bit = lax.axis_index("gy") % 2
    z_bit = lax.axis_index("gz") % 2
    last = PART + dy_ref.shape[1]
    for out in (pair_ref, own_ref):
        out[:, PART:last] = dy_ref[...]
    pair_ref[:, 0:PART] = saved_ref[:, columns((z_bit * 2 + 1 - y_bit) * PART)]
    pair_ref[:, last:] = saved_ref[:, columns(((1 - z_bit) * 2 + 1 - y_bit) * PART)]
    own_ref[:, 0:PART] = saved_ref[:, columns(((1 - z_bit) * 2 + y_bit) * PART)]
    own_ref[:, last:] = saved_ref[:, columns((z_bit * 2 + y_bit) * PART)]


def columns_kernel(own_half, wq0, wq1, wk0, wk1, wv0, wv1, w_cols, sems):
    y_bit = lax.axis_index("gy") % 2
    z_bit = lax.axis_index("gz") % 2
    half = z_bit if own_half else z_bit * 0
    group = columns((z_bit * 2 + y_bit) * PART)
    half_rows = wq0.shape[0]
    copies = []
    for at, pair in enumerate(((wq0, wq1), (wk0, wk1), (wv0, wv1))):
        for side, source in enumerate(pair):
            place = half if side == 0 else 1 - half
            rows = pl.ds(pl.multiple_of(place * half_rows, half_rows), half_rows)
            copies.append(
                pltpu.make_async_copy(
                    source.at[:, group],
                    w_cols.at[rows, at * PART : (at + 1) * PART],
                    sems.at[2 * at + side],
                )
            )
    for copy in copies:
        copy.start()
    for copy in copies:
        copy.wait()


def project_kernel(own, core, pair, far, w_cols, q_ref, k_ref, v_ref):
    width = own.shape[1]
    for at, source in enumerate((own, core, pair, far)):
        rows = slice(at * PART, (at + 1) * PART)
        made = dot_nn(source[...], w_cols[...])
        q_ref[rows, :] = made[:, 0:PART].astype(BF) * jnp.asarray(1.0 / math.sqrt(width // HEADS), BF)
        k_ref[rows, :] = made[:, PART : 2 * PART].astype(BF)
        v_ref[rows, :] = made[:, 2 * PART :].astype(BF)


def early_kernel(
    f_own, f_core, f_pair, f_far, own, core, pair, far, wout,
    do_ref, delta_ref, feat_t_ref, o_ref, saved, dys,
):
    y_bit = lax.axis_index("gy") % 2
    z_bit = lax.axis_index("gz") % 2
    width = f_own.shape[1]
    half = width // 2
    last = PART + width
    for at, (source, spot) in enumerate(((own, last), (core, 0), (pair, 0), (far, last))):
        rows = slice(at * PART, (at + 1) * PART)
        saved[rows, :] = source[:, spot : spot + PART]
        dys[rows, :] = source[:, PART:last]
    for at, source in enumerate((f_own, f_core, f_pair, f_far)):
        wanted = source[:, pl.ds(pl.multiple_of(z_bit * half, PART), half)]
        feat_t_ref[:, at * PART : (at + 1) * PART] = wanted.astype(F32).T.astype(BF)
    w_rows = wout[pl.ds(pl.multiple_of(y_bit * PART, PART), PART), :]
    out_grad = dot_nt(dys[...], w_rows).astype(BF)
    do_ref[...] = out_grad
    head_dim = width // HEADS
    products = (out_grad.astype(F32) * saved[...].astype(F32)).T
    delta_ref[0:1, :] = jnp.sum(products[0:head_dim], axis=0, keepdims=True)
    delta_ref[1:2, :] = jnp.sum(products[head_dim:PART], axis=0, keepdims=True)
    out = dot_nn(saved[...].astype(F32).T.astype(BF), dys[...]).astype(BF)
    for at in range(4):
        low = out[at * 32 : (at + 1) * 32, :]
        o_ref[at * 64 : at * 64 + 32, :] = low[:, 0:half]
        o_ref[at * 64 + 32 : at * 64 + 64, :] = low[:, half:]


def by_head(value):
    low = lax.broadcasted_iota(jnp.int32, value.shape, 1) < PART // 2
    none = jnp.zeros_like(value)
    return (jnp.where(low, value, none), jnp.where(low, none, value))


def row_scale(table, at, tokens):
    low = lax.broadcasted_iota(jnp.int32, (tokens, PART), 1) < PART // 2
    return jnp.where(low, table[:, 2 * at : 2 * at + 1], table[:, 2 * at + 1 : 2 * at + 2])


def score_kernel(times, q_ref, *refs):
    count = len(times)
    keys_in = refs[:count]
    e_ref, part_ref, top_s, total_s = refs[count:]
    q_heads = by_head(q_ref[...])
    for at in range(count):
        keys = keys_in[at][...]
        for head in range(2):
            scores = dot_nt(keys, q_heads[head])
            top = jnp.max(scores, axis=0, keepdims=True)
            grown = jnp.exp(scores - top)
            e_ref[2 * at + head] = grown.astype(BF)
            top_s[2 * at + head : 2 * at + head + 1, :] = top
            total_s[2 * at + head : 2 * at + head + 1, :] = jnp.sum(grown, axis=0, keepdims=True)
    for head in range(2):
        tops = [top_s[2 * at + head : 2 * at + head + 1, :] for at in range(count)]
        most = functools.reduce(jnp.maximum, tops)
        lifts = [jnp.exp(top - most) for top in tops]
        total = functools.reduce(
            jnp.add,
            [
                times[at] * lifts[at] * total_s[2 * at + head : 2 * at + head + 1, :]
                for at in range(count)
            ],
        )
        for at in range(count):
            part_ref[2 * at + head : 2 * at + head + 1, :] = lifts[at] / total
    if part_ref.shape[0] > 2 * count:
        part_ref[2 * count :, :] = jnp.zeros((part_ref.shape[0] - 2 * count, q_ref.shape[0]), F32)


def gradient_kernel(times, q_ref, do_ref, delta_ref, e_ref, part_ref, *refs):
    count = len(times)
    keys_in, values_in = refs[:count], refs[count : 2 * count]
    dq_ref = refs[2 * count]
    outs = refs[2 * count + 1 : 3 * count + 1]
    dq_s = refs[3 * count + 1]
    tokens = q_ref.shape[0]
    head_dim = PART // 2
    turned = part_ref[...].T
    grad = do_ref[...]
    g_heads = by_head(grad)
    grad = grad.astype(F32)
    query = q_ref[...].astype(F32)
    delta = delta_ref[...]
    for at in range(count):
        keys_t = keys_in[at][...].astype(F32).T.astype(BF)
        values = values_in[at][...]
        scale = row_scale(turned, at, tokens)
        q_scaled = by_head((query * scale).astype(BF))
        g_scaled = by_head((grad * scale).astype(BF))
        dks, dvs = [], []
        for head in range(2):
            grown = e_ref[2 * at + head]
            dprob = dot_nt(values, g_heads[head])
            dscore = (grown.astype(F32) * (dprob - delta[head : head + 1, :])).astype(BF)
            dvs.append(dot_nn(grown, g_scaled[head]))
            dks.append(dot_nn(dscore, q_scaled[head]))
            spot = slice(head * head_dim, (head + 1) * head_dim)
            part = part_ref[2 * at + head : 2 * at + head + 1, :] * times[at]
            added = dot_nn(keys_t[spot, :], dscore) * part
            dq_s[spot, :] = added if at == 0 else dq_s[spot, :] + added
        outs[at][:, 0:PART] = (dks[0] + dks[1]).astype(BF)
        outs[at][:, PART:] = (dvs[0] + dvs[1]).astype(BF)
    dq_ref[...] = (dq_s[...].T * (1.0 / math.sqrt(head_dim))).astype(BF)


def collect_kernel(times, dq_ref, *refs):
    total = times[0] * refs[0][...].astype(F32)
    for time, ref in zip(times[1:], refs[1:-1]):
        total = total + time * ref[...].astype(F32)
    refs[-1][:, 0:PART] = dq_ref[...]
    refs[-1][:, PART:] = total.astype(BF)


def place_grads(grads, own, core, count):
    z_bit = lax.axis_index("gz") % 2
    for at in range(count):
        source = slice(at * PART, (at + 1) * PART)
        grads[:, columns(at * 2 * PART + z_bit * PART)] = own[:, source]
        core_at = columns(at * 2 * PART + (1 - z_bit) * PART)
        for low in range(4):
            grads[low * PART : (low + 1) * PART, core_at] = core[
                (low ^ 1) * PART : ((low ^ 1) + 1) * PART, source
            ]


def weight_kernel(chunks, own, core, feat_t, o_ref, pair_ref, mine_ref, *refs):
    outs, (grads, made) = refs[:chunks], refs[chunks:]
    place_grads(grads, own, core, 3)
    mine_ref[...] = grads[0:PART, :]
    pair_ref[...] = grads[2 * PART : 3 * PART, :]
    wide = grads.shape[1]
    made[:, 0:wide] = dot_nn(feat_t[...], grads[...]).astype(BF)
    made[:, wide:] = o_ref[...]
    rows = made.shape[0] // chunks
    for at in range(chunks):
        spot = pl.ds(0, rows)
        if chunks > 1:
            spot = pl.ds(pl.multiple_of((lax.axis_index("gx") ^ at) * rows, rows), rows)
        outs[at][...] = made[spot, :]


def grad_x_kernel(own_half, mine, pair, wq0, wq1, wk0, wk1, wv0, wv1, out, full):
    y_bit = lax.axis_index("gy") % 2
    z_bit = lax.axis_index("gz") % 2
    half = z_bit if own_half else z_bit * 0
    width = wq0.shape[1]
    half_rows = wq0.shape[0]
    for at in range(3):
        for side in range(2):
            spot = slice((at * 2 + side) * PART, (at * 2 + side + 1) * PART)
            base = at * width + side * 2 * PART
            full[:, columns(base + y_bit * PART)] = mine[:, spot]
            full[:, columns(base + (1 - y_bit) * PART)] = pair[:, spot]
    for at, sources in ((half, (wq0, wk0, wv0)), (1 - half, (wq1, wk1, wv1))):
        total = functools.reduce(
            jnp.add,
            [dot_nt(full[:, n * width : (n + 1) * width], sources[n][...]) for n in range(3)],
        )
        out[:, pl.ds(pl.multiple_of(at * half_rows, PART), half_rows)] = total.astype(BF)


def sum_kernel(*refs):
    total = refs[0][...].astype(F32)
    for ref in refs[1:-1]:
        total = total + ref[...].astype(F32)
    refs[-1][...] = total.astype(BF)


def spread_kernel(*refs):
    pieces, outs = refs[:8], refs[8:]
    half = 2 * PART
    rows = pieces[0].shape[0]
    for at, piece in enumerate(pieces):
        place = lax.axis_index("gx") ^ (at // 2)
        bit = (lax.axis_index("gy") % 2) ^ (at % 2)
        spot = pl.ds(pl.multiple_of(place * rows, rows), rows)
        for base, out in enumerate(outs[:3]):
            for side in range(2):
                source = slice((base * 2 + side) * PART, (base * 2 + side + 1) * PART)
                out[spot, columns(side * half + bit * PART)] = piece[:, source].astype(F32)
        spot = pl.ds(pl.multiple_of(bit * PART + place * (rows // 2), rows // 2), rows // 2)
        outs[3][spot, 0:half] = piece[0 : rows // 2, 3 * half :].astype(F32)
        outs[3][spot, half:] = piece[rows // 2 :, 3 * half :].astype(F32)


def on_device(features, grad_y, attn_out, w_query, w_key, w_value, w_out):
    width = features.shape[-1]
    half = width // 2
    tokens = features.shape[0] * features.shape[1] * features.shape[2]
    block_tokens = 4 * tokens
    count_x, count_y, count_z = lax.axis_size("gx"), lax.axis_size("gy"), lax.axis_size("gz")
    z_bit = lax.axis_index("gz") % 2
    y_bit = lax.axis_index("gy") % 2

    own_half = count_z == 2
    if own_half:
        pairs = []
        for weight in (w_query, w_key, w_value):
            pairs += [weight, from_partner(weight, "gz")]
        out_rows = w_out
    else:
        pairs = []
        for weight in (w_query, w_key, w_value):
            whole = lax.all_gather(weight, "gz", axis=0, tiled=True)
            pairs += [whole[:half], whole[half:]]
        whole = lax.all_gather(w_out, "gz", axis=0, tiled=True)
        out_rows = lax.dynamic_slice_in_dim(whole, z_bit * half, half, 0)

    message = shape_of((tokens, width + 2 * PART))
    feat = features.reshape(tokens, width)
    feat_pair = from_partner(feat, "gy")
    feat_core = from_partner(feat, "gz")
    w_cols = call(
        functools.partial(columns_kernel, own_half),
        shape_of((width, 3 * PART)),
        pairs,
        scratch=[pltpu.SemaphoreType.DMA((6,))],
        spaces=[pltpu.HBM if own_half else None, None] * 3,
    )
    pair_message, own = call(
        pack_kernel,
        (message, message),
        [value.reshape(tokens, width) for value in (grad_y, attn_out)],
    )
    feat_pair, feat_core, w_cols, own = lax.optimization_barrier(
        (feat_pair, feat_core, w_cols, own)
    )
    pair = from_partner(pair_message, "gy")
    feat_far = from_partner(feat_pair, "gz")
    feats = [feat, feat_core, feat_pair, feat_far]
    column = shape_of((block_tokens, PART))
    query, own_keys, own_values = call(
        project_kernel,
        (column, column, column),
        [*feats, w_cols],
        flops=2 * block_tokens * width * 3 * PART,
    )
    pair, query = lax.optimization_barrier((pair, query))
    core = from_partner(own, "gz")
    far = from_partner(pair, "gz")

    times = [1.0]
    routes = []
    for axis, step, blocks in (("gx", 1, count_x), ("gy", 2, count_y // 2), ("gz", 2, count_z // 2)):
        if blocks == 1:
            times[0] += 2.0
        elif blocks == 2:
            routes.append((axis, step))
            times.append(2.0)
        else:
            routes += [(axis, step), (axis, -step)]
            times += [1.0, 1.0]
    times = tuple(times)
    count = len(times)
    keys = [own_keys] + [shifted(own_keys, axis, step) for axis, step in routes]
    out_grad, delta, feat_t, out_term = call(
        early_kernel,
        (
            column,
            shape_of((2, block_tokens), F32),
            shape_of((half, block_tokens)),
            shape_of((half, half)),
        ),
        [*feats, own, core, pair, far, out_rows],
        scratch=[pltpu.VMEM((block_tokens, PART), BF), pltpu.VMEM((block_tokens, width), BF)],
        flops=4 * block_tokens * width * PART,
    )
    values = [own_values] + [shifted(own_values, axis, step) for axis, step in routes]
    rows = -(-2 * count // 8) * 8
    pixels = 2 * count * block_tokens * block_tokens
    grown, parts = call(
        functools.partial(score_kernel, times),
        (
            shape_of((2 * count, block_tokens, block_tokens)),
            shape_of((rows, block_tokens), F32),
        ),
        [query, *keys],
        scratch=[pltpu.VMEM((rows, block_tokens), F32), pltpu.VMEM((rows, block_tokens), F32)],
        flops=2 * pixels * PART,
        moved=2 * pixels,
        exps=pixels,
    )
    dq, *partials = call(
        functools.partial(gradient_kernel, times),
        (column, *[shape_of((block_tokens, 2 * PART))] * count),
        [query, out_grad, delta, grown, parts, *keys, *values],
        scratch=[pltpu.VMEM((PART, block_tokens), F32)],
        flops=8 * pixels * PART,
        moved=2 * pixels,
    )
    back = [partials[0]]
    for partial, (axis, step) in zip(partials[1:], routes):
        back.append(shifted(partial, axis, -step))
    grads = call(
        functools.partial(collect_kernel, times), shape_of((block_tokens, 3 * PART)), [dq, *back]
    )
    core_grads = from_partner(grads, "gz")
    planned = count_x == 4 and count_y == 4 and count_z == 2
    chunks = 4 if planned else 1
    piece = shape_of((half // chunks, 8 * PART))
    pair_out, mine, *pieces = call(
        functools.partial(weight_kernel, chunks),
        (shape_of((tokens, 6 * PART)), shape_of((tokens, 6 * PART)), *[piece] * chunks),
        [grads, core_grads, feat_t, out_term],
        scratch=[pltpu.VMEM((block_tokens, 6 * PART), BF), pltpu.VMEM((half, 8 * PART), BF)],
        flops=2 * block_tokens * half * 6 * PART,
    )
    def features_grad(pair_rows):
        return call(
            functools.partial(grad_x_kernel, own_half),
            shape_of((tokens, width)),
            [mine, pair_rows, *pairs],
            scratch=[pltpu.VMEM((tokens, 3 * width), BF)],
            flops=2 * tokens * 3 * width * width,
        ).reshape(features.shape)

    if planned:
        terms = [pieces[0]] + [plane_swap(pieces[at], at, 0) for at in (1, 2, 3)]
        total = call(sum_kernel, piece, terms)
        total, pair_out = lax.optimization_barrier((total, pair_out))
        other = plane_swap(total, 0, 2)
        pair_in = from_partner(pair_out, "gy")
        other, pair_in = lax.optimization_barrier((other, pair_in))
        total = call(sum_kernel, piece, [total, other])
        grad_x = features_grad(pair_in)
        by_x, by_y, by_z = plane_swap(total, 1, 0), plane_swap(total, 2, 0), plane_swap(total, 0, 1)
        by_xy, by_xz = plane_swap(by_y, 1, 0), plane_swap(by_x, 0, 1)
        by_yz, by_xyz = plane_swap(by_z, 2, 0), plane_swap(by_z, 3, 0)
        weights = call(
            spread_kernel,
            tuple([shape_of((half, width), F32)] * 4),
            [total, by_z, by_x, by_xz, by_y, by_yz, by_xy, by_xyz],
        )
    else:
        grad_x = features_grad(from_partner(pair_out, "gy"))
        terms = pieces[0].astype(F32)
        stacked = jnp.zeros((4, width, width), F32)
        for base, at in ((0, 0), (1, 1), (2, 2)):
            for side in range(2):
                tile = terms[:, (base * 2 + side) * PART : (base * 2 + side + 1) * PART]
                stacked = lax.dynamic_update_slice(
                    stacked, tile[None], (at, z_bit * half, side * half + y_bit * PART)
                )
        tile = terms[:, 6 * PART :].reshape(4, 2, 32, half)
        tile = tile.transpose(0, 2, 1, 3).reshape(PART, width)
        stacked = lax.dynamic_update_slice(
            stacked, tile[None], (3, z_bit * half + y_bit * PART, 0)
        )
        stacked = lax.psum(stacked, ("gx", "gy", "gz"))
        held_rows = w_query.shape[0]
        stacked = lax.dynamic_slice_in_dim(stacked, lax.axis_index("gz") * held_rows, held_rows, 1)
        weights = [stacked[at] for at in range(4)]
    return (grad_x, *weights)


def solution(mesh):
    return jax.shard_map(
        on_device,
        mesh=mesh,
        in_specs=(
            P("gx", "gy", "gz", None),
            P("gx", "gy", "gz", None),
            P("gx", "gy", "gz", None),
            P("gz", None),
            P("gz", None),
            P("gz", None),
            P("gz", None),
        ),
        out_specs=(
            P("gx", "gy", "gz", None),
            P("gz", None),
            P("gz", None),
            P("gz", None),
            P("gz", None),
        ),
        check_vma=False,
    )
```

```python
import functools
import math

import jax
import jax.numpy as jnp
from jax import lax
from jax.experimental import pallas as pl
from jax.experimental.pallas import tpu as pltpu
from jax.sharding import PartitionSpec as P

HEADS = 8
PART = 128
BF = jnp.bfloat16
F32 = jnp.float32
VMEM_BYTES = 32 * 1024 * 1024


def from_partner(block, axis):
    route = [(index, index ^ 1) for index in range(lax.axis_size(axis))]
    return lax.ppermute(block, axis, route)


def shifted(value, axis, steps):
    count = lax.axis_size(axis)
    return lax.ppermute(value, axis, [(source, (source + steps) % count) for source in range(count)])


def plane_swap(value, flip_x, flip_y):
    count_x, count_y = lax.axis_size("gx"), lax.axis_size("gy")
    route = []
    for at_x in range(count_x):
        for at_y in range(count_y):
            route.append((at_x * count_y + at_y, (at_x ^ flip_x) * count_y + (at_y ^ flip_y)))
    return lax.ppermute(value, ("gx", "gy"), route)


def dot_nn(left, right):
    return lax.dot_general(left, right, (((1,), (0,)), ((), ())), preferred_element_type=F32)


def dot_nt(left, right):
    return lax.dot_general(left, right, (((1,), (1,)), ((), ())), preferred_element_type=F32)


def dot_tn(left, right):
    return lax.dot_general(left, right, (((0,), (0,)), ((), ())), preferred_element_type=F32)


def columns(start):
    return pl.ds(pl.multiple_of(start, PART), PART)


def call(kernel, out_shape, args, scratch=(), flops=1e6, moved=1e6, exps=0, spaces=None):
    specs = [pl.BlockSpec(memory_space=space or pltpu.VMEM) for space in spaces or [None] * len(args)]
    return pl.pallas_call(
        kernel,
        out_shape=out_shape,
        in_specs=specs,
        scratch_shapes=list(scratch),
        compiler_params=pltpu.CompilerParams(vmem_limit_bytes=VMEM_BYTES),
        cost_estimate=pl.CostEstimate(
            flops=int(flops), bytes_accessed=int(moved), transcendentals=int(exps)
        ),
    )(*args)


def shape_of(dims, dtype=BF):
    return jax.ShapeDtypeStruct(dims, dtype)


def pack_kernel(dy_ref, saved_ref, pair_ref, own_ref, saved_s):
    y_bit = lax.axis_index("gy") % 2
    z_bit = lax.axis_index("gz") % 2
    tokens = pair_ref.shape[0]
    width = dy_ref.shape[-1]
    last = PART + width
    dys = dy_ref[...].reshape(tokens, width)
    saved_s[...] = saved_ref[...].reshape(tokens, width)
    for out in (pair_ref, own_ref):
        out[:, PART:last] = dys
    pair_ref[:, 0:PART] = saved_s[:, columns((z_bit * 2 + 1 - y_bit) * PART)]
    pair_ref[:, last:] = saved_s[:, columns(((1 - z_bit) * 2 + 1 - y_bit) * PART)]
    own_ref[:, 0:PART] = saved_s[:, columns(((1 - z_bit) * 2 + y_bit) * PART)]
    own_ref[:, last:] = saved_s[:, columns((z_bit * 2 + y_bit) * PART)]


def columns_kernel(own_half, wq0, wq1, wk0, wk1, wv0, wv1, w_cols):
    y_bit = lax.axis_index("gy") % 2
    z_bit = lax.axis_index("gz") % 2
    half = z_bit if own_half else z_bit * 0
    group = columns((z_bit * 2 + y_bit) * PART)
    half_rows = wq0.shape[0]
    for at, (first, second) in enumerate(((wq0, wq1), (wk0, wk1), (wv0, wv1))):
        spot = slice(at * PART, (at + 1) * PART)
        w_cols[pl.ds(pl.multiple_of(half * half_rows, half_rows), half_rows), spot] = first[:, group]
        w_cols[pl.ds(pl.multiple_of((1 - half) * half_rows, half_rows), half_rows), spot] = second[:, group]


def project_kernel(own, core, pair, far, w_cols, q_ref, k_ref, v_ref):
    width = own.shape[1]
    for at, source in enumerate((own, core, pair, far)):
        rows = slice(at * PART, (at + 1) * PART)
        made = dot_nn(source[...], w_cols[...])
        q_ref[rows, :] = made[:, 0:PART].astype(BF) * jnp.asarray(1.0 / math.sqrt(width // HEADS), BF)
        k_ref[rows, :] = made[:, PART : 2 * PART].astype(BF)
        v_ref[rows, :] = made[:, 2 * PART :].astype(BF)


def early_kernel(
    f_own, f_core, f_pair, f_far, own, core, pair, far, wout,
    do_ref, delta_ref, feat_t_ref, o_ref, saved, dys,
):
    y_bit = lax.axis_index("gy") % 2
    z_bit = lax.axis_index("gz") % 2
    width = f_own.shape[1]
    half = width // 2
    last = PART + width
    for at, (source, spot) in enumerate(((own, last), (core, 0), (pair, 0), (far, last))):
        rows = slice(at * PART, (at + 1) * PART)
        saved[rows, :] = source[:, spot : spot + PART]
        dys[rows, :] = source[:, PART:last]
    for at, source in enumerate((f_own, f_core, f_pair, f_far)):
        wanted = source[:, pl.ds(pl.multiple_of(z_bit * half, PART), half)]
        feat_t_ref[:, at * PART : (at + 1) * PART] = wanted.astype(F32).T.astype(BF)
    w_rows = wout[pl.ds(pl.multiple_of(y_bit * PART, PART), PART), :]
    out_grad = dot_nt(dys[...], w_rows).astype(BF)
    do_ref[...] = out_grad
    head_dim = width // HEADS
    products = (out_grad.astype(F32) * saved[...].astype(F32)).T
    delta_ref[0:1, :] = jnp.sum(products[0:head_dim], axis=0, keepdims=True)
    delta_ref[1:2, :] = jnp.sum(products[head_dim:PART], axis=0, keepdims=True)
    out = dot_nn(saved[...].astype(F32).T.astype(BF), dys[...]).astype(BF)
    for at in range(4):
        low = out[at * 32 : (at + 1) * 32, :]
        o_ref[at * 64 : at * 64 + 32, :] = low[:, 0:half]
        o_ref[at * 64 + 32 : at * 64 + 64, :] = low[:, half:]


def by_head(value):
    low = lax.broadcasted_iota(jnp.int32, value.shape, 1) < PART // 2
    none = jnp.zeros_like(value)
    return (jnp.where(low, value, none), jnp.where(low, none, value))


def row_scale(table, at, tokens):
    low = lax.broadcasted_iota(jnp.int32, (tokens, PART), 1) < PART // 2
    return jnp.where(low, table[:, 2 * at : 2 * at + 1], table[:, 2 * at + 1 : 2 * at + 2])


def score_kernel(times, q_ref, *refs):
    count = len(times)
    keys_in = refs[:count]
    e_ref, part_ref, top_s, total_s = refs[count:]
    q_heads = by_head(q_ref[...])
    for at in range(count):
        keys = keys_in[at][...]
        for head in range(2):
            scores = dot_nt(keys, q_heads[head])
            top = jnp.max(scores, axis=0, keepdims=True)
            grown = jnp.exp(scores - top)
            e_ref[2 * at + head] = grown.astype(BF)
            top_s[2 * at + head : 2 * at + head + 1, :] = top
            total_s[2 * at + head : 2 * at + head + 1, :] = jnp.sum(grown, axis=0, keepdims=True)
    for head in range(2):
        tops = [top_s[2 * at + head : 2 * at + head + 1, :] for at in range(count)]
        most = functools.reduce(jnp.maximum, tops)
        lifts = [jnp.exp(top - most) for top in tops]
        total = functools.reduce(
            jnp.add,
            [
                times[at] * lifts[at] * total_s[2 * at + head : 2 * at + head + 1, :]
                for at in range(count)
            ],
        )
        for at in range(count):
            part_ref[2 * at + head : 2 * at + head + 1, :] = lifts[at] / total
    if part_ref.shape[0] > 2 * count:
        part_ref[2 * count :, :] = jnp.zeros((part_ref.shape[0] - 2 * count, q_ref.shape[0]), F32)


def gradient_kernel(times, q_ref, do_ref, delta_ref, e_ref, part_ref, *refs):
    count = len(times)
    keys_in, values_in = refs[:count], refs[count : 2 * count]
    dq_ref = refs[2 * count]
    outs = refs[2 * count + 1 : 3 * count + 1]
    dq_s = refs[3 * count + 1]
    tokens = q_ref.shape[0]
    head_dim = PART // 2
    turned = part_ref[...].T
    grad = do_ref[...]
    g_heads = by_head(grad)
    grad = grad.astype(F32)
    query = q_ref[...].astype(F32)
    delta = delta_ref[...]
    for at in range(count):
        keys_t = keys_in[at][...].astype(F32).T.astype(BF)
        values = values_in[at][...]
        scale = row_scale(turned, at, tokens)
        q_scaled = by_head((query * scale).astype(BF))
        g_scaled = by_head((grad * scale).astype(BF))
        dks, dvs = [], []
        for head in range(2):
            grown = e_ref[2 * at + head]
            dprob = dot_nt(values, g_heads[head])
            dscore = (grown.astype(F32) * (dprob - delta[head : head + 1, :])).astype(BF)
            dvs.append(dot_nn(grown, g_scaled[head]))
            dks.append(dot_nn(dscore, q_scaled[head]))
            spot = slice(head * head_dim, (head + 1) * head_dim)
            part = part_ref[2 * at + head : 2 * at + head + 1, :] * times[at]
            added = dot_nn(keys_t[spot, :], dscore) * part
            dq_s[spot, :] = added if at == 0 else dq_s[spot, :] + added
        outs[at][:, 0:PART] = (dks[0] + dks[1]).astype(BF)
        outs[at][:, PART:] = (dvs[0] + dvs[1]).astype(BF)
    dq_ref[...] = (dq_s[...].T * (1.0 / math.sqrt(head_dim))).astype(BF)


def collect_kernel(times, dq_ref, *refs):
    total = times[0] * refs[0][...].astype(F32)
    for time, ref in zip(times[1:], refs[1:-1]):
        total = total + time * ref[...].astype(F32)
    refs[-1][:, 0:PART] = dq_ref[...]
    refs[-1][:, PART:] = total.astype(BF)


def place_grads(grads, own, core, count):
    z_bit = lax.axis_index("gz") % 2
    for at in range(count):
        source = slice(at * PART, (at + 1) * PART)
        grads[:, columns(at * 2 * PART + z_bit * PART)] = own[:, source]
        core_at = columns(at * 2 * PART + (1 - z_bit) * PART)
        for low in range(4):
            grads[low * PART : (low + 1) * PART, core_at] = core[
                (low ^ 1) * PART : ((low ^ 1) + 1) * PART, source
            ]


def weight_kernel(chunks, own, core, feat_t, o_ref, pair_ref, mine_ref, *refs):
    outs, (grads, made) = refs[:chunks], refs[chunks:]
    place_grads(grads, own, core, 3)
    mine_ref[...] = grads[0:PART, :]
    pair_ref[...] = grads[2 * PART : 3 * PART, :]
    wide = grads.shape[1]
    made[:, 0:wide] = dot_nn(feat_t[...], grads[...]).astype(BF)
    made[:, wide:] = o_ref[...]
    rows = made.shape[0] // chunks
    for at in range(chunks):
        spot = pl.ds(0, rows)
        if chunks > 1:
            spot = pl.ds(pl.multiple_of((lax.axis_index("gx") ^ at) * rows, rows), rows)
        outs[at][...] = made[spot, :]


def grad_x_kernel(own_half, mine, pair, wq0, wq1, wk0, wk1, wv0, wv1, out, full, made):
    y_bit = lax.axis_index("gy") % 2
    z_bit = lax.axis_index("gz") % 2
    half = z_bit if own_half else z_bit * 0
    width = wq0.shape[1]
    half_rows = wq0.shape[0]
    for at in range(3):
        for side in range(2):
            spot = slice((at * 2 + side) * PART, (at * 2 + side + 1) * PART)
            base = at * width + side * 2 * PART
            full[:, columns(base + y_bit * PART)] = mine[:, spot]
            full[:, columns(base + (1 - y_bit) * PART)] = pair[:, spot]
    for at, sources in ((half, (wq0, wk0, wv0)), (1 - half, (wq1, wk1, wv1))):
        total = functools.reduce(
            jnp.add,
            [dot_nt(full[:, n * width : (n + 1) * width], sources[n][...]) for n in range(3)],
        )
        made[:, pl.ds(pl.multiple_of(at * half_rows, PART), half_rows)] = total.astype(BF)
    out[...] = made[...].reshape(out.shape)


def sum_kernel(*refs):
    total = refs[0][...].astype(F32)
    for ref in refs[1:-1]:
        total = total + ref[...].astype(F32)
    refs[-1][...] = total.astype(BF)


def spread_kernel(*refs):
    pieces, outs = refs[:8], refs[8:]
    half = 2 * PART
    rows = pieces[0].shape[0]
    for at, piece in enumerate(pieces):
        place = lax.axis_index("gx") ^ (at // 2)
        bit = (lax.axis_index("gy") % 2) ^ (at % 2)
        spot = pl.ds(pl.multiple_of(place * rows, rows), rows)
        for base, out in enumerate(outs[:3]):
            for side in range(2):
                source = slice((base * 2 + side) * PART, (base * 2 + side + 1) * PART)
                out[spot, columns(side * half + bit * PART)] = piece[:, source].astype(F32)
        spot = pl.ds(pl.multiple_of(bit * PART + place * (rows // 2), rows // 2), rows // 2)
        outs[3][spot, 0:half] = piece[0 : rows // 2, 3 * half :].astype(F32)
        outs[3][spot, half:] = piece[rows // 2 :, 3 * half :].astype(F32)


def on_device(features, grad_y, attn_out, w_query, w_key, w_value, w_out):
    width = features.shape[-1]
    half = width // 2
    tokens = features.shape[0] * features.shape[1] * features.shape[2]
    block_tokens = 4 * tokens
    count_x, count_y, count_z = lax.axis_size("gx"), lax.axis_size("gy"), lax.axis_size("gz")
    z_bit = lax.axis_index("gz") % 2
    y_bit = lax.axis_index("gy") % 2

    own_half = count_z == 2
    if own_half:
        pairs = []
        for weight in (w_query, w_key, w_value):
            pairs += [weight, from_partner(weight, "gz")]
        out_rows = w_out
    else:
        pairs = []
        for weight in (w_query, w_key, w_value):
            whole = lax.all_gather(weight, "gz", axis=0, tiled=True)
            pairs += [whole[:half], whole[half:]]
        whole = lax.all_gather(w_out, "gz", axis=0, tiled=True)
        out_rows = lax.dynamic_slice_in_dim(whole, z_bit * half, half, 0)

    message = shape_of((tokens, width + 2 * PART))
    feat = features.reshape(tokens, width)
    feat_pair = from_partner(feat, "gy")
    feat_core = from_partner(feat, "gz")
    w_cols = call(
        functools.partial(columns_kernel, own_half),
        shape_of((width, 3 * PART)),
        pairs,
    )
    pair_message, own = call(
        pack_kernel,
        (message, message),
        [grad_y, attn_out],
        scratch=[pltpu.VMEM((tokens, width), BF)],
    )
    feat_pair, feat_core, w_cols, own = lax.optimization_barrier(
        (feat_pair, feat_core, w_cols, own)
    )
    pair = from_partner(pair_message, "gy")
    feat_far = from_partner(feat_pair, "gz")
    feats = [feat, feat_core, feat_pair, feat_far]
    column = shape_of((block_tokens, PART))
    query, own_keys, own_values = call(
        project_kernel,
        (column, column, column),
        [*feats, w_cols],
        flops=2 * block_tokens * width * 3 * PART,
    )
    pair, query = lax.optimization_barrier((pair, query))
    core = from_partner(own, "gz")
    far = from_partner(pair, "gz")

    times = [1.0]
    routes = []
    for axis, step, blocks in (("gx", 1, count_x), ("gy", 2, count_y // 2), ("gz", 2, count_z // 2)):
        if blocks == 1:
            times[0] += 2.0
        elif blocks == 2:
            routes.append((axis, step))
            times.append(2.0)
        else:
            routes += [(axis, step), (axis, -step)]
            times += [1.0, 1.0]
    times = tuple(times)
    count = len(times)
    keys = [own_keys] + [shifted(own_keys, axis, step) for axis, step in routes]
    out_grad, delta, feat_t, out_term = call(
        early_kernel,
        (
            column,
            shape_of((2, block_tokens), F32),
            shape_of((half, block_tokens)),
            shape_of((half, half)),
        ),
        [*feats, own, core, pair, far, out_rows],
        scratch=[pltpu.VMEM((block_tokens, PART), BF), pltpu.VMEM((block_tokens, width), BF)],
        flops=4 * block_tokens * width * PART,
    )
    own_values, out_grad = lax.optimization_barrier((own_values, out_grad))
    values = [own_values] + [shifted(own_values, axis, step) for axis, step in routes]
    rows = -(-2 * count // 8) * 8
    pixels = 2 * count * block_tokens * block_tokens
    grown, parts = call(
        functools.partial(score_kernel, times),
        (
            shape_of((2 * count, block_tokens, block_tokens)),
            shape_of((rows, block_tokens), F32),
        ),
        [query, *keys],
        scratch=[pltpu.VMEM((rows, block_tokens), F32), pltpu.VMEM((rows, block_tokens), F32)],
        flops=2 * pixels * PART,
        moved=2 * pixels,
        exps=pixels,
    )
    dq, *partials = call(
        functools.partial(gradient_kernel, times),
        (column, *[shape_of((block_tokens, 2 * PART))] * count),
        [query, out_grad, delta, grown, parts, *keys, *values],
        scratch=[pltpu.VMEM((PART, block_tokens), F32)],
        flops=8 * pixels * PART,
        moved=2 * pixels,
    )
    back = [partials[0]]
    for partial, (axis, step) in zip(partials[1:], routes):
        back.append(shifted(partial, axis, -step))
    grads = call(
        functools.partial(collect_kernel, times), shape_of((block_tokens, 3 * PART)), [dq, *back]
    )
    core_grads = from_partner(grads, "gz")
    planned = count_x == 4 and count_y == 4 and count_z == 2
    chunks = 4 if planned else 1
    piece = shape_of((half // chunks, 8 * PART))
    pair_out, mine, *pieces = call(
        functools.partial(weight_kernel, chunks),
        (shape_of((tokens, 6 * PART)), shape_of((tokens, 6 * PART)), *[piece] * chunks),
        [grads, core_grads, feat_t, out_term],
        scratch=[pltpu.VMEM((block_tokens, 6 * PART), BF), pltpu.VMEM((half, 8 * PART), BF)],
        flops=2 * block_tokens * half * 6 * PART,
    )
    def features_grad(pair_rows):
        return call(
            functools.partial(grad_x_kernel, own_half),
            shape_of(features.shape),
            [mine, pair_rows, *pairs],
            scratch=[pltpu.VMEM((tokens, 3 * width), BF), pltpu.VMEM((tokens, width), BF)],
            flops=2 * tokens * 3 * width * width,
        )

    if planned:
        terms = [pieces[0]] + [plane_swap(pieces[at], at, 0) for at in (1, 2, 3)]
        total = call(sum_kernel, piece, terms)
        pair_in = from_partner(pair_out, "gy")
        total, pair_in = lax.optimization_barrier((total, pair_in))
        other = plane_swap(total, 0, 2)
        grad_x = features_grad(pair_in)
        total, grad_x = lax.optimization_barrier((total, grad_x))
        total = call(sum_kernel, piece, [total, other])
        by_x, by_y, by_z = plane_swap(total, 1, 0), plane_swap(total, 2, 0), plane_swap(total, 0, 1)
        by_xy, by_xz = plane_swap(by_y, 1, 0), plane_swap(by_x, 0, 1)
        by_yz, by_xyz = plane_swap(by_z, 2, 0), plane_swap(by_z, 3, 0)
        weights = call(
            spread_kernel,
            tuple([shape_of((half, width), F32)] * 4),
            [total, by_z, by_x, by_xz, by_y, by_yz, by_xy, by_xyz],
        )
    else:
        grad_x = features_grad(from_partner(pair_out, "gy"))
        terms = pieces[0].astype(F32)
        stacked = jnp.zeros((4, width, width), F32)
        for base, at in ((0, 0), (1, 1), (2, 2)):
            for side in range(2):
                tile = terms[:, (base * 2 + side) * PART : (base * 2 + side + 1) * PART]
                stacked = lax.dynamic_update_slice(
                    stacked, tile[None], (at, z_bit * half, side * half + y_bit * PART)
                )
        tile = terms[:, 6 * PART :].reshape(4, 2, 32, half)
        tile = tile.transpose(0, 2, 1, 3).reshape(PART, width)
        stacked = lax.dynamic_update_slice(
            stacked, tile[None], (3, z_bit * half + y_bit * PART, 0)
        )
        stacked = lax.psum(stacked, ("gx", "gy", "gz"))
        held_rows = w_query.shape[0]
        stacked = lax.dynamic_slice_in_dim(stacked, lax.axis_index("gz") * held_rows, held_rows, 1)
        weights = [stacked[at] for at in range(4)]
    return (grad_x, *weights)


def solution(mesh):
    return jax.shard_map(
        on_device,
        mesh=mesh,
        in_specs=(
            P("gx", "gy", "gz", None),
            P("gx", "gy", "gz", None),
            P("gx", "gy", "gz", None),
            P("gz", None),
            P("gz", None),
            P("gz", None),
            P("gz", None),
        ),
        out_specs=(
            P("gx", "gy", "gz", None),
            P("gz", None),
            P("gz", None),
            P("gz", None),
            P("gz", None),
        ),
        check_vma=False,
    )
```

```python
import functools
import math

import jax
import jax.numpy as jnp
from jax import lax
from jax.experimental import pallas as pl
from jax.experimental.pallas import tpu as pltpu
from jax.sharding import PartitionSpec as P

HEADS = 8
PART = 128
BF = jnp.bfloat16
F32 = jnp.float32
VMEM_BYTES = 32 * 1024 * 1024


def from_partner(block, axis):
    route = [(index, index ^ 1) for index in range(lax.axis_size(axis))]
    return lax.ppermute(block, axis, route)


def shifted(value, axis, steps):
    count = lax.axis_size(axis)
    return lax.ppermute(value, axis, [(source, (source + steps) % count) for source in range(count)])


def plane_swap(value, flip_x, flip_y):
    count_x, count_y = lax.axis_size("gx"), lax.axis_size("gy")
    route = []
    for at_x in range(count_x):
        for at_y in range(count_y):
            route.append((at_x * count_y + at_y, (at_x ^ flip_x) * count_y + (at_y ^ flip_y)))
    return lax.ppermute(value, ("gx", "gy"), route)


def dot_nn(left, right):
    return lax.dot_general(left, right, (((1,), (0,)), ((), ())), preferred_element_type=F32)


def dot_nt(left, right):
    return lax.dot_general(left, right, (((1,), (1,)), ((), ())), preferred_element_type=F32)


def dot_tn(left, right):
    return lax.dot_general(left, right, (((0,), (0,)), ((), ())), preferred_element_type=F32)


def columns(start):
    return pl.ds(pl.multiple_of(start, PART), PART)


def call(kernel, out_shape, args, scratch=(), flops=1e6, moved=1e6, exps=0, spaces=None):
    specs = [pl.BlockSpec(memory_space=space or pltpu.VMEM) for space in spaces or [None] * len(args)]
    return pl.pallas_call(
        kernel,
        out_shape=out_shape,
        in_specs=specs,
        scratch_shapes=list(scratch),
        compiler_params=pltpu.CompilerParams(vmem_limit_bytes=VMEM_BYTES),
        cost_estimate=pl.CostEstimate(
            flops=int(flops), bytes_accessed=int(moved), transcendentals=int(exps)
        ),
    )(*args)


def shape_of(dims, dtype=BF):
    return jax.ShapeDtypeStruct(dims, dtype)


def pack_kernel(dy_ref, saved_ref, pair_ref, own_ref, saved_s):
    y_bit = lax.axis_index("gy") % 2
    z_bit = lax.axis_index("gz") % 2
    tokens = pair_ref.shape[0]
    width = dy_ref.shape[-1]
    last = PART + width
    dys = dy_ref[...].reshape(tokens, width)
    saved_s[...] = saved_ref[...].reshape(tokens, width)
    for out in (pair_ref, own_ref):
        out[:, PART:last] = dys
    pair_ref[:, 0:PART] = saved_s[:, columns((z_bit * 2 + 1 - y_bit) * PART)]
    pair_ref[:, last:] = saved_s[:, columns(((1 - z_bit) * 2 + 1 - y_bit) * PART)]
    own_ref[:, 0:PART] = saved_s[:, columns(((1 - z_bit) * 2 + y_bit) * PART)]
    own_ref[:, last:] = saved_s[:, columns((z_bit * 2 + y_bit) * PART)]


def columns_kernel(own_half, wq0, wq1, wk0, wk1, wv0, wv1, w_cols):
    y_bit = lax.axis_index("gy") % 2
    z_bit = lax.axis_index("gz") % 2
    half = z_bit if own_half else z_bit * 0
    group = columns((z_bit * 2 + y_bit) * PART)
    half_rows = wq0.shape[0]
    for at, (first, second) in enumerate(((wq0, wq1), (wk0, wk1), (wv0, wv1))):
        spot = slice(at * PART, (at + 1) * PART)
        w_cols[pl.ds(pl.multiple_of(half * half_rows, half_rows), half_rows), spot] = first[:, group]
        w_cols[pl.ds(pl.multiple_of((1 - half) * half_rows, half_rows), half_rows), spot] = second[:, group]


def project_kernel(own, core, pair, far, w_cols, q_ref, k_ref, v_ref):
    width = own.shape[1]
    for at, source in enumerate((own, core, pair, far)):
        rows = slice(at * PART, (at + 1) * PART)
        made = dot_nn(source[...], w_cols[...])
        q_ref[rows, :] = made[:, 0:PART].astype(BF) * jnp.asarray(1.0 / math.sqrt(width // HEADS), BF)
        k_ref[rows, :] = made[:, PART : 2 * PART].astype(BF)
        v_ref[rows, :] = made[:, 2 * PART :].astype(BF)


def early_kernel(
    f_own, f_core, f_pair, f_far, own, core, pair, far, wout,
    do_ref, delta_ref, feat_t_ref, o_ref, saved, dys,
):
    y_bit = lax.axis_index("gy") % 2
    z_bit = lax.axis_index("gz") % 2
    width = f_own.shape[1]
    half = width // 2
    last = PART + width
    for at, (source, spot) in enumerate(((own, last), (core, 0), (pair, 0), (far, last))):
        rows = slice(at * PART, (at + 1) * PART)
        saved[rows, :] = source[:, spot : spot + PART]
        dys[rows, :] = source[:, PART:last]
    for at, source in enumerate((f_own, f_core, f_pair, f_far)):
        wanted = source[:, pl.ds(pl.multiple_of(z_bit * half, PART), half)]
        feat_t_ref[:, at * PART : (at + 1) * PART] = wanted.astype(F32).T.astype(BF)
    w_rows = wout[pl.ds(pl.multiple_of(y_bit * PART, PART), PART), :]
    out_grad = dot_nt(dys[...], w_rows).astype(BF)
    do_ref[...] = out_grad
    head_dim = width // HEADS
    products = (out_grad.astype(F32) * saved[...].astype(F32)).T
    delta_ref[0:1, :] = jnp.sum(products[0:head_dim], axis=0, keepdims=True)
    delta_ref[1:2, :] = jnp.sum(products[head_dim:PART], axis=0, keepdims=True)
    y_bit = lax.axis_index("gy") % 2
    out = dot_nn(saved[...].astype(F32).T.astype(BF), dys[...]).astype(BF)
    o_ref[pl.ds(pl.multiple_of(y_bit * PART, PART), PART), :] = out
    o_ref[pl.ds(pl.multiple_of((1 - y_bit) * PART, PART), PART), :] = jnp.zeros_like(out)


def by_head(value):
    low = lax.broadcasted_iota(jnp.int32, value.shape, 1) < PART // 2
    none = jnp.zeros_like(value)
    return (jnp.where(low, value, none), jnp.where(low, none, value))


def row_scale(table, at, tokens):
    low = lax.broadcasted_iota(jnp.int32, (tokens, PART), 1) < PART // 2
    return jnp.where(low, table[:, 2 * at : 2 * at + 1], table[:, 2 * at + 1 : 2 * at + 2])


def score_kernel(times, q_ref, *refs):
    count = len(times)
    keys_in = refs[:count]
    e_ref, part_ref, top_s, total_s = refs[count:]
    q_heads = by_head(q_ref[...])
    for at in range(count):
        keys = keys_in[at][...]
        for head in range(2):
            scores = dot_nt(keys, q_heads[head])
            top = jnp.max(scores, axis=0, keepdims=True)
            grown = jnp.exp(scores - top)
            e_ref[2 * at + head] = grown.astype(BF)
            top_s[2 * at + head : 2 * at + head + 1, :] = top
            total_s[2 * at + head : 2 * at + head + 1, :] = jnp.sum(grown, axis=0, keepdims=True)
    for head in range(2):
        tops = [top_s[2 * at + head : 2 * at + head + 1, :] for at in range(count)]
        most = functools.reduce(jnp.maximum, tops)
        lifts = [jnp.exp(top - most) for top in tops]
        total = functools.reduce(
            jnp.add,
            [
                times[at] * lifts[at] * total_s[2 * at + head : 2 * at + head + 1, :]
                for at in range(count)
            ],
        )
        for at in range(count):
            part_ref[2 * at + head : 2 * at + head + 1, :] = lifts[at] / total
    if part_ref.shape[0] > 2 * count:
        part_ref[2 * count :, :] = jnp.zeros((part_ref.shape[0] - 2 * count, q_ref.shape[0]), F32)


def gradient_kernel(times, q_ref, do_ref, delta_ref, e_ref, part_ref, *refs):
    count = len(times)
    keys_in, values_in = refs[:count], refs[count : 2 * count]
    dq_ref = refs[2 * count]
    outs = refs[2 * count + 1 : 3 * count + 1]
    dq_s = refs[3 * count + 1]
    tokens = q_ref.shape[0]
    head_dim = PART // 2
    turned = part_ref[...].T
    grad = do_ref[...]
    g_heads = by_head(grad)
    grad = grad.astype(F32)
    query = q_ref[...].astype(F32)
    delta = delta_ref[...]
    for at in range(count):
        keys_t = keys_in[at][...].astype(F32).T.astype(BF)
        values = values_in[at][...]
        scale = row_scale(turned, at, tokens)
        q_scaled = by_head((query * scale).astype(BF))
        g_scaled = by_head((grad * scale).astype(BF))
        dks, dvs = [], []
        for head in range(2):
            grown = e_ref[2 * at + head]
            dprob = dot_nt(values, g_heads[head])
            dscore = (grown.astype(F32) * (dprob - delta[head : head + 1, :])).astype(BF)
            dvs.append(dot_nn(grown, g_scaled[head]))
            dks.append(dot_nn(dscore, q_scaled[head]))
            spot = slice(head * head_dim, (head + 1) * head_dim)
            part = part_ref[2 * at + head : 2 * at + head + 1, :] * times[at]
            added = dot_nn(keys_t[spot, :], dscore) * part
            dq_s[spot, :] = added if at == 0 else dq_s[spot, :] + added
        outs[at][:, 0:PART] = (dks[0] + dks[1]).astype(BF)
        outs[at][:, PART:] = (dvs[0] + dvs[1]).astype(BF)
    dq_ref[...] = (dq_s[...].T * (1.0 / math.sqrt(head_dim))).astype(BF)


def collect_kernel(times, dq_ref, *refs):
    total = times[0] * refs[0][...].astype(F32)
    for time, ref in zip(times[1:], refs[1:-1]):
        total = total + time * ref[...].astype(F32)
    refs[-1][:, 0:PART] = dq_ref[...]
    refs[-1][:, PART:] = total.astype(BF)


def place_grads(grads, own, core, count):
    z_bit = lax.axis_index("gz") % 2
    for at in range(count):
        source = slice(at * PART, (at + 1) * PART)
        grads[:, columns(at * 2 * PART + z_bit * PART)] = own[:, source]
        core_at = columns(at * 2 * PART + (1 - z_bit) * PART)
        for low in range(4):
            grads[low * PART : (low + 1) * PART, core_at] = core[
                (low ^ 1) * PART : ((low ^ 1) + 1) * PART, source
            ]


def weight_kernel(chunks, own, core, feat_t, pair_ref, mine_ref, *refs):
    outs, (grads, made) = refs[:chunks], refs[chunks:]
    place_grads(grads, own, core, 3)
    mine_ref[...] = grads[0:PART, :]
    pair_ref[...] = grads[2 * PART : 3 * PART, :]
    made[...] = dot_nn(feat_t[...], grads[...]).astype(BF)
    rows = made.shape[0] // chunks
    for at in range(chunks):
        spot = pl.ds(0, rows)
        if chunks > 1:
            spot = pl.ds(pl.multiple_of((lax.axis_index("gx") ^ at) * rows, rows), rows)
        outs[at][...] = made[spot, :]


def grad_x_kernel(own_half, mine, pair, wq0, wq1, wk0, wk1, wv0, wv1, out, full, made):
    y_bit = lax.axis_index("gy") % 2
    z_bit = lax.axis_index("gz") % 2
    half = z_bit if own_half else z_bit * 0
    width = wq0.shape[1]
    half_rows = wq0.shape[0]
    for at in range(3):
        for side in range(2):
            spot = slice((at * 2 + side) * PART, (at * 2 + side + 1) * PART)
            base = at * width + side * 2 * PART
            full[:, columns(base + y_bit * PART)] = mine[:, spot]
            full[:, columns(base + (1 - y_bit) * PART)] = pair[:, spot]
    for at, sources in ((half, (wq0, wk0, wv0)), (1 - half, (wq1, wk1, wv1))):
        total = functools.reduce(
            jnp.add,
            [dot_nt(full[:, n * width : (n + 1) * width], sources[n][...]) for n in range(3)],
        )
        made[:, pl.ds(pl.multiple_of(at * half_rows, PART), half_rows)] = total.astype(BF)
    out[...] = made[...].reshape(out.shape)


def sum_kernel(*refs):
    total = refs[0][...].astype(F32)
    for ref in refs[1:-1]:
        total = total + ref[...].astype(F32)
    refs[-1][...] = total.astype(BF)


def spread_kernel(*refs):
    pieces, out_sum, outs = refs[:8], refs[8], refs[9:]
    half = 2 * PART
    rows = pieces[0].shape[0]
    for at, piece in enumerate(pieces):
        place = lax.axis_index("gx") ^ (at // 2)
        bit = (lax.axis_index("gy") % 2) ^ (at % 2)
        spot = pl.ds(pl.multiple_of(place * rows, rows), rows)
        for base, out in enumerate(outs[:3]):
            for side in range(2):
                source = slice((base * 2 + side) * PART, (base * 2 + side + 1) * PART)
                out[spot, columns(side * half + bit * PART)] = piece[:, source].astype(F32)
    outs[3][...] = out_sum[...].astype(F32)


def on_device(features, grad_y, attn_out, w_query, w_key, w_value, w_out):
    width = features.shape[-1]
    half = width // 2
    tokens = features.shape[0] * features.shape[1] * features.shape[2]
    block_tokens = 4 * tokens
    count_x, count_y, count_z = lax.axis_size("gx"), lax.axis_size("gy"), lax.axis_size("gz")
    z_bit = lax.axis_index("gz") % 2
    y_bit = lax.axis_index("gy") % 2

    own_half = count_z == 2
    if own_half:
        pairs = []
        for weight in (w_query, w_key, w_value):
            pairs += [weight, from_partner(weight, "gz")]
        out_rows = w_out
    else:
        pairs = []
        for weight in (w_query, w_key, w_value):
            whole = lax.all_gather(weight, "gz", axis=0, tiled=True)
            pairs += [whole[:half], whole[half:]]
        whole = lax.all_gather(w_out, "gz", axis=0, tiled=True)
        out_rows = lax.dynamic_slice_in_dim(whole, z_bit * half, half, 0)

    message = shape_of((tokens, width + 2 * PART))
    feat = features.reshape(tokens, width)
    feat_pair = from_partner(feat, "gy")
    feat_core = from_partner(feat, "gz")
    w_cols = call(
        functools.partial(columns_kernel, own_half),
        shape_of((width, 3 * PART)),
        pairs,
    )
    pair_message, own = call(
        pack_kernel,
        (message, message),
        [grad_y, attn_out],
        scratch=[pltpu.VMEM((tokens, width), BF)],
    )
    feat_pair, feat_core, w_cols, own = lax.optimization_barrier(
        (feat_pair, feat_core, w_cols, own)
    )
    pair = from_partner(pair_message, "gy")
    feat_far = from_partner(feat_pair, "gz")
    feats = [feat, feat_core, feat_pair, feat_far]
    column = shape_of((block_tokens, PART))
    query, own_keys, own_values = call(
        project_kernel,
        (column, column, column),
        [*feats, w_cols],
        flops=2 * block_tokens * width * 3 * PART,
    )
    pair, query = lax.optimization_barrier((pair, query))
    core = from_partner(own, "gz")
    far = from_partner(pair, "gz")

    times = [1.0]
    routes = []
    for axis, step, blocks in (("gx", 1, count_x), ("gy", 2, count_y // 2), ("gz", 2, count_z // 2)):
        if blocks == 1:
            times[0] += 2.0
        elif blocks == 2:
            routes.append((axis, step))
            times.append(2.0)
        else:
            routes += [(axis, step), (axis, -step)]
            times += [1.0, 1.0]
    times = tuple(times)
    count = len(times)
    keys = [own_keys] + [shifted(own_keys, axis, step) for axis, step in routes]
    out_grad, delta, feat_t, out_term = call(
        early_kernel,
        (
            column,
            shape_of((2, block_tokens), F32),
            shape_of((half, block_tokens)),
            shape_of((half, width)),
        ),
        [*feats, own, core, pair, far, out_rows],
        scratch=[pltpu.VMEM((block_tokens, PART), BF), pltpu.VMEM((block_tokens, width), BF)],
        flops=4 * block_tokens * width * PART,
    )
    own_values, out_grad = lax.optimization_barrier((own_values, out_grad))
    values = [own_values] + [shifted(own_values, axis, step) for axis, step in routes]
    rows = -(-2 * count // 8) * 8
    pixels = 2 * count * block_tokens * block_tokens
    grown, parts = call(
        functools.partial(score_kernel, times),
        (
            shape_of((2 * count, block_tokens, block_tokens)),
            shape_of((rows, block_tokens), F32),
        ),
        [query, *keys],
        scratch=[pltpu.VMEM((rows, block_tokens), F32), pltpu.VMEM((rows, block_tokens), F32)],
        flops=2 * pixels * PART,
        moved=2 * pixels,
        exps=pixels,
    )
    dq, *partials = call(
        functools.partial(gradient_kernel, times),
        (column, *[shape_of((block_tokens, 2 * PART))] * count),
        [query, out_grad, delta, grown, parts, *keys, *values],
        scratch=[pltpu.VMEM((PART, block_tokens), F32)],
        flops=8 * pixels * PART,
        moved=2 * pixels,
    )
    planned = count_x == 4 and count_y == 4 and count_z == 2
    plane = ("gx", "gy")
    if planned:
        out_sum = lax.psum_scatter(out_term, plane, scatter_dimension=0, tiled=True)
        partials, out_sum = lax.optimization_barrier((partials, out_sum))
    back = [partials[0]]
    for partial, (axis, step) in zip(partials[1:], routes):
        back.append(shifted(partial, axis, -step))
    grads = call(
        functools.partial(collect_kernel, times), shape_of((block_tokens, 3 * PART)), [dq, *back]
    )
    core_grads = from_partner(grads, "gz")
    chunks = 4 if planned else 1
    piece = shape_of((half // chunks, 6 * PART))
    pair_out, mine, *pieces = call(
        functools.partial(weight_kernel, chunks),
        (shape_of((tokens, 6 * PART)), shape_of((tokens, 6 * PART)), *[piece] * chunks),
        [grads, core_grads, feat_t],
        scratch=[pltpu.VMEM((block_tokens, 6 * PART), BF), pltpu.VMEM((half, 6 * PART), BF)],
        flops=2 * block_tokens * half * 6 * PART,
    )
    def features_grad(pair_rows):
        return call(
            functools.partial(grad_x_kernel, own_half),
            shape_of(features.shape),
            [mine, pair_rows, *pairs],
            scratch=[pltpu.VMEM((tokens, 3 * width), BF), pltpu.VMEM((tokens, width), BF)],
            flops=2 * tokens * 3 * width * width,
        )

    if planned:
        out_sum = lax.all_gather(out_sum, plane, axis=0, tiled=True)
        terms = [pieces[0]] + [plane_swap(pieces[at], at, 0) for at in (1, 2, 3)]
        total = call(sum_kernel, piece, terms)
        pair_in = from_partner(pair_out, "gy")
        total, pair_in, out_sum = lax.optimization_barrier((total, pair_in, out_sum))
        other = plane_swap(total, 0, 2)
        grad_x = features_grad(pair_in)
        total, grad_x = lax.optimization_barrier((total, grad_x))
        total = call(sum_kernel, piece, [total, other])
        by_x, by_y, by_z = plane_swap(total, 1, 0), plane_swap(total, 2, 0), plane_swap(total, 0, 1)
        by_xy, by_xz = plane_swap(by_y, 1, 0), plane_swap(by_x, 0, 1)
        by_yz, by_xyz = plane_swap(by_z, 2, 0), plane_swap(by_z, 3, 0)
        weights = call(
            spread_kernel,
            tuple([shape_of((half, width), F32)] * 4),
            [total, by_z, by_x, by_xz, by_y, by_yz, by_xy, by_xyz, out_sum],
        )
    else:
        grad_x = features_grad(from_partner(pair_out, "gy"))
        terms = pieces[0].astype(F32)
        stacked = jnp.zeros((4, width, width), F32)
        for base, at in ((0, 0), (1, 1), (2, 2)):
            for side in range(2):
                tile = terms[:, (base * 2 + side) * PART : (base * 2 + side + 1) * PART]
                stacked = lax.dynamic_update_slice(
                    stacked, tile[None], (at, z_bit * half, side * half + y_bit * PART)
                )
        stacked = lax.dynamic_update_slice(
            stacked, out_term.astype(F32)[None], (3, z_bit * half, 0)
        )
        stacked = lax.psum(stacked, ("gx", "gy", "gz"))
        held_rows = w_query.shape[0]
        stacked = lax.dynamic_slice_in_dim(stacked, lax.axis_index("gz") * held_rows, held_rows, 1)
        weights = [stacked[at] for at in range(4)]
    return (grad_x, *weights)


def solution(mesh):
    return jax.shard_map(
        on_device,
        mesh=mesh,
        in_specs=(
            P("gx", "gy", "gz", None),
            P("gx", "gy", "gz", None),
            P("gx", "gy", "gz", None),
            P("gz", None),
            P("gz", None),
            P("gz", None),
            P("gz", None),
        ),
        out_specs=(
            P("gx", "gy", "gz", None),
            P("gz", None),
            P("gz", None),
            P("gz", None),
            P("gz", None),
        ),
        check_vma=False,
    )
```

```python
import functools
import math

import jax
import jax.numpy as jnp
from jax import lax
from jax.experimental import pallas as pl
from jax.experimental.pallas import tpu as pltpu
from jax.sharding import PartitionSpec as P

HEADS = 8
PART = 128
BF = jnp.bfloat16
F32 = jnp.float32
VMEM_BYTES = 32 * 1024 * 1024


def from_partner(block, axis):
    route = [(index, index ^ 1) for index in range(lax.axis_size(axis))]
    return lax.ppermute(block, axis, route)


def shifted(value, axis, steps):
    count = lax.axis_size(axis)
    return lax.ppermute(value, axis, [(source, (source + steps) % count) for source in range(count)])


def plane_swap(value, flip_x, flip_y):
    count_x, count_y = lax.axis_size("gx"), lax.axis_size("gy")
    route = []
    for at_x in range(count_x):
        for at_y in range(count_y):
            route.append((at_x * count_y + at_y, (at_x ^ flip_x) * count_y + (at_y ^ flip_y)))
    return lax.ppermute(value, ("gx", "gy"), route)


def dot_nn(left, right):
    return lax.dot_general(left, right, (((1,), (0,)), ((), ())), preferred_element_type=F32)


def dot_nt(left, right):
    return lax.dot_general(left, right, (((1,), (1,)), ((), ())), preferred_element_type=F32)


def dot_tn(left, right):
    return lax.dot_general(left, right, (((0,), (0,)), ((), ())), preferred_element_type=F32)


def columns(start):
    return pl.ds(pl.multiple_of(start, PART), PART)


def call(kernel, out_shape, args, scratch=(), flops=1e6, moved=1e6, exps=0, spaces=None):
    specs = [pl.BlockSpec(memory_space=space or pltpu.VMEM) for space in spaces or [None] * len(args)]
    return pl.pallas_call(
        kernel,
        out_shape=out_shape,
        in_specs=specs,
        scratch_shapes=list(scratch),
        compiler_params=pltpu.CompilerParams(vmem_limit_bytes=VMEM_BYTES),
        cost_estimate=pl.CostEstimate(
            flops=int(flops), bytes_accessed=int(moved), transcendentals=int(exps)
        ),
    )(*args)


def shape_of(dims, dtype=BF):
    return jax.ShapeDtypeStruct(dims, dtype)


def pack_kernel(dy_ref, saved_ref, pair_ref, own_ref, saved_s):
    y_bit = lax.axis_index("gy") % 2
    z_bit = lax.axis_index("gz") % 2
    tokens = pair_ref.shape[0]
    width = dy_ref.shape[-1]
    last = PART + width
    dys = dy_ref[...].reshape(tokens, width)
    saved_s[...] = saved_ref[...].reshape(tokens, width)
    for out in (pair_ref, own_ref):
        out[:, PART:last] = dys
    pair_ref[:, 0:PART] = saved_s[:, columns((z_bit * 2 + 1 - y_bit) * PART)]
    pair_ref[:, last:] = saved_s[:, columns(((1 - z_bit) * 2 + 1 - y_bit) * PART)]
    own_ref[:, 0:PART] = saved_s[:, columns(((1 - z_bit) * 2 + y_bit) * PART)]
    own_ref[:, last:] = saved_s[:, columns((z_bit * 2 + y_bit) * PART)]


def columns_kernel(own_half, wq0, wq1, wk0, wk1, wv0, wv1, w_cols):
    y_bit = lax.axis_index("gy") % 2
    z_bit = lax.axis_index("gz") % 2
    half = z_bit if own_half else z_bit * 0
    group = columns((z_bit * 2 + y_bit) * PART)
    half_rows = wq0.shape[0]
    for at, (first, second) in enumerate(((wq0, wq1), (wk0, wk1), (wv0, wv1))):
        spot = slice(at * PART, (at + 1) * PART)
        w_cols[pl.ds(pl.multiple_of(half * half_rows, half_rows), half_rows), spot] = first[:, group]
        w_cols[pl.ds(pl.multiple_of((1 - half) * half_rows, half_rows), half_rows), spot] = second[:, group]


def project_kernel(own, core, pair, far, w_cols, q_ref, kv_ref):
    width = own.shape[1]
    for at, source in enumerate((own, core, pair, far)):
        rows = slice(at * PART, (at + 1) * PART)
        made = dot_nn(source[...], w_cols[...])
        q_ref[rows, :] = made[:, 0:PART].astype(BF) * jnp.asarray(1.0 / math.sqrt(width // HEADS), BF)
        kv_ref[rows, :] = made[:, PART:].astype(BF)


def early_kernel(
    f_own, f_core, f_pair, f_far, own, core, pair, far, wout,
    do_ref, delta_ref, feat_t_ref, o_ref, saved, dys,
):
    y_bit = lax.axis_index("gy") % 2
    z_bit = lax.axis_index("gz") % 2
    width = f_own.shape[1]
    half = width // 2
    last = PART + width
    for at, (source, spot) in enumerate(((own, last), (core, 0), (pair, 0), (far, last))):
        rows = slice(at * PART, (at + 1) * PART)
        saved[rows, :] = source[:, spot : spot + PART]
        dys[rows, :] = source[:, PART:last]
    for at, source in enumerate((f_own, f_core, f_pair, f_far)):
        wanted = source[:, pl.ds(pl.multiple_of(z_bit * half, PART), half)]
        feat_t_ref[:, at * PART : (at + 1) * PART] = wanted.astype(F32).T.astype(BF)
    w_rows = wout[pl.ds(pl.multiple_of(y_bit * PART, PART), PART), :]
    out_grad = dot_nt(dys[...], w_rows).astype(BF)
    do_ref[...] = out_grad
    head_dim = width // HEADS
    products = (out_grad.astype(F32) * saved[...].astype(F32)).T
    delta_ref[0:1, :] = jnp.sum(products[0:head_dim], axis=0, keepdims=True)
    delta_ref[1:2, :] = jnp.sum(products[head_dim:PART], axis=0, keepdims=True)
    out = dot_nn(saved[...].astype(F32).T.astype(BF), dys[...]).astype(BF)
    for at in range(4):
        low = out[at * 32 : (at + 1) * 32, :]
        o_ref[at * 64 : at * 64 + 32, :] = low[:, 0:half]
        o_ref[at * 64 + 32 : at * 64 + 64, :] = low[:, half:]


def by_head(value):
    low = lax.broadcasted_iota(jnp.int32, value.shape, 1) < PART // 2
    none = jnp.zeros_like(value)
    return (jnp.where(low, value, none), jnp.where(low, none, value))


def row_scale(table, at, tokens):
    low = lax.broadcasted_iota(jnp.int32, (tokens, PART), 1) < PART // 2
    return jnp.where(low, table[:, 2 * at : 2 * at + 1], table[:, 2 * at + 1 : 2 * at + 2])


def score_kernel(q_ref, *refs):
    count = len(refs) - 2
    e_ref, table_ref = refs[count:]
    half = table_ref.shape[0] // 2
    q_heads = by_head(q_ref[...])
    if half > 2 * count:
        table_ref[...] = jnp.zeros_like(table_ref)
    for at in range(count):
        keys = refs[at][:, 0:PART]
        for head in range(2):
            scores = dot_nt(keys, q_heads[head])
            top = jnp.max(scores, axis=0, keepdims=True)
            grown = jnp.exp(scores - top)
            row = 2 * at + head
            e_ref[row] = grown.astype(BF)
            table_ref[row : row + 1, :] = top
            table_ref[half + row : half + row + 1, :] = jnp.sum(grown, axis=0, keepdims=True)


def gradient_kernel(times, groups, q_ref, do_ref, delta_ref, *refs):
    count = len(times)
    e_refs, tables = refs[: 2 * len(groups) : 2], refs[1 : 2 * len(groups) : 2]
    refs = refs[2 * len(groups) :]
    kvs, dq_ref, outs, dq_s, part_s = (
        refs[:count], refs[count], refs[count + 1 : 2 * count + 1], refs[-2], refs[-1]
    )
    where = [(group, at) for group, blocks in enumerate(groups) for at in range(blocks)]
    if part_s.shape[0] > 2 * count:
        part_s[...] = jnp.zeros_like(part_s)
    for head in range(2):
        tops, totals = [], []
        for group, at in where:
            half = tables[group].shape[0] // 2
            row = 2 * at + head
            tops.append(tables[group][row : row + 1, :])
            totals.append(tables[group][half + row : half + row + 1, :])
        most = functools.reduce(jnp.maximum, tops)
        lifts = [jnp.exp(top - most) for top in tops]
        total = functools.reduce(
            jnp.add, [time * lift * part for time, lift, part in zip(times, lifts, totals)]
        )
        for at in range(count):
            part_s[2 * at + head : 2 * at + head + 1, :] = lifts[at] / total
    tokens = q_ref.shape[0]
    head_dim = PART // 2
    turned = part_s[...].T
    grad = do_ref[...]
    g_heads = by_head(grad)
    grad = grad.astype(F32)
    query = q_ref[...].astype(F32)
    delta = delta_ref[...]
    for at in range(count):
        keys_t = kvs[at][:, 0:PART].astype(F32).T.astype(BF)
        values = kvs[at][:, PART:]
        group, place = where[at]
        scale = row_scale(turned, at, tokens)
        q_scaled = by_head((query * scale).astype(BF))
        g_scaled = by_head((grad * scale).astype(BF))
        dks, dvs = [], []
        for head in range(2):
            grown = e_refs[group][2 * place + head]
            dprob = dot_nt(values, g_heads[head])
            dscore = (grown.astype(F32) * (dprob - delta[head : head + 1, :])).astype(BF)
            dvs.append(dot_nn(grown, g_scaled[head]))
            dks.append(dot_nn(dscore, q_scaled[head]))
            spot = slice(head * head_dim, (head + 1) * head_dim)
            part = part_s[2 * at + head : 2 * at + head + 1, :] * times[at]
            added = dot_nn(keys_t[spot, :], dscore) * part
            dq_s[spot, :] = added if at == 0 else dq_s[spot, :] + added
        outs[at][:, 0:PART] = (dks[0] + dks[1]).astype(BF)
        outs[at][:, PART:] = (dvs[0] + dvs[1]).astype(BF)
    dq_ref[...] = (dq_s[...].T * (1.0 / math.sqrt(head_dim))).astype(BF)


def collect_kernel(times, dq_ref, *refs):
    total = times[0] * refs[0][...].astype(F32)
    for time, ref in zip(times[1:], refs[1:-1]):
        total = total + time * ref[...].astype(F32)
    refs[-1][:, 0:PART] = dq_ref[...]
    refs[-1][:, PART:] = total.astype(BF)


def place_grads(grads, own, core, count):
    z_bit = lax.axis_index("gz") % 2
    for at in range(count):
        source = slice(at * PART, (at + 1) * PART)
        grads[:, columns(at * 2 * PART + z_bit * PART)] = own[:, source]
        core_at = columns(at * 2 * PART + (1 - z_bit) * PART)
        for low in range(4):
            grads[low * PART : (low + 1) * PART, core_at] = core[
                (low ^ 1) * PART : ((low ^ 1) + 1) * PART, source
            ]


def weight_kernel(chunks, own, core, feat_t, o_ref, pair_ref, mine_ref, *refs):
    outs, (grads, made) = refs[:chunks], refs[chunks:]
    place_grads(grads, own, core, 3)
    mine_ref[...] = grads[0:PART, :]
    pair_ref[...] = grads[2 * PART : 3 * PART, :]
    wide = grads.shape[1]
    made[:, 0:wide] = dot_nn(feat_t[...], grads[...]).astype(BF)
    made[:, wide:] = o_ref[...]
    rows = made.shape[0] // chunks
    for at in range(chunks):
        spot = pl.ds(0, rows)
        if chunks > 1:
            spot = pl.ds(pl.multiple_of((lax.axis_index("gx") ^ at) * rows, rows), rows)
        outs[at][...] = made[spot, :]


def grad_x_kernel(own_half, mine, pair, wq0, wq1, wk0, wk1, wv0, wv1, out, full, made):
    y_bit = lax.axis_index("gy") % 2
    z_bit = lax.axis_index("gz") % 2
    half = z_bit if own_half else z_bit * 0
    width = wq0.shape[1]
    half_rows = wq0.shape[0]
    for at in range(3):
        for side in range(2):
            spot = slice((at * 2 + side) * PART, (at * 2 + side + 1) * PART)
            base = at * width + side * 2 * PART
            full[:, columns(base + y_bit * PART)] = mine[:, spot]
            full[:, columns(base + (1 - y_bit) * PART)] = pair[:, spot]
    for at, sources in ((half, (wq0, wk0, wv0)), (1 - half, (wq1, wk1, wv1))):
        total = functools.reduce(
            jnp.add,
            [dot_nt(full[:, n * width : (n + 1) * width], sources[n][...]) for n in range(3)],
        )
        made[:, pl.ds(pl.multiple_of(at * half_rows, PART), half_rows)] = total.astype(BF)
    out[...] = made[...].reshape(out.shape)


def sum_kernel(*refs):
    total = refs[0][...].astype(F32)
    for ref in refs[1:-1]:
        total = total + ref[...].astype(F32)
    refs[-1][...] = total.astype(BF)


def spread_kernel(*refs):
    pieces, outs = refs[:8], refs[8:]
    half = 2 * PART
    rows = pieces[0].shape[0]
    for at, piece in enumerate(pieces):
        place = lax.axis_index("gx") ^ (at // 2)
        bit = (lax.axis_index("gy") % 2) ^ (at % 2)
        spot = pl.ds(pl.multiple_of(place * rows, rows), rows)
        for base, out in enumerate(outs[:3]):
            for side in range(2):
                source = slice((base * 2 + side) * PART, (base * 2 + side + 1) * PART)
                out[spot, columns(side * half + bit * PART)] = piece[:, source].astype(F32)
        spot = pl.ds(pl.multiple_of(bit * PART + place * (rows // 2), rows // 2), rows // 2)
        outs[3][spot, 0:half] = piece[0 : rows // 2, 3 * half :].astype(F32)
        outs[3][spot, half:] = piece[rows // 2 :, 3 * half :].astype(F32)


def on_device(features, grad_y, attn_out, w_query, w_key, w_value, w_out):
    width = features.shape[-1]
    half = width // 2
    tokens = features.shape[0] * features.shape[1] * features.shape[2]
    block_tokens = 4 * tokens
    count_x, count_y, count_z = lax.axis_size("gx"), lax.axis_size("gy"), lax.axis_size("gz")
    z_bit = lax.axis_index("gz") % 2
    y_bit = lax.axis_index("gy") % 2

    own_half = count_z == 2
    if own_half:
        pairs = []
        for weight in (w_query, w_key, w_value):
            pairs += [weight, from_partner(weight, "gz")]
        out_rows = w_out
    else:
        pairs = []
        for weight in (w_query, w_key, w_value):
            whole = lax.all_gather(weight, "gz", axis=0, tiled=True)
            pairs += [whole[:half], whole[half:]]
        whole = lax.all_gather(w_out, "gz", axis=0, tiled=True)
        out_rows = lax.dynamic_slice_in_dim(whole, z_bit * half, half, 0)

    message = shape_of((tokens, width + 2 * PART))
    feat = features.reshape(tokens, width)
    feat_pair = from_partner(feat, "gy")
    feat_core = from_partner(feat, "gz")
    w_cols = call(
        functools.partial(columns_kernel, own_half),
        shape_of((width, 3 * PART)),
        pairs,
    )
    feat_pair, feat_core, w_cols = lax.optimization_barrier((feat_pair, feat_core, w_cols))
    feat_far = from_partner(feat_pair, "gz")
    feats = [feat, feat_core, feat_pair, feat_far]
    column = shape_of((block_tokens, PART))
    both = shape_of((block_tokens, 2 * PART))
    query, own_kv = call(
        project_kernel,
        (column, both),
        [*feats, w_cols],
        flops=2 * block_tokens * width * 3 * PART,
    )

    times = [1.0]
    routes = []
    for axis, step, blocks in (("gx", 1, count_x), ("gy", 2, count_y // 2), ("gz", 2, count_z // 2)):
        if blocks == 1:
            times[0] += 2.0
        elif blocks == 2:
            routes.append((axis, step))
            times.append(2.0)
        else:
            routes += [(axis, step), (axis, -step)]
            times += [1.0, 1.0]
    times = tuple(times)
    count = len(times)
    near = [own_kv] + [shifted(own_kv, axis, step) for axis, step in routes]
    late_dy, late_saved, query = lax.optimization_barrier((grad_y, attn_out, query))
    pair_message, own = call(
        pack_kernel,
        (message, message),
        [late_dy, late_saved],
        scratch=[pltpu.VMEM((tokens, width), BF)],
    )
    pair = from_partner(pair_message, "gy")
    core = from_partner(own, "gz")
    far = from_partner(pair, "gz")
    out_grad, delta, feat_t, out_term = call(
        early_kernel,
        (
            column,
            shape_of((2, block_tokens), F32),
            shape_of((half, block_tokens)),
            shape_of((half, half)),
        ),
        [*feats, own, core, pair, far, out_rows],
        scratch=[pltpu.VMEM((block_tokens, PART), BF), pltpu.VMEM((block_tokens, width), BF)],
        flops=4 * block_tokens * width * PART,
    )
    pixels = 2 * block_tokens * block_tokens
    groups = (2, count - 2)
    scored = []
    place = 0
    for blocks in groups:
        rows = -(-2 * blocks // 8) * 8
        scored += call(
            score_kernel,
            (
                shape_of((2 * blocks, block_tokens, block_tokens)),
                shape_of((2 * rows, block_tokens), F32),
            ),
            [query, *near[place : place + blocks]],
            flops=2 * pixels * blocks * PART,
            moved=2 * pixels * blocks,
            exps=pixels * blocks,
        )
        place += blocks
    dq, *partials = call(
        functools.partial(gradient_kernel, times, groups),
        (column, *[both] * count),
        [query, out_grad, delta, *scored, *near],
        scratch=[
            pltpu.VMEM((PART, block_tokens), F32),
            pltpu.VMEM((-(-2 * count // 8) * 8, block_tokens), F32),
        ],
        flops=8 * pixels * count * PART,
        moved=2 * pixels * count,
    )
    back = [partials[0]]
    for partial, (axis, step) in zip(partials[1:], routes):
        back.append(shifted(partial, axis, -step))
    grads = call(
        functools.partial(collect_kernel, times), shape_of((block_tokens, 3 * PART)), [dq, *back]
    )
    core_grads = from_partner(grads, "gz")
    planned = count_x == 4 and count_y == 4 and count_z == 2
    chunks = 4 if planned else 1
    piece = shape_of((half // chunks, 8 * PART))
    pair_out, mine, *pieces = call(
        functools.partial(weight_kernel, chunks),
        (shape_of((tokens, 6 * PART)), shape_of((tokens, 6 * PART)), *[piece] * chunks),
        [grads, core_grads, feat_t, out_term],
        scratch=[pltpu.VMEM((block_tokens, 6 * PART), BF), pltpu.VMEM((half, 8 * PART), BF)],
        flops=2 * block_tokens * half * 6 * PART,
    )
    def features_grad(pair_rows):
        return call(
            functools.partial(grad_x_kernel, own_half),
            shape_of(features.shape),
            [mine, pair_rows, *pairs],
            scratch=[pltpu.VMEM((tokens, 3 * width), BF), pltpu.VMEM((tokens, width), BF)],
            flops=2 * tokens * 3 * width * width,
        )

    if planned:
        terms = [pieces[0]] + [plane_swap(pieces[at], at, 0) for at in (1, 2, 3)]
        total = call(sum_kernel, piece, terms)
        pair_in = from_partner(pair_out, "gy")
        total, pair_in = lax.optimization_barrier((total, pair_in))
        other = plane_swap(total, 0, 2)
        grad_x = features_grad(pair_in)
        total, grad_x = lax.optimization_barrier((total, grad_x))
        total = call(sum_kernel, piece, [total, other])
        by_x, by_y, by_z = plane_swap(total, 1, 0), plane_swap(total, 2, 0), plane_swap(total, 0, 1)
        by_xy, by_xz = plane_swap(by_y, 1, 0), plane_swap(by_x, 0, 1)
        by_yz, by_xyz = plane_swap(by_z, 2, 0), plane_swap(by_z, 3, 0)
        weights = call(
            spread_kernel,
            tuple([shape_of((half, width), F32)] * 4),
            [total, by_z, by_x, by_xz, by_y, by_yz, by_xy, by_xyz],
        )
    else:
        grad_x = features_grad(from_partner(pair_out, "gy"))
        terms = pieces[0].astype(F32)
        stacked = jnp.zeros((4, width, width), F32)
        for base, at in ((0, 0), (1, 1), (2, 2)):
            for side in range(2):
                tile = terms[:, (base * 2 + side) * PART : (base * 2 + side + 1) * PART]
                stacked = lax.dynamic_update_slice(
                    stacked, tile[None], (at, z_bit * half, side * half + y_bit * PART)
                )
        tile = terms[:, 6 * PART :].reshape(4, 2, 32, half)
        tile = tile.transpose(0, 2, 1, 3).reshape(PART, width)
        stacked = lax.dynamic_update_slice(
            stacked, tile[None], (3, z_bit * half + y_bit * PART, 0)
        )
        stacked = lax.psum(stacked, ("gx", "gy", "gz"))
        held_rows = w_query.shape[0]
        stacked = lax.dynamic_slice_in_dim(stacked, lax.axis_index("gz") * held_rows, held_rows, 1)
        weights = [stacked[at] for at in range(4)]
    return (grad_x, *weights)


def solution(mesh):
    return jax.shard_map(
        on_device,
        mesh=mesh,
        in_specs=(
            P("gx", "gy", "gz", None),
            P("gx", "gy", "gz", None),
            P("gx", "gy", "gz", None),
            P("gz", None),
            P("gz", None),
            P("gz", None),
            P("gz", None),
        ),
        out_specs=(
            P("gx", "gy", "gz", None),
            P("gz", None),
            P("gz", None),
            P("gz", None),
            P("gz", None),
        ),
        check_vma=False,
    )
```

```python
import functools
import math

import jax
import jax.numpy as jnp
from jax import lax
from jax.experimental import pallas as pl
from jax.experimental.pallas import tpu as pltpu
from jax.sharding import PartitionSpec as P

HEADS = 8
PART = 128
BF = jnp.bfloat16
F32 = jnp.float32
VMEM_BYTES = 32 * 1024 * 1024


def from_partner(block, axis):
    route = [(index, index ^ 1) for index in range(lax.axis_size(axis))]
    return lax.ppermute(block, axis, route)


def shifted(value, axis, steps):
    count = lax.axis_size(axis)
    return lax.ppermute(value, axis, [(source, (source + steps) % count) for source in range(count)])


def plane_swap(value, flip_x, flip_y):
    count_x, count_y = lax.axis_size("gx"), lax.axis_size("gy")
    route = []
    for at_x in range(count_x):
        for at_y in range(count_y):
            route.append((at_x * count_y + at_y, (at_x ^ flip_x) * count_y + (at_y ^ flip_y)))
    return lax.ppermute(value, ("gx", "gy"), route)


def dot_nn(left, right):
    return lax.dot_general(left, right, (((1,), (0,)), ((), ())), preferred_element_type=F32)


def dot_nt(left, right):
    return lax.dot_general(left, right, (((1,), (1,)), ((), ())), preferred_element_type=F32)


def dot_tn(left, right):
    return lax.dot_general(left, right, (((0,), (0,)), ((), ())), preferred_element_type=F32)


def columns(start):
    return pl.ds(pl.multiple_of(start, PART), PART)


def call(kernel, out_shape, args, scratch=(), flops=1e6, moved=1e6, exps=0, spaces=None):
    specs = [pl.BlockSpec(memory_space=space or pltpu.VMEM) for space in spaces or [None] * len(args)]
    return pl.pallas_call(
        kernel,
        out_shape=out_shape,
        in_specs=specs,
        scratch_shapes=list(scratch),
        compiler_params=pltpu.CompilerParams(vmem_limit_bytes=VMEM_BYTES),
        cost_estimate=pl.CostEstimate(
            flops=int(flops), bytes_accessed=int(moved), transcendentals=int(exps)
        ),
    )(*args)


def shape_of(dims, dtype=BF):
    return jax.ShapeDtypeStruct(dims, dtype)


def pack_kernel(dy_ref, saved_ref, pair_ref, own_ref, saved_s):
    y_bit = lax.axis_index("gy") % 2
    z_bit = lax.axis_index("gz") % 2
    tokens = pair_ref.shape[0]
    width = dy_ref.shape[-1]
    last = PART + width
    dys = dy_ref[...].reshape(tokens, width)
    saved_s[...] = saved_ref[...].reshape(tokens, width)
    for out in (pair_ref, own_ref):
        out[:, PART:last] = dys
    pair_ref[:, 0:PART] = saved_s[:, columns((z_bit * 2 + 1 - y_bit) * PART)]
    pair_ref[:, last:] = saved_s[:, columns(((1 - z_bit) * 2 + 1 - y_bit) * PART)]
    own_ref[:, 0:PART] = saved_s[:, columns(((1 - z_bit) * 2 + y_bit) * PART)]
    own_ref[:, last:] = saved_s[:, columns((z_bit * 2 + y_bit) * PART)]


def columns_kernel(own_half, wq0, wq1, wk0, wk1, wv0, wv1, w_cols):
    y_bit = lax.axis_index("gy") % 2
    z_bit = lax.axis_index("gz") % 2
    half = z_bit if own_half else z_bit * 0
    group = columns((z_bit * 2 + y_bit) * PART)
    half_rows = wq0.shape[0]
    for at, (first, second) in enumerate(((wq0, wq1), (wk0, wk1), (wv0, wv1))):
        spot = slice(at * PART, (at + 1) * PART)
        w_cols[pl.ds(pl.multiple_of(half * half_rows, half_rows), half_rows), spot] = first[:, group]
        w_cols[pl.ds(pl.multiple_of((1 - half) * half_rows, half_rows), half_rows), spot] = second[:, group]


def project_kernel(own, core, pair, far, w_cols, q_ref, kv_ref):
    width = own.shape[1]
    for at, source in enumerate((own, core, pair, far)):
        rows = slice(at * PART, (at + 1) * PART)
        made = dot_nn(source[...], w_cols[...])
        q_ref[rows, :] = made[:, 0:PART].astype(BF) * jnp.asarray(1.0 / math.sqrt(width // HEADS), BF)
        kv_ref[rows, :] = made[:, PART:].astype(BF)


def early_kernel(
    f_own, f_core, f_pair, f_far, own, core, pair, far, wout,
    do_ref, delta_ref, feat_t_ref, o_ref, saved, dys,
):
    y_bit = lax.axis_index("gy") % 2
    z_bit = lax.axis_index("gz") % 2
    width = f_own.shape[1]
    half = width // 2
    last = PART + width
    for at, (source, spot) in enumerate(((own, last), (core, 0), (pair, 0), (far, last))):
        rows = slice(at * PART, (at + 1) * PART)
        saved[rows, :] = source[:, spot : spot + PART]
        dys[rows, :] = source[:, PART:last]
    for at, source in enumerate((f_own, f_core, f_pair, f_far)):
        wanted = source[:, pl.ds(pl.multiple_of(z_bit * half, PART), half)]
        feat_t_ref[:, at * PART : (at + 1) * PART] = wanted.astype(F32).T.astype(BF)
    w_rows = wout[pl.ds(pl.multiple_of(y_bit * PART, PART), PART), :]
    out_grad = dot_nt(dys[...], w_rows).astype(BF)
    do_ref[...] = out_grad
    head_dim = width // HEADS
    products = (out_grad.astype(F32) * saved[...].astype(F32)).T
    delta_ref[0:1, :] = jnp.sum(products[0:head_dim], axis=0, keepdims=True)
    delta_ref[1:2, :] = jnp.sum(products[head_dim:PART], axis=0, keepdims=True)
    out = dot_nn(saved[...].astype(F32).T.astype(BF), dys[...]).astype(BF)
    for at in range(4):
        low = out[at * 32 : (at + 1) * 32, :]
        o_ref[at * 64 : at * 64 + 32, :] = low[:, 0:half]
        o_ref[at * 64 + 32 : at * 64 + 64, :] = low[:, half:]


def by_head(value):
    low = lax.broadcasted_iota(jnp.int32, value.shape, 1) < PART // 2
    none = jnp.zeros_like(value)
    return (jnp.where(low, value, none), jnp.where(low, none, value))


def row_scale(table, at, tokens):
    low = lax.broadcasted_iota(jnp.int32, (tokens, PART), 1) < PART // 2
    return jnp.where(low, table[:, 2 * at : 2 * at + 1], table[:, 2 * at + 1 : 2 * at + 2])


def score_kernel(q_ref, *refs):
    count = len(refs) - 2
    e_ref, table_ref = refs[count:]
    half = table_ref.shape[0] // 2
    q_heads = by_head(q_ref[...])
    if half > 2 * count:
        table_ref[...] = jnp.zeros_like(table_ref)
    for at in range(count):
        keys = refs[at][:, 0:PART]
        for head in range(2):
            scores = dot_nt(keys, q_heads[head])
            top = jnp.max(scores, axis=0, keepdims=True)
            grown = jnp.exp(scores - top)
            row = 2 * at + head
            e_ref[row] = grown.astype(BF)
            table_ref[row : row + 1, :] = top
            table_ref[half + row : half + row + 1, :] = jnp.sum(grown, axis=0, keepdims=True)


def gradient_kernel(times, groups, q_ref, do_ref, delta_ref, *refs):
    count = len(times)
    e_refs, tables = refs[: 2 * len(groups) : 2], refs[1 : 2 * len(groups) : 2]
    refs = refs[2 * len(groups) :]
    kvs, dq_ref, outs, dq_s, part_s = (
        refs[:count], refs[count], refs[count + 1 : 2 * count + 1], refs[-2], refs[-1]
    )
    where = [(group, at) for group, blocks in enumerate(groups) for at in range(blocks)]
    if part_s.shape[0] > 2 * count:
        part_s[...] = jnp.zeros_like(part_s)
    for head in range(2):
        tops, totals = [], []
        for group, at in where:
            half = tables[group].shape[0] // 2
            row = 2 * at + head
            tops.append(tables[group][row : row + 1, :])
            totals.append(tables[group][half + row : half + row + 1, :])
        most = functools.reduce(jnp.maximum, tops)
        lifts = [jnp.exp(top - most) for top in tops]
        total = functools.reduce(
            jnp.add, [time * lift * part for time, lift, part in zip(times, lifts, totals)]
        )
        for at in range(count):
            part_s[2 * at + head : 2 * at + head + 1, :] = lifts[at] / total
    tokens = q_ref.shape[0]
    head_dim = PART // 2
    turned = part_s[...].T
    grad = do_ref[...]
    g_heads = by_head(grad)
    grad = grad.astype(F32)
    query = q_ref[...].astype(F32)
    delta = delta_ref[...]
    for at in range(count):
        keys_t = kvs[at][:, 0:PART].astype(F32).T.astype(BF)
        values = kvs[at][:, PART:]
        group, place = where[at]
        scale = row_scale(turned, at, tokens)
        q_scaled = by_head((query * scale).astype(BF))
        g_scaled = by_head((grad * scale).astype(BF))
        dks, dvs = [], []
        for head in range(2):
            grown = e_refs[group][2 * place + head]
            dprob = dot_nt(values, g_heads[head])
            dscore = (grown.astype(F32) * (dprob - delta[head : head + 1, :])).astype(BF)
            dvs.append(dot_nn(grown, g_scaled[head]))
            dks.append(dot_nn(dscore, q_scaled[head]))
            spot = slice(head * head_dim, (head + 1) * head_dim)
            part = part_s[2 * at + head : 2 * at + head + 1, :] * times[at]
            added = dot_nn(keys_t[spot, :], dscore) * part
            dq_s[spot, :] = added if at == 0 else dq_s[spot, :] + added
        outs[at][:, 0:PART] = (dks[0] + dks[1]).astype(BF)
        outs[at][:, PART:] = (dvs[0] + dvs[1]).astype(BF)
    dq_ref[...] = (dq_s[...].T * (1.0 / math.sqrt(head_dim))).astype(BF)


def collect_kernel(times, dq_ref, *refs):
    total = times[0] * refs[0][...].astype(F32)
    for time, ref in zip(times[1:], refs[1:-1]):
        total = total + time * ref[...].astype(F32)
    refs[-1][:, 0:PART] = dq_ref[...]
    refs[-1][:, PART:] = total.astype(BF)


def place_grads(grads, own, core, count):
    z_bit = lax.axis_index("gz") % 2
    for at in range(count):
        source = slice(at * PART, (at + 1) * PART)
        grads[:, columns(at * 2 * PART + z_bit * PART)] = own[:, source]
        core_at = columns(at * 2 * PART + (1 - z_bit) * PART)
        for low in range(4):
            grads[low * PART : (low + 1) * PART, core_at] = core[
                (low ^ 1) * PART : ((low ^ 1) + 1) * PART, source
            ]


def weight_kernel(chunks, own, core, feat_t, o_ref, pair_ref, mine_ref, *refs):
    outs, (grads, made) = refs[:chunks], refs[chunks:]
    place_grads(grads, own, core, 3)
    mine_ref[...] = grads[0:PART, :]
    pair_ref[...] = grads[2 * PART : 3 * PART, :]
    wide = grads.shape[1]
    made[:, 0:wide] = dot_nn(feat_t[...], grads[...]).astype(BF)
    made[:, wide:] = o_ref[...]
    rows = made.shape[0] // chunks
    for at in range(chunks):
        spot = pl.ds(0, rows)
        if chunks > 1:
            spot = pl.ds(pl.multiple_of((lax.axis_index("gx") ^ at) * rows, rows), rows)
        outs[at][...] = made[spot, :]


def grad_x_kernel(own_half, mine, pair, wq0, wq1, wk0, wk1, wv0, wv1, out, full, made):
    y_bit = lax.axis_index("gy") % 2
    z_bit = lax.axis_index("gz") % 2
    half = z_bit if own_half else z_bit * 0
    width = wq0.shape[1]
    half_rows = wq0.shape[0]
    for at in range(3):
        for side in range(2):
            spot = slice((at * 2 + side) * PART, (at * 2 + side + 1) * PART)
            base = at * width + side * 2 * PART
            full[:, columns(base + y_bit * PART)] = mine[:, spot]
            full[:, columns(base + (1 - y_bit) * PART)] = pair[:, spot]
    for at, sources in ((half, (wq0, wk0, wv0)), (1 - half, (wq1, wk1, wv1))):
        total = functools.reduce(
            jnp.add,
            [dot_nt(full[:, n * width : (n + 1) * width], sources[n][...]) for n in range(3)],
        )
        made[:, pl.ds(pl.multiple_of(at * half_rows, PART), half_rows)] = total.astype(BF)
    out[...] = made[...].reshape(out.shape)


def sum_kernel(*refs):
    total = refs[0][...].astype(F32)
    for ref in refs[1:-1]:
        total = total + ref[...].astype(F32)
    refs[-1][...] = total.astype(BF)


def spread_kernel(*refs):
    pieces, outs = refs[:8], refs[8:]
    half = 2 * PART
    rows = pieces[0].shape[0]
    for at, piece in enumerate(pieces):
        place = lax.axis_index("gx") ^ (at // 2)
        bit = (lax.axis_index("gy") % 2) ^ (at % 2)
        spot = pl.ds(pl.multiple_of(place * rows, rows), rows)
        for base, out in enumerate(outs[:3]):
            for side in range(2):
                source = slice((base * 2 + side) * PART, (base * 2 + side + 1) * PART)
                out[spot, columns(side * half + bit * PART)] = piece[:, source].astype(F32)
        spot = pl.ds(pl.multiple_of(bit * PART + place * (rows // 2), rows // 2), rows // 2)
        outs[3][spot, 0:half] = piece[0 : rows // 2, 3 * half :].astype(F32)
        outs[3][spot, half:] = piece[rows // 2 :, 3 * half :].astype(F32)


def on_device(features, grad_y, attn_out, w_query, w_key, w_value, w_out):
    width = features.shape[-1]
    half = width // 2
    tokens = features.shape[0] * features.shape[1] * features.shape[2]
    block_tokens = 4 * tokens
    count_x, count_y, count_z = lax.axis_size("gx"), lax.axis_size("gy"), lax.axis_size("gz")
    z_bit = lax.axis_index("gz") % 2
    y_bit = lax.axis_index("gy") % 2

    own_half = count_z == 2
    if own_half:
        pairs = []
        for weight in (w_query, w_key, w_value):
            pairs += [weight, from_partner(weight, "gz")]
        out_rows = w_out
    else:
        pairs = []
        for weight in (w_query, w_key, w_value):
            whole = lax.all_gather(weight, "gz", axis=0, tiled=True)
            pairs += [whole[:half], whole[half:]]
        whole = lax.all_gather(w_out, "gz", axis=0, tiled=True)
        out_rows = lax.dynamic_slice_in_dim(whole, z_bit * half, half, 0)

    message = shape_of((tokens, width + 2 * PART))
    feat = features.reshape(tokens, width)
    feat_pair = from_partner(feat, "gy")
    feat_core = from_partner(feat, "gz")
    w_cols = call(
        functools.partial(columns_kernel, own_half),
        shape_of((width, 3 * PART)),
        pairs,
    )
    feat_pair, feat_core, w_cols = lax.optimization_barrier((feat_pair, feat_core, w_cols))
    feat_far = from_partner(feat_pair, "gz")
    feats = [feat, feat_core, feat_pair, feat_far]
    column = shape_of((block_tokens, PART))
    both = shape_of((block_tokens, 2 * PART))
    query, own_kv = call(
        project_kernel,
        (column, both),
        [*feats, w_cols],
        flops=2 * block_tokens * width * 3 * PART,
    )

    times = [1.0]
    routes = []
    for axis, step, blocks in (("gx", 1, count_x), ("gy", 2, count_y // 2), ("gz", 2, count_z // 2)):
        if blocks == 1:
            times[0] += 2.0
        elif blocks == 2:
            routes.append((axis, step))
            times.append(2.0)
        else:
            routes += [(axis, step), (axis, -step)]
            times += [1.0, 1.0]
    times = tuple(times)
    count = len(times)
    near = [own_kv] + [shifted(own_kv, axis, step) for axis, step in routes]
    late_dy, late_saved, query = lax.optimization_barrier((grad_y, attn_out, query))
    pair_message, own = call(
        pack_kernel,
        (message, message),
        [late_dy, late_saved],
        scratch=[pltpu.VMEM((tokens, width), BF)],
    )
    pair = from_partner(pair_message, "gy")
    core = from_partner(own, "gz")
    far = from_partner(pair, "gz")
    out_grad, delta, feat_t, out_term = call(
        early_kernel,
        (
            column,
            shape_of((2, block_tokens), F32),
            shape_of((half, block_tokens)),
            shape_of((half, half)),
        ),
        [*feats, own, core, pair, far, out_rows],
        scratch=[pltpu.VMEM((block_tokens, PART), BF), pltpu.VMEM((block_tokens, width), BF)],
        flops=4 * block_tokens * width * PART,
    )
    pixels = 2 * block_tokens * block_tokens
    groups = (2, count - 2)
    scored = []
    place = 0
    for blocks in groups:
        rows = -(-2 * blocks // 8) * 8
        scored += call(
            score_kernel,
            (
                shape_of((2 * blocks, block_tokens, block_tokens)),
                shape_of((2 * rows, block_tokens), F32),
            ),
            [query, *near[place : place + blocks]],
            flops=2 * pixels * blocks * PART,
            moved=2 * pixels * blocks,
            exps=pixels * blocks,
        )
        place += blocks
    dq, *partials = call(
        functools.partial(gradient_kernel, times, groups),
        (column, *[both] * count),
        [query, out_grad, delta, *scored, *near],
        scratch=[
            pltpu.VMEM((PART, block_tokens), F32),
            pltpu.VMEM((-(-2 * count // 8) * 8, block_tokens), F32),
        ],
        flops=8 * pixels * count * PART,
        moved=2 * pixels * count,
    )
    back = []
    for partial, (axis, step) in reversed(list(zip(partials[1:], routes))):
        back.append(shifted(partial, axis, -step))
    back.append(partials[0])
    grads = call(
        functools.partial(collect_kernel, times[::-1]), shape_of((block_tokens, 3 * PART)), [dq, *back]
    )
    core_grads = from_partner(grads, "gz")
    planned = count_x == 4 and count_y == 4 and count_z == 2
    chunks = 4 if planned else 1
    piece = shape_of((half // chunks, 8 * PART))
    pair_out, mine, *pieces = call(
        functools.partial(weight_kernel, chunks),
        (shape_of((tokens, 6 * PART)), shape_of((tokens, 6 * PART)), *[piece] * chunks),
        [grads, core_grads, feat_t, out_term],
        scratch=[pltpu.VMEM((block_tokens, 6 * PART), BF), pltpu.VMEM((half, 8 * PART), BF)],
        flops=2 * block_tokens * half * 6 * PART,
    )
    def features_grad(pair_rows):
        return call(
            functools.partial(grad_x_kernel, own_half),
            shape_of(features.shape),
            [mine, pair_rows, *pairs],
            scratch=[pltpu.VMEM((tokens, 3 * width), BF), pltpu.VMEM((tokens, width), BF)],
            flops=2 * tokens * 3 * width * width,
        )

    if planned:
        terms = [pieces[0]] + [plane_swap(pieces[at], at, 0) for at in (1, 2, 3)]
        total = call(sum_kernel, piece, terms)
        pair_in = from_partner(pair_out, "gy")
        total, pair_in = lax.optimization_barrier((total, pair_in))
        other = plane_swap(total, 0, 2)
        grad_x = features_grad(pair_in)
        total, grad_x = lax.optimization_barrier((total, grad_x))
        total = call(sum_kernel, piece, [total, other])
        by_x, by_y, by_z = plane_swap(total, 1, 0), plane_swap(total, 2, 0), plane_swap(total, 0, 1)
        by_xy, by_xz = plane_swap(by_y, 1, 0), plane_swap(by_x, 0, 1)
        by_yz, by_xyz = plane_swap(by_z, 2, 0), plane_swap(by_xy, 0, 1)
        weights = call(
            spread_kernel,
            tuple([shape_of((half, width), F32)] * 4),
            [total, by_z, by_x, by_xz, by_y, by_yz, by_xy, by_xyz],
        )
    else:
        grad_x = features_grad(from_partner(pair_out, "gy"))
        terms = pieces[0].astype(F32)
        stacked = jnp.zeros((4, width, width), F32)
        for base, at in ((0, 0), (1, 1), (2, 2)):
            for side in range(2):
                tile = terms[:, (base * 2 + side) * PART : (base * 2 + side + 1) * PART]
                stacked = lax.dynamic_update_slice(
                    stacked, tile[None], (at, z_bit * half, side * half + y_bit * PART)
                )
        tile = terms[:, 6 * PART :].reshape(4, 2, 32, half)
        tile = tile.transpose(0, 2, 1, 3).reshape(PART, width)
        stacked = lax.dynamic_update_slice(
            stacked, tile[None], (3, z_bit * half + y_bit * PART, 0)
        )
        stacked = lax.psum(stacked, ("gx", "gy", "gz"))
        held_rows = w_query.shape[0]
        stacked = lax.dynamic_slice_in_dim(stacked, lax.axis_index("gz") * held_rows, held_rows, 1)
        weights = [stacked[at] for at in range(4)]
    return (grad_x, *weights)


def solution(mesh):
    return jax.shard_map(
        on_device,
        mesh=mesh,
        in_specs=(
            P("gx", "gy", "gz", None),
            P("gx", "gy", "gz", None),
            P("gx", "gy", "gz", None),
            P("gz", None),
            P("gz", None),
            P("gz", None),
            P("gz", None),
        ),
        out_specs=(
            P("gx", "gy", "gz", None),
            P("gz", None),
            P("gz", None),
            P("gz", None),
            P("gz", None),
        ),
        check_vma=False,
    )
```

```python
import functools
import math

import jax
import jax.numpy as jnp
from jax import lax
from jax.experimental import pallas as pl
from jax.experimental.pallas import tpu as pltpu
from jax.sharding import PartitionSpec as P

HEADS = 8
PART = 128
BF = jnp.bfloat16
F32 = jnp.float32
VMEM_BYTES = 32 * 1024 * 1024


def from_partner(block, axis):
    route = [(index, index ^ 1) for index in range(lax.axis_size(axis))]
    return lax.ppermute(block, axis, route)


def shifted(value, axis, steps):
    count = lax.axis_size(axis)
    return lax.ppermute(value, axis, [(source, (source + steps) % count) for source in range(count)])


def plane_swap(value, flip_x, flip_y):
    count_x, count_y = lax.axis_size("gx"), lax.axis_size("gy")
    route = []
    for at_x in range(count_x):
        for at_y in range(count_y):
            route.append((at_x * count_y + at_y, (at_x ^ flip_x) * count_y + (at_y ^ flip_y)))
    return lax.ppermute(value, ("gx", "gy"), route)


def dot_nn(left, right):
    return lax.dot_general(left, right, (((1,), (0,)), ((), ())), preferred_element_type=F32)


def dot_nt(left, right):
    return lax.dot_general(left, right, (((1,), (1,)), ((), ())), preferred_element_type=F32)


def dot_tn(left, right):
    return lax.dot_general(left, right, (((0,), (0,)), ((), ())), preferred_element_type=F32)


def columns(start):
    return pl.ds(pl.multiple_of(start, PART), PART)


def call(kernel, out_shape, args, scratch=(), flops=1e6, moved=1e6, exps=0, spaces=None):
    specs = [pl.BlockSpec(memory_space=space or pltpu.VMEM) for space in spaces or [None] * len(args)]
    return pl.pallas_call(
        kernel,
        out_shape=out_shape,
        in_specs=specs,
        scratch_shapes=list(scratch),
        compiler_params=pltpu.CompilerParams(vmem_limit_bytes=VMEM_BYTES),
        cost_estimate=pl.CostEstimate(
            flops=int(flops), bytes_accessed=int(moved), transcendentals=int(exps)
        ),
    )(*args)


def shape_of(dims, dtype=BF):
    return jax.ShapeDtypeStruct(dims, dtype)


def pack_kernel(dy_ref, saved_ref, pair_ref, own_ref, saved_s):
    y_bit = lax.axis_index("gy") % 2
    z_bit = lax.axis_index("gz") % 2
    tokens = pair_ref.shape[0]
    width = dy_ref.shape[-1]
    last = PART + width
    dys = dy_ref[...].reshape(tokens, width)
    saved_s[...] = saved_ref[...].reshape(tokens, width)
    for out in (pair_ref, own_ref):
        out[:, PART:last] = dys
    pair_ref[:, 0:PART] = saved_s[:, columns((z_bit * 2 + 1 - y_bit) * PART)]
    pair_ref[:, last:] = saved_s[:, columns(((1 - z_bit) * 2 + 1 - y_bit) * PART)]
    own_ref[:, 0:PART] = saved_s[:, columns(((1 - z_bit) * 2 + y_bit) * PART)]
    own_ref[:, last:] = saved_s[:, columns((z_bit * 2 + y_bit) * PART)]


def columns_kernel(own_half, wq0, wq1, wk0, wk1, wv0, wv1, w_cols):
    y_bit = lax.axis_index("gy") % 2
    z_bit = lax.axis_index("gz") % 2
    half = z_bit if own_half else z_bit * 0
    group = columns((z_bit * 2 + y_bit) * PART)
    half_rows = wq0.shape[0]
    for at, (first, second) in enumerate(((wq0, wq1), (wk0, wk1), (wv0, wv1))):
        spot = slice(at * PART, (at + 1) * PART)
        w_cols[pl.ds(pl.multiple_of(half * half_rows, half_rows), half_rows), spot] = first[:, group]
        w_cols[pl.ds(pl.multiple_of((1 - half) * half_rows, half_rows), half_rows), spot] = second[:, group]


def project_kernel(own, core, pair, far, w_cols, q_ref, kv_ref):
    width = own.shape[1]
    for at, source in enumerate((own, core, pair, far)):
        rows = slice(at * PART, (at + 1) * PART)
        made = dot_nn(source[...], w_cols[...])
        q_ref[rows, :] = made[:, 0:PART].astype(BF) * jnp.asarray(1.0 / math.sqrt(width // HEADS), BF)
        kv_ref[rows, :] = made[:, PART:].astype(BF)


def early_kernel(
    f_own, f_core, f_pair, f_far, own, core, pair, far, wout,
    do_ref, delta_ref, feat_t_ref, o_ref, saved, dys,
):
    y_bit = lax.axis_index("gy") % 2
    z_bit = lax.axis_index("gz") % 2
    width = f_own.shape[1]
    half = width // 2
    last = PART + width
    for at, (source, spot) in enumerate(((own, last), (core, 0), (pair, 0), (far, last))):
        rows = slice(at * PART, (at + 1) * PART)
        saved[rows, :] = source[:, spot : spot + PART]
        dys[rows, :] = source[:, PART:last]
    for at, source in enumerate((f_own, f_core, f_pair, f_far)):
        wanted = source[:, pl.ds(pl.multiple_of(z_bit * half, PART), half)]
        feat_t_ref[:, at * PART : (at + 1) * PART] = wanted.astype(F32).T.astype(BF)
    w_rows = wout[pl.ds(pl.multiple_of(y_bit * PART, PART), PART), :]
    out_grad = dot_nt(dys[...], w_rows).astype(BF)
    do_ref[...] = out_grad
    head_dim = width // HEADS
    products = (out_grad.astype(F32) * saved[...].astype(F32)).T
    delta_ref[0:1, :] = jnp.sum(products[0:head_dim], axis=0, keepdims=True)
    delta_ref[1:2, :] = jnp.sum(products[head_dim:PART], axis=0, keepdims=True)
    out = dot_nn(saved[...].astype(F32).T.astype(BF), dys[...]).astype(BF)
    for at in range(4):
        low = out[at * 32 : (at + 1) * 32, :]
        o_ref[at * 64 : at * 64 + 32, :] = low[:, 0:half]
        o_ref[at * 64 + 32 : at * 64 + 64, :] = low[:, half:]


def by_head(value):
    low = lax.broadcasted_iota(jnp.int32, value.shape, 1) < PART // 2
    none = jnp.zeros_like(value)
    return (jnp.where(low, value, none), jnp.where(low, none, value))


def row_scale(table, at, tokens):
    low = lax.broadcasted_iota(jnp.int32, (tokens, PART), 1) < PART // 2
    return jnp.where(low, table[:, 2 * at : 2 * at + 1], table[:, 2 * at + 1 : 2 * at + 2])


def score_kernel(q_ref, do_ref, delta_ref, *refs):
    count = len(refs) - 3
    e_ref, ds_ref, table_ref = refs[count:]
    half = table_ref.shape[0] // 2
    q_heads = by_head(q_ref[...])
    g_heads = by_head(do_ref[...])
    delta = delta_ref[...]
    if half > 2 * count:
        table_ref[...] = jnp.zeros_like(table_ref)
    for at in range(count):
        keys = refs[at][:, 0:PART]
        values = refs[at][:, PART:]
        for head in range(2):
            scores = dot_nt(keys, q_heads[head])
            top = jnp.max(scores, axis=0, keepdims=True)
            grown = jnp.exp(scores - top)
            row = 2 * at + head
            rounded = grown.astype(BF)
            e_ref[row] = rounded
            dprob = dot_nt(values, g_heads[head])
            ds_ref[row] = (rounded.astype(F32) * (dprob - delta[head : head + 1, :])).astype(BF)
            table_ref[row : row + 1, :] = top
            table_ref[half + row : half + row + 1, :] = jnp.sum(grown, axis=0, keepdims=True)


def gradient_kernel(times, groups, q_ref, do_ref, *refs):
    count = len(times)
    e_refs, ds_refs, tables = (refs[at : 3 * len(groups) : 3] for at in range(3))
    refs = refs[3 * len(groups) :]
    kvs, dq_ref, outs, dq_s, part_s = (
        refs[:count], refs[count], refs[count + 1 : 2 * count + 1], refs[-2], refs[-1]
    )
    where = [(group, at) for group, blocks in enumerate(groups) for at in range(blocks)]
    if part_s.shape[0] > 2 * count:
        part_s[...] = jnp.zeros_like(part_s)
    for head in range(2):
        tops, totals = [], []
        for group, at in where:
            half = tables[group].shape[0] // 2
            row = 2 * at + head
            tops.append(tables[group][row : row + 1, :])
            totals.append(tables[group][half + row : half + row + 1, :])
        most = functools.reduce(jnp.maximum, tops)
        lifts = [jnp.exp(top - most) for top in tops]
        total = functools.reduce(
            jnp.add, [time * lift * part for time, lift, part in zip(times, lifts, totals)]
        )
        for at in range(count):
            part_s[2 * at + head : 2 * at + head + 1, :] = lifts[at] / total
    tokens = q_ref.shape[0]
    head_dim = PART // 2
    turned = part_s[...].T
    grad = do_ref[...].astype(F32)
    query = q_ref[...].astype(F32)
    for at in range(count):
        keys_t = kvs[at][:, 0:PART].astype(F32).T.astype(BF)
        group, place = where[at]
        scale = row_scale(turned, at, tokens)
        q_scaled = by_head((query * scale).astype(BF))
        g_scaled = by_head((grad * scale).astype(BF))
        dks, dvs = [], []
        for head in range(2):
            grown = e_refs[group][2 * place + head]
            dscore = ds_refs[group][2 * place + head]
            dvs.append(dot_nn(grown, g_scaled[head]))
            dks.append(dot_nn(dscore, q_scaled[head]))
            spot = slice(head * head_dim, (head + 1) * head_dim)
            part = part_s[2 * at + head : 2 * at + head + 1, :] * times[at]
            added = dot_nn(keys_t[spot, :], dscore) * part
            dq_s[spot, :] = added if at == 0 else dq_s[spot, :] + added
        outs[at][:, 0:PART] = (dks[0] + dks[1]).astype(BF)
        outs[at][:, PART:] = (dvs[0] + dvs[1]).astype(BF)
    dq_ref[...] = (dq_s[...].T * (1.0 / math.sqrt(head_dim))).astype(BF)


def collect_kernel(times, dq_ref, *refs):
    total = times[0] * refs[0][...].astype(F32)
    for time, ref in zip(times[1:], refs[1:-1]):
        total = total + time * ref[...].astype(F32)
    refs[-1][:, 0:PART] = dq_ref[...]
    refs[-1][:, PART:] = total.astype(BF)


def place_grads(grads, own, core, count):
    z_bit = lax.axis_index("gz") % 2
    for at in range(count):
        source = slice(at * PART, (at + 1) * PART)
        grads[:, columns(at * 2 * PART + z_bit * PART)] = own[:, source]
        core_at = columns(at * 2 * PART + (1 - z_bit) * PART)
        for low in range(4):
            grads[low * PART : (low + 1) * PART, core_at] = core[
                (low ^ 1) * PART : ((low ^ 1) + 1) * PART, source
            ]


def weight_kernel(chunks, own, core, feat_t, o_ref, pair_ref, mine_ref, *refs):
    outs, (grads, made) = refs[:chunks], refs[chunks:]
    place_grads(grads, own, core, 3)
    mine_ref[...] = grads[0:PART, :]
    pair_ref[...] = grads[2 * PART : 3 * PART, :]
    wide = grads.shape[1]
    made[:, 0:wide] = dot_nn(feat_t[...], grads[...]).astype(BF)
    made[:, wide:] = o_ref[...]
    rows = made.shape[0] // chunks
    for at in range(chunks):
        spot = pl.ds(0, rows)
        if chunks > 1:
            spot = pl.ds(pl.multiple_of((lax.axis_index("gx") ^ at) * rows, rows), rows)
        outs[at][...] = made[spot, :]


def grad_x_kernel(own_half, mine, pair, wq0, wq1, wk0, wk1, wv0, wv1, out, full, made):
    y_bit = lax.axis_index("gy") % 2
    z_bit = lax.axis_index("gz") % 2
    half = z_bit if own_half else z_bit * 0
    width = wq0.shape[1]
    half_rows = wq0.shape[0]
    for at in range(3):
        for side in range(2):
            spot = slice((at * 2 + side) * PART, (at * 2 + side + 1) * PART)
            base = at * width + side * 2 * PART
            full[:, columns(base + y_bit * PART)] = mine[:, spot]
            full[:, columns(base + (1 - y_bit) * PART)] = pair[:, spot]
    for at, sources in ((half, (wq0, wk0, wv0)), (1 - half, (wq1, wk1, wv1))):
        total = functools.reduce(
            jnp.add,
            [dot_nt(full[:, n * width : (n + 1) * width], sources[n][...]) for n in range(3)],
        )
        made[:, pl.ds(pl.multiple_of(at * half_rows, PART), half_rows)] = total.astype(BF)
    out[...] = made[...].reshape(out.shape)


def sum_kernel(*refs):
    total = refs[0][...].astype(F32)
    for ref in refs[1:-1]:
        total = total + ref[...].astype(F32)
    refs[-1][...] = total.astype(BF)


def spread_kernel(*refs):
    pieces, outs = refs[:8], refs[8:]
    half = 2 * PART
    rows = pieces[0].shape[0]
    for at, piece in enumerate(pieces):
        place = lax.axis_index("gx") ^ (at // 2)
        bit = (lax.axis_index("gy") % 2) ^ (at % 2)
        spot = pl.ds(pl.multiple_of(place * rows, rows), rows)
        for base, out in enumerate(outs[:3]):
            for side in range(2):
                source = slice((base * 2 + side) * PART, (base * 2 + side + 1) * PART)
                out[spot, columns(side * half + bit * PART)] = piece[:, source].astype(F32)
        spot = pl.ds(pl.multiple_of(bit * PART + place * (rows // 2), rows // 2), rows // 2)
        outs[3][spot, 0:half] = piece[0 : rows // 2, 3 * half :].astype(F32)
        outs[3][spot, half:] = piece[rows // 2 :, 3 * half :].astype(F32)


def on_device(features, grad_y, attn_out, w_query, w_key, w_value, w_out):
    width = features.shape[-1]
    half = width // 2
    tokens = features.shape[0] * features.shape[1] * features.shape[2]
    block_tokens = 4 * tokens
    count_x, count_y, count_z = lax.axis_size("gx"), lax.axis_size("gy"), lax.axis_size("gz")
    z_bit = lax.axis_index("gz") % 2
    y_bit = lax.axis_index("gy") % 2

    own_half = count_z == 2
    if own_half:
        pairs = []
        for weight in (w_query, w_key, w_value):
            pairs += [weight, from_partner(weight, "gz")]
        out_rows = w_out
    else:
        pairs = []
        for weight in (w_query, w_key, w_value):
            whole = lax.all_gather(weight, "gz", axis=0, tiled=True)
            pairs += [whole[:half], whole[half:]]
        whole = lax.all_gather(w_out, "gz", axis=0, tiled=True)
        out_rows = lax.dynamic_slice_in_dim(whole, z_bit * half, half, 0)

    message = shape_of((tokens, width + 2 * PART))
    feat = features.reshape(tokens, width)
    feat_pair = from_partner(feat, "gy")
    feat_core = from_partner(feat, "gz")
    w_cols = call(
        functools.partial(columns_kernel, own_half),
        shape_of((width, 3 * PART)),
        pairs,
    )
    feat_pair, feat_core, w_cols = lax.optimization_barrier((feat_pair, feat_core, w_cols))
    feat_far = from_partner(feat_pair, "gz")
    feats = [feat, feat_core, feat_pair, feat_far]
    column = shape_of((block_tokens, PART))
    both = shape_of((block_tokens, 2 * PART))
    query, own_kv = call(
        project_kernel,
        (column, both),
        [*feats, w_cols],
        flops=2 * block_tokens * width * 3 * PART,
    )

    times = [1.0]
    routes = []
    for axis, step, blocks in (("gx", 1, count_x), ("gy", 2, count_y // 2), ("gz", 2, count_z // 2)):
        if blocks == 1:
            times[0] += 2.0
        elif blocks == 2:
            routes.append((axis, step))
            times.append(2.0)
        else:
            routes += [(axis, step), (axis, -step)]
            times += [1.0, 1.0]
    times = tuple(times)
    count = len(times)
    near = [own_kv] + [shifted(own_kv, axis, step) for axis, step in routes]
    late_dy, late_saved, query = lax.optimization_barrier((grad_y, attn_out, query))
    pair_message, own = call(
        pack_kernel,
        (message, message),
        [late_dy, late_saved],
        scratch=[pltpu.VMEM((tokens, width), BF)],
    )
    pair = from_partner(pair_message, "gy")
    core = from_partner(own, "gz")
    far = from_partner(pair, "gz")
    out_grad, delta, feat_t, out_term = call(
        early_kernel,
        (
            column,
            shape_of((2, block_tokens), F32),
            shape_of((half, block_tokens)),
            shape_of((half, half)),
        ),
        [*feats, own, core, pair, far, out_rows],
        scratch=[pltpu.VMEM((block_tokens, PART), BF), pltpu.VMEM((block_tokens, width), BF)],
        flops=4 * block_tokens * width * PART,
    )
    pixels = 2 * block_tokens * block_tokens
    groups = (2, count - 2)
    scored = []
    place = 0
    for blocks in groups:
        rows = -(-2 * blocks // 8) * 8
        scored += call(
            score_kernel,
            (
                shape_of((2 * blocks, block_tokens, block_tokens)),
                shape_of((2 * blocks, block_tokens, block_tokens)),
                shape_of((2 * rows, block_tokens), F32),
            ),
            [query, out_grad, delta, *near[place : place + blocks]],
            flops=4 * pixels * blocks * PART,
            moved=4 * pixels * blocks,
            exps=pixels * blocks,
        )
        place += blocks
    dq, *partials = call(
        functools.partial(gradient_kernel, times, groups),
        (column, *[both] * count),
        [query, out_grad, *scored, *near],
        scratch=[
            pltpu.VMEM((PART, block_tokens), F32),
            pltpu.VMEM((-(-2 * count // 8) * 8, block_tokens), F32),
        ],
        flops=6 * pixels * count * PART,
        moved=4 * pixels * count,
    )
    back = []
    for partial, (axis, step) in reversed(list(zip(partials[1:], routes))):
        back.append(shifted(partial, axis, -step))
    back.append(partials[0])
    grads = call(
        functools.partial(collect_kernel, times[::-1]), shape_of((block_tokens, 3 * PART)), [dq, *back]
    )
    core_grads = from_partner(grads, "gz")
    planned = count_x == 4 and count_y == 4 and count_z == 2
    chunks = 4 if planned else 1
    piece = shape_of((half // chunks, 8 * PART))
    pair_out, mine, *pieces = call(
        functools.partial(weight_kernel, chunks),
        (shape_of((tokens, 6 * PART)), shape_of((tokens, 6 * PART)), *[piece] * chunks),
        [grads, core_grads, feat_t, out_term],
        scratch=[pltpu.VMEM((block_tokens, 6 * PART), BF), pltpu.VMEM((half, 8 * PART), BF)],
        flops=2 * block_tokens * half * 6 * PART,
    )
    def features_grad(pair_rows):
        return call(
            functools.partial(grad_x_kernel, own_half),
            shape_of(features.shape),
            [mine, pair_rows, *pairs],
            scratch=[pltpu.VMEM((tokens, 3 * width), BF), pltpu.VMEM((tokens, width), BF)],
            flops=2 * tokens * 3 * width * width,
        )

    if planned:
        terms = [pieces[0]] + [plane_swap(pieces[at], at, 0) for at in (1, 2, 3)]
        total = call(sum_kernel, piece, terms)
        pair_in = from_partner(pair_out, "gy")
        total, pair_in = lax.optimization_barrier((total, pair_in))
        other = plane_swap(total, 0, 2)
        grad_x = features_grad(pair_in)
        total, grad_x = lax.optimization_barrier((total, grad_x))
        total = call(sum_kernel, piece, [total, other])
        by_x, by_y, by_z = plane_swap(total, 1, 0), plane_swap(total, 2, 0), plane_swap(total, 0, 1)
        by_xy, by_xz = plane_swap(by_y, 1, 0), plane_swap(by_x, 0, 1)
        by_yz, by_xyz = plane_swap(by_z, 2, 0), plane_swap(by_xy, 0, 1)
        weights = call(
            spread_kernel,
            tuple([shape_of((half, width), F32)] * 4),
            [total, by_z, by_x, by_xz, by_y, by_yz, by_xy, by_xyz],
        )
    else:
        grad_x = features_grad(from_partner(pair_out, "gy"))
        terms = pieces[0].astype(F32)
        stacked = jnp.zeros((4, width, width), F32)
        for base, at in ((0, 0), (1, 1), (2, 2)):
            for side in range(2):
                tile = terms[:, (base * 2 + side) * PART : (base * 2 + side + 1) * PART]
                stacked = lax.dynamic_update_slice(
                    stacked, tile[None], (at, z_bit * half, side * half + y_bit * PART)
                )
        tile = terms[:, 6 * PART :].reshape(4, 2, 32, half)
        tile = tile.transpose(0, 2, 1, 3).reshape(PART, width)
        stacked = lax.dynamic_update_slice(
            stacked, tile[None], (3, z_bit * half + y_bit * PART, 0)
        )
        stacked = lax.psum(stacked, ("gx", "gy", "gz"))
        held_rows = w_query.shape[0]
        stacked = lax.dynamic_slice_in_dim(stacked, lax.axis_index("gz") * held_rows, held_rows, 1)
        weights = [stacked[at] for at in range(4)]
    return (grad_x, *weights)


def solution(mesh):
    return jax.shard_map(
        on_device,
        mesh=mesh,
        in_specs=(
            P("gx", "gy", "gz", None),
            P("gx", "gy", "gz", None),
            P("gx", "gy", "gz", None),
            P("gz", None),
            P("gz", None),
            P("gz", None),
            P("gz", None),
        ),
        out_specs=(
            P("gx", "gy", "gz", None),
            P("gz", None),
            P("gz", None),
            P("gz", None),
            P("gz", None),
        ),
        check_vma=False,
    )
```

```python
import functools
import math

import jax
import jax.numpy as jnp
from jax import lax
from jax.experimental import pallas as pl
from jax.experimental.pallas import tpu as pltpu
from jax.sharding import PartitionSpec as P

HEADS = 8
PART = 128
BF = jnp.bfloat16
F32 = jnp.float32
VMEM_BYTES = 32 * 1024 * 1024


def from_partner(block, axis):
    route = [(index, index ^ 1) for index in range(lax.axis_size(axis))]
    return lax.ppermute(block, axis, route)


def shifted(value, axis, steps):
    count = lax.axis_size(axis)
    return lax.ppermute(value, axis, [(source, (source + steps) % count) for source in range(count)])


def plane_swap(value, flip_x, flip_y):
    count_x, count_y = lax.axis_size("gx"), lax.axis_size("gy")
    route = []
    for at_x in range(count_x):
        for at_y in range(count_y):
            route.append((at_x * count_y + at_y, (at_x ^ flip_x) * count_y + (at_y ^ flip_y)))
    return lax.ppermute(value, ("gx", "gy"), route)


def dot_nn(left, right):
    return lax.dot_general(left, right, (((1,), (0,)), ((), ())), preferred_element_type=F32)


def dot_nt(left, right):
    return lax.dot_general(left, right, (((1,), (1,)), ((), ())), preferred_element_type=F32)


def dot_tn(left, right):
    return lax.dot_general(left, right, (((0,), (0,)), ((), ())), preferred_element_type=F32)


def columns(start):
    return pl.ds(pl.multiple_of(start, PART), PART)


def call(kernel, out_shape, args, scratch=(), flops=1e6, moved=1e6, exps=0, spaces=None):
    specs = [pl.BlockSpec(memory_space=space or pltpu.VMEM) for space in spaces or [None] * len(args)]
    return pl.pallas_call(
        kernel,
        out_shape=out_shape,
        in_specs=specs,
        scratch_shapes=list(scratch),
        compiler_params=pltpu.CompilerParams(vmem_limit_bytes=VMEM_BYTES),
        cost_estimate=pl.CostEstimate(
            flops=int(flops), bytes_accessed=int(moved), transcendentals=int(exps)
        ),
    )(*args)


def shape_of(dims, dtype=BF):
    return jax.ShapeDtypeStruct(dims, dtype)


def pack_kernel(dy_ref, saved_ref, pair_ref, own_ref, saved_s):
    y_bit = lax.axis_index("gy") % 2
    z_bit = lax.axis_index("gz") % 2
    tokens = pair_ref.shape[0]
    width = dy_ref.shape[-1]
    last = PART + width
    dys = dy_ref[...].reshape(tokens, width)
    saved_s[...] = saved_ref[...].reshape(tokens, width)
    for out in (pair_ref, own_ref):
        out[:, PART:last] = dys
    pair_ref[:, 0:PART] = saved_s[:, columns((z_bit * 2 + 1 - y_bit) * PART)]
    pair_ref[:, last:] = saved_s[:, columns(((1 - z_bit) * 2 + 1 - y_bit) * PART)]
    own_ref[:, 0:PART] = saved_s[:, columns(((1 - z_bit) * 2 + y_bit) * PART)]
    own_ref[:, last:] = saved_s[:, columns((z_bit * 2 + y_bit) * PART)]


def columns_kernel(own_half, wq0, wq1, wk0, wk1, wv0, wv1, w_cols):
    y_bit = lax.axis_index("gy") % 2
    z_bit = lax.axis_index("gz") % 2
    half = z_bit if own_half else z_bit * 0
    group = columns((z_bit * 2 + y_bit) * PART)
    half_rows = wq0.shape[0]
    for at, (first, second) in enumerate(((wq0, wq1), (wk0, wk1), (wv0, wv1))):
        spot = slice(at * PART, (at + 1) * PART)
        w_cols[pl.ds(pl.multiple_of(half * half_rows, half_rows), half_rows), spot] = first[:, group]
        w_cols[pl.ds(pl.multiple_of((1 - half) * half_rows, half_rows), half_rows), spot] = second[:, group]


def project_kernel(own, core, pair, far, w_cols, q_ref, kv_ref):
    width = own.shape[1]
    for at, source in enumerate((own, core, pair, far)):
        rows = slice(at * PART, (at + 1) * PART)
        made = dot_nn(source[...], w_cols[...])
        q_ref[rows, :] = made[:, 0:PART].astype(BF) * jnp.asarray(1.0 / math.sqrt(width // HEADS), BF)
        kv_ref[rows, :] = made[:, PART:].astype(BF)


def early_kernel(
    f_own, f_core, f_pair, f_far, own, core, pair, far, wout,
    do_ref, delta_ref, feat_t_ref, o_ref, saved, dys,
):
    y_bit = lax.axis_index("gy") % 2
    z_bit = lax.axis_index("gz") % 2
    width = f_own.shape[1]
    half = width // 2
    last = PART + width
    for at, (source, spot) in enumerate(((own, last), (core, 0), (pair, 0), (far, last))):
        rows = slice(at * PART, (at + 1) * PART)
        saved[rows, :] = source[:, spot : spot + PART]
        dys[rows, :] = source[:, PART:last]
    for at, source in enumerate((f_own, f_core, f_pair, f_far)):
        wanted = source[:, pl.ds(pl.multiple_of(z_bit * half, PART), half)]
        feat_t_ref[:, at * PART : (at + 1) * PART] = wanted.astype(F32).T.astype(BF)
    w_rows = wout[pl.ds(pl.multiple_of(y_bit * PART, PART), PART), :]
    out_grad = dot_nt(dys[...], w_rows).astype(BF)
    do_ref[...] = out_grad
    head_dim = width // HEADS
    products = (out_grad.astype(F32) * saved[...].astype(F32)).T
    delta_ref[0:1, :] = jnp.sum(products[0:head_dim], axis=0, keepdims=True)
    delta_ref[1:2, :] = jnp.sum(products[head_dim:PART], axis=0, keepdims=True)
    out = dot_nn(saved[...].astype(F32).T.astype(BF), dys[...]).astype(BF)
    for at in range(4):
        low = out[at * 32 : (at + 1) * 32, :]
        o_ref[at * 64 : at * 64 + 32, :] = low[:, 0:half]
        o_ref[at * 64 + 32 : at * 64 + 64, :] = low[:, half:]


def by_head(value):
    low = lax.broadcasted_iota(jnp.int32, value.shape, 1) < PART // 2
    none = jnp.zeros_like(value)
    return (jnp.where(low, value, none), jnp.where(low, none, value))


def row_scale(table, at, tokens):
    low = lax.broadcasted_iota(jnp.int32, (tokens, PART), 1) < PART // 2
    return jnp.where(low, table[:, 2 * at : 2 * at + 1], table[:, 2 * at + 1 : 2 * at + 2])


def score_kernel(q_ref, do_ref, delta_ref, *refs):
    count = len(refs) - 3
    e_ref, ds_ref, table_ref = refs[count:]
    half = table_ref.shape[0] // 2
    q_heads = by_head(q_ref[...])
    g_heads = by_head(do_ref[...])
    delta = delta_ref[...]
    if half > 2 * count:
        table_ref[...] = jnp.zeros_like(table_ref)
    for at in range(count):
        keys = refs[at][:, 0:PART]
        values = refs[at][:, PART:]
        for head in range(2):
            scores = dot_nt(keys, q_heads[head])
            top = jnp.max(scores, axis=0, keepdims=True)
            grown = jnp.exp(scores - top)
            row = 2 * at + head
            rounded = grown.astype(BF)
            e_ref[row] = rounded
            dprob = dot_nt(values, g_heads[head])
            ds_ref[row] = (rounded.astype(F32) * (dprob - delta[head : head + 1, :])).astype(BF)
            table_ref[row : row + 1, :] = top
            table_ref[half + row : half + row + 1, :] = jnp.sum(grown, axis=0, keepdims=True)


def gradient_kernel(times, groups, q_ref, do_ref, *refs):
    count = len(times)
    e_refs, ds_refs, tables = (refs[at : 3 * len(groups) : 3] for at in range(3))
    refs = refs[3 * len(groups) :]
    part_s, outs = refs[0], refs[1:]
    where = [(group, at) for group, blocks in enumerate(groups) for at in range(blocks)]
    if part_s.shape[0] > 2 * count:
        part_s[...] = jnp.zeros_like(part_s)
    for head in range(2):
        tops, totals = [], []
        for group, at in where:
            half = tables[group].shape[0] // 2
            row = 2 * at + head
            tops.append(tables[group][row : row + 1, :])
            totals.append(tables[group][half + row : half + row + 1, :])
        most = functools.reduce(jnp.maximum, tops)
        lifts = [jnp.exp(top - most) for top in tops]
        total = functools.reduce(
            jnp.add, [time * lift * part for time, lift, part in zip(times, lifts, totals)]
        )
        for at in range(count):
            part_s[2 * at + head : 2 * at + head + 1, :] = lifts[at] / total
    turned = part_s[...].T
    for at, (group, place) in enumerate(where):
        if at > 0:
            block_partials(turned, at, place, q_ref, do_ref, e_refs[group], ds_refs[group], outs[at - 1])


def block_partials(turned, at, place, q_ref, do_ref, e_ref, ds_ref, out_ref):
    scale = row_scale(turned, at, q_ref.shape[0])
    q_scaled = by_head((q_ref[...].astype(F32) * scale).astype(BF))
    g_scaled = by_head((do_ref[...].astype(F32) * scale).astype(BF))
    dks, dvs = [], []
    for head in range(2):
        dvs.append(dot_nn(e_ref[2 * place + head], g_scaled[head]))
        dks.append(dot_nn(ds_ref[2 * place + head], q_scaled[head]))
    out_ref[:, 0:PART] = (dks[0] + dks[1]).astype(BF)
    out_ref[:, PART:] = (dvs[0] + dvs[1]).astype(BF)


def query_kernel(times, groups, part_ref, q_ref, do_ref, e_ref, *refs):
    ds_refs, kvs = refs[: len(groups)], refs[len(groups) : -3]
    dq_ref, own_ref, dq_s = refs[-3:]
    block_partials(part_ref[...].T, 0, 0, q_ref, do_ref, e_ref, ds_refs[0], own_ref)
    head_dim = PART // 2
    where = [(group, at) for group, blocks in enumerate(groups) for at in range(blocks)]
    for at, (group, place) in enumerate(where):
        keys_t = kvs[at][:, 0:PART].astype(F32).T.astype(BF)
        for head in range(2):
            spot = slice(head * head_dim, (head + 1) * head_dim)
            part = part_ref[2 * at + head : 2 * at + head + 1, :] * times[at]
            added = dot_nn(keys_t[spot, :], ds_refs[group][2 * place + head]) * part
            dq_s[spot, :] = added if at == 0 else dq_s[spot, :] + added
    dq_ref[...] = (dq_s[...].T * (1.0 / math.sqrt(head_dim))).astype(BF)


def collect_kernel(times, dq_ref, *refs):
    total = times[0] * refs[0][...].astype(F32)
    for time, ref in zip(times[1:], refs[1:-1]):
        total = total + time * ref[...].astype(F32)
    refs[-1][:, 0:PART] = dq_ref[...]
    refs[-1][:, PART:] = total.astype(BF)


def place_grads(grads, own, core, count):
    z_bit = lax.axis_index("gz") % 2
    for at in range(count):
        source = slice(at * PART, (at + 1) * PART)
        grads[:, columns(at * 2 * PART + z_bit * PART)] = own[:, source]
        core_at = columns(at * 2 * PART + (1 - z_bit) * PART)
        for low in range(4):
            grads[low * PART : (low + 1) * PART, core_at] = core[
                (low ^ 1) * PART : ((low ^ 1) + 1) * PART, source
            ]


def weight_kernel(chunks, own, core, feat_t, o_ref, pair_ref, mine_ref, *refs):
    outs, (grads, made) = refs[:chunks], refs[chunks:]
    place_grads(grads, own, core, 3)
    mine_ref[...] = grads[0:PART, :]
    pair_ref[...] = grads[2 * PART : 3 * PART, :]
    wide = grads.shape[1]
    made[:, 0:wide] = dot_nn(feat_t[...], grads[...]).astype(BF)
    made[:, wide:] = o_ref[...]
    rows = made.shape[0] // chunks
    for at in range(chunks):
        spot = pl.ds(0, rows)
        if chunks > 1:
            spot = pl.ds(pl.multiple_of((lax.axis_index("gx") ^ at) * rows, rows), rows)
        outs[at][...] = made[spot, :]


def grad_x_kernel(own_half, mine, pair, wq0, wq1, wk0, wk1, wv0, wv1, out, full, made):
    y_bit = lax.axis_index("gy") % 2
    z_bit = lax.axis_index("gz") % 2
    half = z_bit if own_half else z_bit * 0
    width = wq0.shape[1]
    half_rows = wq0.shape[0]
    for at in range(3):
        for side in range(2):
            spot = slice((at * 2 + side) * PART, (at * 2 + side + 1) * PART)
            base = at * width + side * 2 * PART
            full[:, columns(base + y_bit * PART)] = mine[:, spot]
            full[:, columns(base + (1 - y_bit) * PART)] = pair[:, spot]
    for at, sources in ((half, (wq0, wk0, wv0)), (1 - half, (wq1, wk1, wv1))):
        total = functools.reduce(
            jnp.add,
            [dot_nt(full[:, n * width : (n + 1) * width], sources[n][...]) for n in range(3)],
        )
        made[:, pl.ds(pl.multiple_of(at * half_rows, PART), half_rows)] = total.astype(BF)
    out[...] = made[...].reshape(out.shape)


def sum_kernel(*refs):
    total = refs[0][...].astype(F32)
    for ref in refs[1:-1]:
        total = total + ref[...].astype(F32)
    refs[-1][...] = total.astype(BF)


def spread_kernel(*refs):
    pieces, outs = refs[:8], refs[8:]
    half = 2 * PART
    rows = pieces[0].shape[0]
    for at, piece in enumerate(pieces):
        place = lax.axis_index("gx") ^ (at // 2)
        bit = (lax.axis_index("gy") % 2) ^ (at % 2)
        spot = pl.ds(pl.multiple_of(place * rows, rows), rows)
        for base, out in enumerate(outs[:3]):
            for side in range(2):
                source = slice((base * 2 + side) * PART, (base * 2 + side + 1) * PART)
                out[spot, columns(side * half + bit * PART)] = piece[:, source].astype(F32)
        spot = pl.ds(pl.multiple_of(bit * PART + place * (rows // 2), rows // 2), rows // 2)
        outs[3][spot, 0:half] = piece[0 : rows // 2, 3 * half :].astype(F32)
        outs[3][spot, half:] = piece[rows // 2 :, 3 * half :].astype(F32)


def on_device(features, grad_y, attn_out, w_query, w_key, w_value, w_out):
    width = features.shape[-1]
    half = width // 2
    tokens = features.shape[0] * features.shape[1] * features.shape[2]
    block_tokens = 4 * tokens
    count_x, count_y, count_z = lax.axis_size("gx"), lax.axis_size("gy"), lax.axis_size("gz")
    z_bit = lax.axis_index("gz") % 2
    y_bit = lax.axis_index("gy") % 2

    own_half = count_z == 2
    if own_half:
        pairs = []
        for weight in (w_query, w_key, w_value):
            pairs += [weight, from_partner(weight, "gz")]
        out_rows = w_out
    else:
        pairs = []
        for weight in (w_query, w_key, w_value):
            whole = lax.all_gather(weight, "gz", axis=0, tiled=True)
            pairs += [whole[:half], whole[half:]]
        whole = lax.all_gather(w_out, "gz", axis=0, tiled=True)
        out_rows = lax.dynamic_slice_in_dim(whole, z_bit * half, half, 0)

    message = shape_of((tokens, width + 2 * PART))
    feat = features.reshape(tokens, width)
    feat_pair = from_partner(feat, "gy")
    feat_core = from_partner(feat, "gz")
    w_cols = call(
        functools.partial(columns_kernel, own_half),
        shape_of((width, 3 * PART)),
        pairs,
    )
    feat_pair, feat_core, w_cols = lax.optimization_barrier((feat_pair, feat_core, w_cols))
    feat_far = from_partner(feat_pair, "gz")
    feats = [feat, feat_core, feat_pair, feat_far]
    column = shape_of((block_tokens, PART))
    both = shape_of((block_tokens, 2 * PART))
    query, own_kv = call(
        project_kernel,
        (column, both),
        [*feats, w_cols],
        flops=2 * block_tokens * width * 3 * PART,
    )

    times = [1.0]
    routes = []
    for axis, step, blocks in (("gx", 1, count_x), ("gy", 2, count_y // 2), ("gz", 2, count_z // 2)):
        if blocks == 1:
            times[0] += 2.0
        elif blocks == 2:
            routes.append((axis, step))
            times.append(2.0)
        else:
            routes += [(axis, step), (axis, -step)]
            times += [1.0, 1.0]
    times = tuple(times)
    count = len(times)
    near = [own_kv] + [shifted(own_kv, axis, step) for axis, step in routes]
    late_dy, late_saved, query = lax.optimization_barrier((grad_y, attn_out, query))
    pair_message, own = call(
        pack_kernel,
        (message, message),
        [late_dy, late_saved],
        scratch=[pltpu.VMEM((tokens, width), BF)],
    )
    pair = from_partner(pair_message, "gy")
    core = from_partner(own, "gz")
    far = from_partner(pair, "gz")
    out_grad, delta, feat_t, out_term = call(
        early_kernel,
        (
            column,
            shape_of((2, block_tokens), F32),
            shape_of((half, block_tokens)),
            shape_of((half, half)),
        ),
        [*feats, own, core, pair, far, out_rows],
        scratch=[pltpu.VMEM((block_tokens, PART), BF), pltpu.VMEM((block_tokens, width), BF)],
        flops=4 * block_tokens * width * PART,
    )
    pixels = 2 * block_tokens * block_tokens
    groups = (2, count - 2)
    scored = []
    place = 0
    for blocks in groups:
        rows = -(-2 * blocks // 8) * 8
        scored += call(
            score_kernel,
            (
                shape_of((2 * blocks, block_tokens, block_tokens)),
                shape_of((2 * blocks, block_tokens, block_tokens)),
                shape_of((2 * rows, block_tokens), F32),
            ),
            [query, out_grad, delta, *near[place : place + blocks]],
            flops=4 * pixels * blocks * PART,
            moved=4 * pixels * blocks,
            exps=pixels * blocks,
        )
        place += blocks
    table = shape_of((-(-2 * count // 8) * 8, block_tokens), F32)
    parts, *partials = call(
        functools.partial(gradient_kernel, times, groups),
        (table, *[both] * (count - 1)),
        [query, out_grad, *scored],
        flops=4 * pixels * count * PART,
        moved=4 * pixels * count,
    )
    dq, own_partial = call(
        functools.partial(query_kernel, times, groups),
        (column, both),
        [parts, query, out_grad, scored[0], *scored[1::3], *near],
        scratch=[pltpu.VMEM((PART, block_tokens), F32)],
        flops=2 * pixels * count * PART,
        moved=2 * pixels * count,
    )
    back = []
    for partial, (axis, step) in reversed(list(zip(partials, routes))):
        back.append(shifted(partial, axis, -step))
    back.append(own_partial)
    grads = call(
        functools.partial(collect_kernel, times[::-1]), shape_of((block_tokens, 3 * PART)), [dq, *back]
    )
    core_grads = from_partner(grads, "gz")
    planned = count_x == 4 and count_y == 4 and count_z == 2
    chunks = 4 if planned else 1
    piece = shape_of((half // chunks, 8 * PART))
    pair_out, mine, *pieces = call(
        functools.partial(weight_kernel, chunks),
        (shape_of((tokens, 6 * PART)), shape_of((tokens, 6 * PART)), *[piece] * chunks),
        [grads, core_grads, feat_t, out_term],
        scratch=[pltpu.VMEM((block_tokens, 6 * PART), BF), pltpu.VMEM((half, 8 * PART), BF)],
        flops=2 * block_tokens * half * 6 * PART,
    )
    def features_grad(pair_rows):
        return call(
            functools.partial(grad_x_kernel, own_half),
            shape_of(features.shape),
            [mine, pair_rows, *pairs],
            scratch=[pltpu.VMEM((tokens, 3 * width), BF), pltpu.VMEM((tokens, width), BF)],
            flops=2 * tokens * 3 * width * width,
        )

    if planned:
        terms = [pieces[0]] + [plane_swap(pieces[at], at, 0) for at in (1, 2, 3)]
        total = call(sum_kernel, piece, terms)
        pair_in = from_partner(pair_out, "gy")
        total, pair_in = lax.optimization_barrier((total, pair_in))
        other = plane_swap(total, 0, 2)
        grad_x = features_grad(pair_in)
        total, grad_x = lax.optimization_barrier((total, grad_x))
        total = call(sum_kernel, piece, [total, other])
        by_x, by_y, by_z = plane_swap(total, 1, 0), plane_swap(total, 2, 0), plane_swap(total, 0, 1)
        by_xy, by_xz = plane_swap(by_y, 1, 0), plane_swap(by_x, 0, 1)
        by_yz, by_xyz = plane_swap(by_z, 2, 0), plane_swap(by_xy, 0, 1)
        weights = call(
            spread_kernel,
            tuple([shape_of((half, width), F32)] * 4),
            [total, by_z, by_x, by_xz, by_y, by_yz, by_xy, by_xyz],
        )
    else:
        grad_x = features_grad(from_partner(pair_out, "gy"))
        terms = pieces[0].astype(F32)
        stacked = jnp.zeros((4, width, width), F32)
        for base, at in ((0, 0), (1, 1), (2, 2)):
            for side in range(2):
                tile = terms[:, (base * 2 + side) * PART : (base * 2 + side + 1) * PART]
                stacked = lax.dynamic_update_slice(
                    stacked, tile[None], (at, z_bit * half, side * half + y_bit * PART)
                )
        tile = terms[:, 6 * PART :].reshape(4, 2, 32, half)
        tile = tile.transpose(0, 2, 1, 3).reshape(PART, width)
        stacked = lax.dynamic_update_slice(
            stacked, tile[None], (3, z_bit * half + y_bit * PART, 0)
        )
        stacked = lax.psum(stacked, ("gx", "gy", "gz"))
        held_rows = w_query.shape[0]
        stacked = lax.dynamic_slice_in_dim(stacked, lax.axis_index("gz") * held_rows, held_rows, 1)
        weights = [stacked[at] for at in range(4)]
    return (grad_x, *weights)


def solution(mesh):
    return jax.shard_map(
        on_device,
        mesh=mesh,
        in_specs=(
            P("gx", "gy", "gz", None),
            P("gx", "gy", "gz", None),
            P("gx", "gy", "gz", None),
            P("gz", None),
            P("gz", None),
            P("gz", None),
            P("gz", None),
        ),
        out_specs=(
            P("gx", "gy", "gz", None),
            P("gz", None),
            P("gz", None),
            P("gz", None),
            P("gz", None),
        ),
        check_vma=False,
    )
```

```python
import functools
import math

import jax
import jax.numpy as jnp
from jax import lax
from jax.experimental import pallas as pl
from jax.experimental.pallas import tpu as pltpu
from jax.sharding import PartitionSpec as P

HEADS = 8
PART = 128
BF = jnp.bfloat16
F32 = jnp.float32
VMEM_BYTES = 32 * 1024 * 1024


def from_partner(block, axis):
    route = [(index, index ^ 1) for index in range(lax.axis_size(axis))]
    return lax.ppermute(block, axis, route)


def shifted(value, axis, steps):
    count = lax.axis_size(axis)
    return lax.ppermute(value, axis, [(source, (source + steps) % count) for source in range(count)])


def plane_swap(value, flip_x, flip_y):
    count_x, count_y = lax.axis_size("gx"), lax.axis_size("gy")
    route = []
    for at_x in range(count_x):
        for at_y in range(count_y):
            route.append((at_x * count_y + at_y, (at_x ^ flip_x) * count_y + (at_y ^ flip_y)))
    return lax.ppermute(value, ("gx", "gy"), route)


def dot_nn(left, right):
    return lax.dot_general(left, right, (((1,), (0,)), ((), ())), preferred_element_type=F32)


def dot_nt(left, right):
    return lax.dot_general(left, right, (((1,), (1,)), ((), ())), preferred_element_type=F32)


def dot_tn(left, right):
    return lax.dot_general(left, right, (((0,), (0,)), ((), ())), preferred_element_type=F32)


def columns(start):
    return pl.ds(pl.multiple_of(start, PART), PART)


def call(kernel, out_shape, args, scratch=(), flops=1e6, moved=1e6, exps=0, spaces=None):
    specs = [pl.BlockSpec(memory_space=space or pltpu.VMEM) for space in spaces or [None] * len(args)]
    return pl.pallas_call(
        kernel,
        out_shape=out_shape,
        in_specs=specs,
        scratch_shapes=list(scratch),
        compiler_params=pltpu.CompilerParams(vmem_limit_bytes=VMEM_BYTES),
        cost_estimate=pl.CostEstimate(
            flops=int(flops), bytes_accessed=int(moved), transcendentals=int(exps)
        ),
    )(*args)


def shape_of(dims, dtype=BF):
    return jax.ShapeDtypeStruct(dims, dtype)


def pack_kernel(dy_ref, saved_ref, pair_ref, own_ref, saved_s):
    y_bit = lax.axis_index("gy") % 2
    z_bit = lax.axis_index("gz") % 2
    tokens = pair_ref.shape[0]
    width = dy_ref.shape[-1]
    last = PART + width
    dys = dy_ref[...].reshape(tokens, width)
    saved_s[...] = saved_ref[...].reshape(tokens, width)
    for out in (pair_ref, own_ref):
        out[:, PART:last] = dys
    pair_ref[:, 0:PART] = saved_s[:, columns((z_bit * 2 + 1 - y_bit) * PART)]
    pair_ref[:, last:] = saved_s[:, columns(((1 - z_bit) * 2 + 1 - y_bit) * PART)]
    own_ref[:, 0:PART] = saved_s[:, columns(((1 - z_bit) * 2 + y_bit) * PART)]
    own_ref[:, last:] = saved_s[:, columns((z_bit * 2 + y_bit) * PART)]


def columns_kernel(own_half, wq0, wq1, wk0, wk1, wv0, wv1, w_cols):
    y_bit = lax.axis_index("gy") % 2
    z_bit = lax.axis_index("gz") % 2
    half = z_bit if own_half else z_bit * 0
    group = columns((z_bit * 2 + y_bit) * PART)
    half_rows = wq0.shape[0]
    for at, (first, second) in enumerate(((wq0, wq1), (wk0, wk1), (wv0, wv1))):
        spot = slice(at * PART, (at + 1) * PART)
        w_cols[pl.ds(pl.multiple_of(half * half_rows, half_rows), half_rows), spot] = first[:, group]
        w_cols[pl.ds(pl.multiple_of((1 - half) * half_rows, half_rows), half_rows), spot] = second[:, group]


def project_kernel(own, core, pair, far, w_cols, q_ref, kv_ref):
    width = own.shape[1]
    for at, source in enumerate((own, core, pair, far)):
        rows = slice(at * PART, (at + 1) * PART)
        made = dot_nn(source[...], w_cols[...])
        q_ref[rows, :] = made[:, 0:PART].astype(BF) * jnp.asarray(1.0 / math.sqrt(width // HEADS), BF)
        kv_ref[rows, :] = made[:, PART:].astype(BF)


def early_kernel(
    f_own, f_core, f_pair, f_far, own, core, pair, far, wout,
    do_ref, delta_ref, feat_t_ref, o_ref, saved, dys,
):
    y_bit = lax.axis_index("gy") % 2
    z_bit = lax.axis_index("gz") % 2
    width = f_own.shape[1]
    half = width // 2
    last = PART + width
    for at, (source, spot) in enumerate(((own, last), (core, 0), (pair, 0), (far, last))):
        rows = slice(at * PART, (at + 1) * PART)
        saved[rows, :] = source[:, spot : spot + PART]
        dys[rows, :] = source[:, PART:last]
    for at, source in enumerate((f_own, f_core, f_pair, f_far)):
        wanted = source[:, pl.ds(pl.multiple_of(z_bit * half, PART), half)]
        feat_t_ref[:, at * PART : (at + 1) * PART] = wanted.astype(F32).T.astype(BF)
    w_rows = wout[pl.ds(pl.multiple_of(y_bit * PART, PART), PART), :]
    out_grad = dot_nt(dys[...], w_rows).astype(BF)
    do_ref[...] = out_grad
    head_dim = width // HEADS
    products = (out_grad.astype(F32) * saved[...].astype(F32)).T
    delta_ref[0:1, :] = jnp.sum(products[0:head_dim], axis=0, keepdims=True)
    delta_ref[1:2, :] = jnp.sum(products[head_dim:PART], axis=0, keepdims=True)
    out = dot_nn(saved[...].astype(F32).T.astype(BF), dys[...]).astype(BF)
    for at in range(4):
        low = out[at * 32 : (at + 1) * 32, :]
        o_ref[at * 64 : at * 64 + 32, :] = low[:, 0:half]
        o_ref[at * 64 + 32 : at * 64 + 64, :] = low[:, half:]


def by_head(value):
    low = lax.broadcasted_iota(jnp.int32, value.shape, 1) < PART // 2
    none = jnp.zeros_like(value)
    return (jnp.where(low, value, none), jnp.where(low, none, value))


def row_scale(table, at, tokens):
    low = lax.broadcasted_iota(jnp.int32, (tokens, PART), 1) < PART // 2
    return jnp.where(low, table[:, 2 * at : 2 * at + 1], table[:, 2 * at + 1 : 2 * at + 2])


def score_kernel(q_ref, do_ref, delta_ref, *refs):
    count = len(refs) - 3
    e_ref, ds_ref, table_ref = refs[count:]
    half = table_ref.shape[0] // 2
    q_heads = by_head(q_ref[...])
    g_heads = by_head(do_ref[...])
    delta = delta_ref[...]
    if half > 2 * count:
        table_ref[...] = jnp.zeros_like(table_ref)
    for at in range(count):
        keys = refs[at][:, 0:PART]
        values = refs[at][:, PART:]
        for head in range(2):
            scores = dot_nt(keys, q_heads[head])
            top = jnp.max(scores, axis=0, keepdims=True)
            grown = jnp.exp(scores - top)
            row = 2 * at + head
            rounded = grown.astype(BF)
            e_ref[row] = rounded
            dprob = dot_nt(values, g_heads[head])
            ds_ref[row] = (rounded.astype(F32) * (dprob - delta[head : head + 1, :])).astype(BF)
            table_ref[row : row + 1, :] = top
            table_ref[half + row : half + row + 1, :] = jnp.sum(grown, axis=0, keepdims=True)


def gradient_kernel(times, groups, q_ref, do_ref, *refs):
    count = len(times)
    e_refs, ds_refs, tables = (refs[at : 3 * len(groups) : 3] for at in range(3))
    refs = refs[3 * len(groups) :]
    part_s, outs = refs[0], refs[1:]
    where = [(group, at) for group, blocks in enumerate(groups) for at in range(blocks)]
    if part_s.shape[0] > 2 * count:
        part_s[...] = jnp.zeros_like(part_s)
    for head in range(2):
        tops, totals = [], []
        for group, at in where:
            half = tables[group].shape[0] // 2
            row = 2 * at + head
            tops.append(tables[group][row : row + 1, :])
            totals.append(tables[group][half + row : half + row + 1, :])
        most = functools.reduce(jnp.maximum, tops)
        lifts = [jnp.exp(top - most) for top in tops]
        total = functools.reduce(
            jnp.add, [time * lift * part for time, lift, part in zip(times, lifts, totals)]
        )
        for at in range(count):
            part_s[2 * at + head : 2 * at + head + 1, :] = lifts[at] / total
    turned = part_s[...].T
    for at, (group, place) in enumerate(where):
        if at > 0:
            block_partials(turned, at, place, q_ref, do_ref, e_refs[group], ds_refs[group], outs[at - 1])


def block_partials(turned, at, place, q_ref, do_ref, e_ref, ds_ref, out_ref):
    scale = row_scale(turned, at, q_ref.shape[0])
    q_scaled = by_head((q_ref[...].astype(F32) * scale).astype(BF))
    g_scaled = by_head((do_ref[...].astype(F32) * scale).astype(BF))
    dks, dvs = [], []
    for head in range(2):
        dvs.append(dot_nn(e_ref[2 * place + head], g_scaled[head]))
        dks.append(dot_nn(ds_ref[2 * place + head], q_scaled[head]))
    out_ref[:, 0:PART] = (dks[0] + dks[1]).astype(BF)
    out_ref[:, PART:] = (dvs[0] + dvs[1]).astype(BF)


def query_kernel(times, groups, part_ref, q_ref, do_ref, e_ref, *refs):
    ds_refs, kvs = refs[: len(groups)], refs[len(groups) : -3]
    dq_ref, own_ref, dq_s = refs[-3:]
    block_partials(part_ref[...].T, 0, 0, q_ref, do_ref, e_ref, ds_refs[0], own_ref)
    head_dim = PART // 2
    where = [(group, at) for group, blocks in enumerate(groups) for at in range(blocks)]
    for at, (group, place) in enumerate(where):
        keys_t = kvs[at][:, 0:PART].astype(F32).T.astype(BF)
        for head in range(2):
            spot = slice(head * head_dim, (head + 1) * head_dim)
            part = part_ref[2 * at + head : 2 * at + head + 1, :] * times[at]
            added = dot_nn(keys_t[spot, :], ds_refs[group][2 * place + head]) * part
            dq_s[spot, :] = added if at == 0 else dq_s[spot, :] + added
    dq_ref[...] = (dq_s[...].T * (1.0 / math.sqrt(head_dim))).astype(BF)


def collect_kernel(times, dq_ref, *refs):
    total = times[0] * refs[0][...].astype(F32)
    for time, ref in zip(times[1:], refs[1:-1]):
        total = total + time * ref[...].astype(F32)
    refs[-1][:, 0:PART] = dq_ref[...]
    refs[-1][:, PART:] = total.astype(BF)


def place_grads(grads, own, core, count):
    z_bit = lax.axis_index("gz") % 2
    for at in range(count):
        source = slice(at * PART, (at + 1) * PART)
        grads[:, columns(at * 2 * PART + z_bit * PART)] = own[:, source]
        core_at = columns(at * 2 * PART + (1 - z_bit) * PART)
        for low in range(4):
            grads[low * PART : (low + 1) * PART, core_at] = core[
                (low ^ 1) * PART : ((low ^ 1) + 1) * PART, source
            ]


def weight_kernel(chunks, own, core, feat_t, o_ref, pair_ref, mine_ref, *refs):
    outs, (grads, made) = refs[:chunks], refs[chunks:]
    place_grads(grads, own, core, 3)
    mine_ref[...] = grads[0:PART, :]
    pair_ref[...] = grads[2 * PART : 3 * PART, :]
    wide = grads.shape[1]
    made[:, 0:wide] = dot_nn(feat_t[...], grads[...]).astype(BF)
    made[:, wide:] = o_ref[...]
    rows = made.shape[0] // chunks
    for at in range(chunks):
        spot = pl.ds(0, rows)
        if chunks > 1:
            spot = pl.ds(pl.multiple_of((lax.axis_index("gx") ^ at) * rows, rows), rows)
        outs[at][...] = made[spot, :]


def grad_x_kernel(own_half, mine, pair, wq0, wq1, wk0, wk1, wv0, wv1, out, full, made):
    y_bit = lax.axis_index("gy") % 2
    z_bit = lax.axis_index("gz") % 2
    half = z_bit if own_half else z_bit * 0
    width = wq0.shape[1]
    half_rows = wq0.shape[0]
    for at in range(3):
        for side in range(2):
            spot = slice((at * 2 + side) * PART, (at * 2 + side + 1) * PART)
            base = at * width + side * 2 * PART
            full[:, columns(base + y_bit * PART)] = mine[:, spot]
            full[:, columns(base + (1 - y_bit) * PART)] = pair[:, spot]
    for at, sources in ((half, (wq0, wk0, wv0)), (1 - half, (wq1, wk1, wv1))):
        total = functools.reduce(
            jnp.add,
            [dot_nt(full[:, n * width : (n + 1) * width], sources[n][...]) for n in range(3)],
        )
        made[:, pl.ds(pl.multiple_of(at * half_rows, PART), half_rows)] = total.astype(BF)
    out[...] = made[...].reshape(out.shape)


def sum_kernel(*refs):
    total = refs[0][...].astype(F32)
    for ref in refs[1:-1]:
        total = total + ref[...].astype(F32)
    refs[-1][...] = total.astype(BF)


def spread_kernel(*refs):
    pieces, outs = refs[:8], refs[8:]
    half = 2 * PART
    rows = pieces[0].shape[0]
    for at, piece in enumerate(pieces):
        place = lax.axis_index("gx") ^ (at // 2)
        bit = (lax.axis_index("gy") % 2) ^ (at % 2)
        spot = pl.ds(pl.multiple_of(place * rows, rows), rows)
        for base, out in enumerate(outs[:3]):
            for side in range(2):
                source = slice((base * 2 + side) * PART, (base * 2 + side + 1) * PART)
                out[spot, columns(side * half + bit * PART)] = piece[:, source].astype(F32)
        spot = pl.ds(pl.multiple_of(bit * PART + place * (rows // 2), rows // 2), rows // 2)
        outs[3][spot, 0:half] = piece[0 : rows // 2, 3 * half :].astype(F32)
        outs[3][spot, half:] = piece[rows // 2 :, 3 * half :].astype(F32)


def on_device(features, grad_y, attn_out, w_query, w_key, w_value, w_out):
    width = features.shape[-1]
    half = width // 2
    tokens = features.shape[0] * features.shape[1] * features.shape[2]
    block_tokens = 4 * tokens
    count_x, count_y, count_z = lax.axis_size("gx"), lax.axis_size("gy"), lax.axis_size("gz")
    z_bit = lax.axis_index("gz") % 2
    y_bit = lax.axis_index("gy") % 2

    own_half = count_z == 2
    if own_half:
        pairs = []
        for weight in (w_query, w_key, w_value):
            pairs += [weight, from_partner(weight, "gz")]
        out_rows = w_out
    else:
        pairs = []
        for weight in (w_query, w_key, w_value):
            whole = lax.all_gather(weight, "gz", axis=0, tiled=True)
            pairs += [whole[:half], whole[half:]]
        whole = lax.all_gather(w_out, "gz", axis=0, tiled=True)
        out_rows = lax.dynamic_slice_in_dim(whole, z_bit * half, half, 0)

    message = shape_of((tokens, width + 2 * PART))
    feat = features.reshape(tokens, width)
    feat_pair = from_partner(feat, "gy")
    feat_core = from_partner(feat, "gz")
    w_cols = call(
        functools.partial(columns_kernel, own_half),
        shape_of((width, 3 * PART)),
        pairs,
    )
    feat_pair, feat_core, w_cols = lax.optimization_barrier((feat_pair, feat_core, w_cols))
    feat_far = from_partner(feat_pair, "gz")
    feats = [feat, feat_core, feat_pair, feat_far]
    column = shape_of((block_tokens, PART))
    both = shape_of((block_tokens, 2 * PART))
    query, own_kv = call(
        project_kernel,
        (column, both),
        [*feats, w_cols],
        flops=2 * block_tokens * width * 3 * PART,
    )

    times = [1.0]
    routes = []
    for axis, step, blocks in (("gx", 1, count_x), ("gy", 2, count_y // 2), ("gz", 2, count_z // 2)):
        if blocks == 1:
            times[0] += 2.0
        elif blocks == 2:
            routes.append((axis, step))
            times.append(2.0)
        else:
            routes += [(axis, step), (axis, -step)]
            times += [1.0, 1.0]
    times = tuple(times)
    count = len(times)
    near = [own_kv] + [shifted(own_kv, axis, step) for axis, step in routes]
    late_dy, late_saved, query = lax.optimization_barrier((grad_y, attn_out, query))
    pair_message, own = call(
        pack_kernel,
        (message, message),
        [late_dy, late_saved],
        scratch=[pltpu.VMEM((tokens, width), BF)],
    )
    pair = from_partner(pair_message, "gy")
    core = from_partner(own, "gz")
    far = from_partner(pair, "gz")
    out_grad, delta, feat_t, out_term = call(
        early_kernel,
        (
            column,
            shape_of((2, block_tokens), F32),
            shape_of((half, block_tokens)),
            shape_of((half, half)),
        ),
        [*feats, own, core, pair, far, out_rows],
        scratch=[pltpu.VMEM((block_tokens, PART), BF), pltpu.VMEM((block_tokens, width), BF)],
        flops=4 * block_tokens * width * PART,
    )
    pixels = 2 * block_tokens * block_tokens
    groups = (2, count - 2)
    scored = []
    place = 0
    for blocks in groups:
        rows = -(-2 * blocks // 8) * 8
        scored += call(
            score_kernel,
            (
                shape_of((2 * blocks, block_tokens, block_tokens)),
                shape_of((2 * blocks, block_tokens, block_tokens)),
                shape_of((2 * rows, block_tokens), F32),
            ),
            [query, out_grad, delta, *near[place : place + blocks]],
            flops=4 * pixels * blocks * PART,
            moved=4 * pixels * blocks,
            exps=pixels * blocks,
        )
        place += blocks
    table = shape_of((-(-2 * count // 8) * 8, block_tokens), F32)
    parts, *partials = call(
        functools.partial(gradient_kernel, times, groups),
        (table, *[both] * (count - 1)),
        [query, out_grad, *scored],
        flops=4 * pixels * count * PART,
        moved=4 * pixels * count,
    )
    dq, own_partial = call(
        functools.partial(query_kernel, times, groups),
        (column, both),
        [parts, query, out_grad, scored[0], *scored[1::3], *near],
        scratch=[pltpu.VMEM((PART, block_tokens), F32)],
        flops=2 * pixels * count * PART,
        moved=2 * pixels * count,
    )
    back = []
    for partial, (axis, step) in reversed(list(zip(partials, routes))):
        back.append(shifted(partial, axis, -step))
    back.append(own_partial)
    grads = call(
        functools.partial(collect_kernel, times[::-1]), shape_of((block_tokens, 3 * PART)), [dq, *back]
    )
    core_grads = from_partner(grads, "gz")
    planned = count_x == 4 and count_y == 4 and count_z == 2
    chunks = 4 if planned else 1
    piece = shape_of((half // chunks, 8 * PART))
    pair_out, mine, *pieces = call(
        functools.partial(weight_kernel, chunks),
        (shape_of((tokens, 6 * PART)), shape_of((tokens, 6 * PART)), *[piece] * chunks),
        [grads, core_grads, feat_t, out_term],
        scratch=[pltpu.VMEM((block_tokens, 6 * PART), BF), pltpu.VMEM((half, 8 * PART), BF)],
        flops=2 * block_tokens * half * 6 * PART,
    )
    def features_grad(pair_rows):
        return call(
            functools.partial(grad_x_kernel, own_half),
            shape_of(features.shape),
            [mine, pair_rows, *pairs],
            scratch=[pltpu.VMEM((tokens, 3 * width), BF), pltpu.VMEM((tokens, width), BF)],
            flops=2 * tokens * 3 * width * width,
        )

    if planned:
        terms = [pieces[0]] + [plane_swap(pieces[at], at, 0) for at in (1, 2, 3)]
        total = call(sum_kernel, piece, terms)
        pair_in = from_partner(pair_out, "gy")
        other = plane_swap(total, 0, 2)
        grad_x = features_grad(pair_in)
        total = call(sum_kernel, piece, [total, other])
        by_x, by_y, by_z = plane_swap(total, 1, 0), plane_swap(total, 2, 0), plane_swap(total, 0, 1)
        by_xy, by_xz = plane_swap(by_y, 1, 0), plane_swap(by_x, 0, 1)
        by_yz, by_xyz = plane_swap(by_z, 2, 0), plane_swap(by_xy, 0, 1)
        weights = call(
            spread_kernel,
            tuple([shape_of((half, width), F32)] * 4),
            [total, by_z, by_x, by_xz, by_y, by_yz, by_xy, by_xyz],
        )
    else:
        grad_x = features_grad(from_partner(pair_out, "gy"))
        terms = pieces[0].astype(F32)
        stacked = jnp.zeros((4, width, width), F32)
        for base, at in ((0, 0), (1, 1), (2, 2)):
            for side in range(2):
                tile = terms[:, (base * 2 + side) * PART : (base * 2 + side + 1) * PART]
                stacked = lax.dynamic_update_slice(
                    stacked, tile[None], (at, z_bit * half, side * half + y_bit * PART)
                )
        tile = terms[:, 6 * PART :].reshape(4, 2, 32, half)
        tile = tile.transpose(0, 2, 1, 3).reshape(PART, width)
        stacked = lax.dynamic_update_slice(
            stacked, tile[None], (3, z_bit * half + y_bit * PART, 0)
        )
        stacked = lax.psum(stacked, ("gx", "gy", "gz"))
        held_rows = w_query.shape[0]
        stacked = lax.dynamic_slice_in_dim(stacked, lax.axis_index("gz") * held_rows, held_rows, 1)
        weights = [stacked[at] for at in range(4)]
    return (grad_x, *weights)


def solution(mesh):
    return jax.shard_map(
        on_device,
        mesh=mesh,
        in_specs=(
            P("gx", "gy", "gz", None),
            P("gx", "gy", "gz", None),
            P("gx", "gy", "gz", None),
            P("gz", None),
            P("gz", None),
            P("gz", None),
            P("gz", None),
        ),
        out_specs=(
            P("gx", "gy", "gz", None),
            P("gz", None),
            P("gz", None),
            P("gz", None),
            P("gz", None),
        ),
        check_vma=False,
    )
```

```python
import functools
import math

import jax
import jax.numpy as jnp
from jax import lax
from jax.experimental import pallas as pl
from jax.experimental.pallas import tpu as pltpu
from jax.sharding import PartitionSpec as P

HEADS = 8
PART = 128
BF = jnp.bfloat16
F32 = jnp.float32
VMEM_BYTES = 32 * 1024 * 1024


def from_partner(block, axis):
    route = [(index, index ^ 1) for index in range(lax.axis_size(axis))]
    return lax.ppermute(block, axis, route)


def shifted(value, axis, steps):
    count = lax.axis_size(axis)
    return lax.ppermute(value, axis, [(source, (source + steps) % count) for source in range(count)])


def plane_swap(value, flip_x, flip_y):
    count_x, count_y = lax.axis_size("gx"), lax.axis_size("gy")
    route = []
    for at_x in range(count_x):
        for at_y in range(count_y):
            route.append((at_x * count_y + at_y, (at_x ^ flip_x) * count_y + (at_y ^ flip_y)))
    return lax.ppermute(value, ("gx", "gy"), route)


def dot_nn(left, right):
    return lax.dot_general(left, right, (((1,), (0,)), ((), ())), preferred_element_type=F32)


def dot_nt(left, right):
    return lax.dot_general(left, right, (((1,), (1,)), ((), ())), preferred_element_type=F32)


def dot_tn(left, right):
    return lax.dot_general(left, right, (((0,), (0,)), ((), ())), preferred_element_type=F32)


def columns(start):
    return pl.ds(pl.multiple_of(start, PART), PART)


def call(kernel, out_shape, args, scratch=(), flops=1e6, moved=1e6, exps=0, spaces=None):
    specs = [pl.BlockSpec(memory_space=space or pltpu.VMEM) for space in spaces or [None] * len(args)]
    return pl.pallas_call(
        kernel,
        out_shape=out_shape,
        in_specs=specs,
        scratch_shapes=list(scratch),
        compiler_params=pltpu.CompilerParams(vmem_limit_bytes=VMEM_BYTES),
        cost_estimate=pl.CostEstimate(
            flops=int(flops), bytes_accessed=int(moved), transcendentals=int(exps)
        ),
    )(*args)


def shape_of(dims, dtype=BF):
    return jax.ShapeDtypeStruct(dims, dtype)


def pack_kernel(dy_ref, saved_ref, pair_ref, own_ref, saved_s):
    y_bit = lax.axis_index("gy") % 2
    z_bit = lax.axis_index("gz") % 2
    tokens = pair_ref.shape[0]
    width = dy_ref.shape[-1]
    last = PART + width
    dys = dy_ref[...].reshape(tokens, width)
    saved_s[...] = saved_ref[...].reshape(tokens, width)
    for out in (pair_ref, own_ref):
        out[:, PART:last] = dys
    pair_ref[:, 0:PART] = saved_s[:, columns((z_bit * 2 + 1 - y_bit) * PART)]
    pair_ref[:, last:] = saved_s[:, columns(((1 - z_bit) * 2 + 1 - y_bit) * PART)]
    own_ref[:, 0:PART] = saved_s[:, columns(((1 - z_bit) * 2 + y_bit) * PART)]
    own_ref[:, last:] = saved_s[:, columns((z_bit * 2 + y_bit) * PART)]


def columns_kernel(own_half, wq0, wq1, wk0, wk1, wv0, wv1, w_cols):
    y_bit = lax.axis_index("gy") % 2
    z_bit = lax.axis_index("gz") % 2
    half = z_bit if own_half else z_bit * 0
    group = columns((z_bit * 2 + y_bit) * PART)
    half_rows = wq0.shape[0]
    for at, (first, second) in enumerate(((wq0, wq1), (wk0, wk1), (wv0, wv1))):
        spot = slice(at * PART, (at + 1) * PART)
        w_cols[pl.ds(pl.multiple_of(half * half_rows, half_rows), half_rows), spot] = first[:, group]
        w_cols[pl.ds(pl.multiple_of((1 - half) * half_rows, half_rows), half_rows), spot] = second[:, group]


def project_kernel(own, core, pair, far, w_cols, q_ref, kv_ref):
    width = own.shape[1]
    for at, source in enumerate((own, core, pair, far)):
        rows = slice(at * PART, (at + 1) * PART)
        made = dot_nn(source[...], w_cols[...])
        q_ref[rows, :] = made[:, 0:PART].astype(BF) * jnp.asarray(1.0 / math.sqrt(width // HEADS), BF)
        kv_ref[rows, :] = made[:, PART:].astype(BF)


def early_kernel(
    f_own, f_core, f_pair, f_far, own, core, pair, far, wout,
    do_ref, delta_ref, feat_t_ref, o_ref, saved, dys,
):
    y_bit = lax.axis_index("gy") % 2
    z_bit = lax.axis_index("gz") % 2
    width = f_own.shape[1]
    half = width // 2
    last = PART + width
    for at, (source, spot) in enumerate(((own, last), (core, 0), (pair, 0), (far, last))):
        rows = slice(at * PART, (at + 1) * PART)
        saved[rows, :] = source[:, spot : spot + PART]
        dys[rows, :] = source[:, PART:last]
    for at, source in enumerate((f_own, f_core, f_pair, f_far)):
        wanted = source[:, pl.ds(pl.multiple_of(z_bit * half, PART), half)]
        feat_t_ref[:, at * PART : (at + 1) * PART] = wanted.astype(F32).T.astype(BF)
    w_rows = wout[pl.ds(pl.multiple_of(y_bit * PART, PART), PART), :]
    out_grad = dot_nt(dys[...], w_rows).astype(BF)
    do_ref[...] = out_grad
    head_dim = width // HEADS
    products = (out_grad.astype(F32) * saved[...].astype(F32)).T
    delta_ref[0:1, :] = jnp.sum(products[0:head_dim], axis=0, keepdims=True)
    delta_ref[1:2, :] = jnp.sum(products[head_dim:PART], axis=0, keepdims=True)
    out = dot_nn(saved[...].astype(F32).T.astype(BF), dys[...]).astype(BF)
    for at in range(4):
        low = out[at * 32 : (at + 1) * 32, :]
        o_ref[at * 64 : at * 64 + 32, :] = low[:, 0:half]
        o_ref[at * 64 + 32 : at * 64 + 64, :] = low[:, half:]


def by_head(value):
    low = lax.broadcasted_iota(jnp.int32, value.shape, 1) < PART // 2
    none = jnp.zeros_like(value)
    return (jnp.where(low, value, none), jnp.where(low, none, value))


def row_scale(table, at, tokens):
    low = lax.broadcasted_iota(jnp.int32, (tokens, PART), 1) < PART // 2
    return jnp.where(low, table[:, 2 * at : 2 * at + 1], table[:, 2 * at + 1 : 2 * at + 2])


def score_kernel(q_ref, do_ref, delta_ref, *refs):
    count = len(refs) - 3
    e_ref, ds_ref, table_ref = refs[count:]
    half = table_ref.shape[0] // 2
    q_heads = by_head(q_ref[...])
    g_heads = by_head(do_ref[...])
    delta = delta_ref[...]
    if half > 2 * count:
        table_ref[...] = jnp.zeros_like(table_ref)
    for at in range(count):
        keys = refs[at][:, 0:PART]
        values = refs[at][:, PART:]
        for head in range(2):
            scores = dot_nt(keys, q_heads[head])
            top = jnp.max(scores, axis=0, keepdims=True)
            grown = jnp.exp(scores - top)
            row = 2 * at + head
            rounded = grown.astype(BF)
            e_ref[row] = rounded
            dprob = dot_nt(values, g_heads[head])
            ds_ref[row] = (rounded.astype(F32) * (dprob - delta[head : head + 1, :])).astype(BF)
            table_ref[row : row + 1, :] = top
            table_ref[half + row : half + row + 1, :] = jnp.sum(grown, axis=0, keepdims=True)


def gradient_kernel(times, groups, q_ref, do_ref, *refs):
    count = len(times)
    e_refs, ds_refs, tables = (refs[at : 3 * len(groups) : 3] for at in range(3))
    refs = refs[3 * len(groups) :]
    part_s, outs = refs[0], refs[1:]
    where = [(group, at) for group, blocks in enumerate(groups) for at in range(blocks)]
    if part_s.shape[0] > 2 * count:
        part_s[...] = jnp.zeros_like(part_s)
    for head in range(2):
        tops, totals = [], []
        for group, at in where:
            half = tables[group].shape[0] // 2
            row = 2 * at + head
            tops.append(tables[group][row : row + 1, :])
            totals.append(tables[group][half + row : half + row + 1, :])
        most = functools.reduce(jnp.maximum, tops)
        lifts = [jnp.exp(top - most) for top in tops]
        total = functools.reduce(
            jnp.add, [time * lift * part for time, lift, part in zip(times, lifts, totals)]
        )
        for at in range(count):
            part_s[2 * at + head : 2 * at + head + 1, :] = lifts[at] / total
    turned = part_s[...].T
    for at, (group, place) in enumerate(where):
        if at > 0:
            block_partials(turned, at, place, q_ref, do_ref, e_refs[group], ds_refs[group], outs[at - 1])


def block_partials(turned, at, place, q_ref, do_ref, e_ref, ds_ref, out_ref):
    scale = row_scale(turned, at, q_ref.shape[0])
    q_scaled = by_head((q_ref[...].astype(F32) * scale).astype(BF))
    g_scaled = by_head((do_ref[...].astype(F32) * scale).astype(BF))
    dks, dvs = [], []
    for head in range(2):
        dvs.append(dot_nn(e_ref[2 * place + head], g_scaled[head]))
        dks.append(dot_nn(ds_ref[2 * place + head], q_scaled[head]))
    out_ref[:, 0:PART] = (dks[0] + dks[1]).astype(BF)
    out_ref[:, PART:] = (dvs[0] + dvs[1]).astype(BF)


def query_kernel(times, groups, part_ref, q_ref, do_ref, e_ref, *refs):
    ds_refs, kvs = refs[: len(groups)], refs[len(groups) : -3]
    dq_ref, own_ref, dq_s = refs[-3:]
    block_partials(part_ref[...].T, 0, 0, q_ref, do_ref, e_ref, ds_refs[0], own_ref)
    head_dim = PART // 2
    where = [(group, at) for group, blocks in enumerate(groups) for at in range(blocks)]
    for at, (group, place) in enumerate(where):
        keys_t = kvs[at][:, 0:PART].astype(F32).T.astype(BF)
        for head in range(2):
            spot = slice(head * head_dim, (head + 1) * head_dim)
            part = part_ref[2 * at + head : 2 * at + head + 1, :] * times[at]
            added = dot_nn(keys_t[spot, :], ds_refs[group][2 * place + head]) * part
            dq_s[spot, :] = added if at == 0 else dq_s[spot, :] + added
    dq_ref[...] = (dq_s[...].T * (1.0 / math.sqrt(head_dim))).astype(BF)


def collect_kernel(times, dq_ref, *refs):
    out_ref, pair_ref = refs[-2:]
    total = times[0] * refs[0][...].astype(F32)
    for time, ref in zip(times[1:], refs[1:-2]):
        total = total + time * ref[...].astype(F32)
    out_ref[:, 0:PART] = dq_ref[...]
    out_ref[:, PART:] = total.astype(BF)
    pair_ref[...] = out_ref[2 * PART :, :]


def place_grads(grads, own, core, count):
    z_bit = lax.axis_index("gz") % 2
    for at in range(count):
        source = slice(at * PART, (at + 1) * PART)
        grads[:, columns(at * 2 * PART + z_bit * PART)] = own[:, source]
        core_at = columns(at * 2 * PART + (1 - z_bit) * PART)
        for low in range(4):
            grads[low * PART : (low + 1) * PART, core_at] = core[
                (low ^ 1) * PART : ((low ^ 1) + 1) * PART, source
            ]


def weight_kernel(chunks, own, core, feat_t, o_ref, *refs):
    outs, (grads, made) = refs[:chunks], refs[chunks:]
    place_grads(grads, own, core, 3)
    wide = grads.shape[1]
    made[:, 0:wide] = dot_nn(feat_t[...], grads[...]).astype(BF)
    made[:, wide:] = o_ref[...]
    rows = made.shape[0] // chunks
    for at in range(chunks):
        spot = pl.ds(0, rows)
        if chunks > 1:
            spot = pl.ds(pl.multiple_of((lax.axis_index("gx") ^ at) * rows, rows), rows)
        outs[at][...] = made[spot, :]


def grad_x_kernel(own_half, own, core, pair, far, wq0, wq1, wk0, wk1, wv0, wv1, out, full, made):
    y_bit = lax.axis_index("gy") % 2
    z_bit = lax.axis_index("gz") % 2
    half = z_bit if own_half else z_bit * 0
    width = wq0.shape[1]
    half_rows = wq0.shape[0]
    sources = (
        (own, 0, z_bit, y_bit), (core, 1, 1 - z_bit, y_bit),
        (pair, 0, z_bit, 1 - y_bit), (far, 1, 1 - z_bit, 1 - y_bit),
    )
    for at in range(3):
        spot = slice(at * PART, (at + 1) * PART)
        for source, part, z_at, y_at in sources:
            full[:, columns(at * width + z_at * 2 * PART + y_at * PART)] = source[
                part * PART : (part + 1) * PART, spot
            ]
    for at, sources in ((half, (wq0, wk0, wv0)), (1 - half, (wq1, wk1, wv1))):
        total = functools.reduce(
            jnp.add,
            [dot_nt(full[:, n * width : (n + 1) * width], sources[n][...]) for n in range(3)],
        )
        made[:, pl.ds(pl.multiple_of(at * half_rows, PART), half_rows)] = total.astype(BF)
    out[...] = made[...].reshape(out.shape)


def sum_kernel(*refs):
    total = refs[0][...].astype(F32)
    for ref in refs[1:-1]:
        total = total + ref[...].astype(F32)
    refs[-1][...] = total.astype(BF)


def spread_kernel(*refs):
    pieces, outs = refs[:8], refs[8:]
    half = 2 * PART
    rows = pieces[0].shape[0]
    for at, piece in enumerate(pieces):
        place = lax.axis_index("gx") ^ (at // 2)
        bit = (lax.axis_index("gy") % 2) ^ (at % 2)
        spot = pl.ds(pl.multiple_of(place * rows, rows), rows)
        for base, out in enumerate(outs[:3]):
            for side in range(2):
                source = slice((base * 2 + side) * PART, (base * 2 + side + 1) * PART)
                out[spot, columns(side * half + bit * PART)] = piece[:, source].astype(F32)
        spot = pl.ds(pl.multiple_of(bit * PART + place * (rows // 2), rows // 2), rows // 2)
        outs[3][spot, 0:half] = piece[0 : rows // 2, 3 * half :].astype(F32)
        outs[3][spot, half:] = piece[rows // 2 :, 3 * half :].astype(F32)


def on_device(features, grad_y, attn_out, w_query, w_key, w_value, w_out):
    width = features.shape[-1]
    half = width // 2
    tokens = features.shape[0] * features.shape[1] * features.shape[2]
    block_tokens = 4 * tokens
    count_x, count_y, count_z = lax.axis_size("gx"), lax.axis_size("gy"), lax.axis_size("gz")
    z_bit = lax.axis_index("gz") % 2
    y_bit = lax.axis_index("gy") % 2

    own_half = count_z == 2
    if own_half:
        pairs = []
        for weight in (w_query, w_key, w_value):
            pairs += [weight, from_partner(weight, "gz")]
        out_rows = w_out
    else:
        pairs = []
        for weight in (w_query, w_key, w_value):
            whole = lax.all_gather(weight, "gz", axis=0, tiled=True)
            pairs += [whole[:half], whole[half:]]
        whole = lax.all_gather(w_out, "gz", axis=0, tiled=True)
        out_rows = lax.dynamic_slice_in_dim(whole, z_bit * half, half, 0)

    message = shape_of((tokens, width + 2 * PART))
    feat = features.reshape(tokens, width)
    feat_pair = from_partner(feat, "gy")
    feat_core = from_partner(feat, "gz")
    w_cols = call(
        functools.partial(columns_kernel, own_half),
        shape_of((width, 3 * PART)),
        pairs,
    )
    feat_pair, feat_core, w_cols = lax.optimization_barrier((feat_pair, feat_core, w_cols))
    feat_far = from_partner(feat_pair, "gz")
    feats = [feat, feat_core, feat_pair, feat_far]
    column = shape_of((block_tokens, PART))
    both = shape_of((block_tokens, 2 * PART))
    query, own_kv = call(
        project_kernel,
        (column, both),
        [*feats, w_cols],
        flops=2 * block_tokens * width * 3 * PART,
    )

    times = [1.0]
    routes = []
    for axis, step, blocks in (("gx", 1, count_x), ("gy", 2, count_y // 2), ("gz", 2, count_z // 2)):
        if blocks == 1:
            times[0] += 2.0
        elif blocks == 2:
            routes.append((axis, step))
            times.append(2.0)
        else:
            routes += [(axis, step), (axis, -step)]
            times += [1.0, 1.0]
    times = tuple(times)
    count = len(times)
    near = [own_kv] + [shifted(own_kv, axis, step) for axis, step in routes]
    late_dy, late_saved, query = lax.optimization_barrier((grad_y, attn_out, query))
    pair_message, own = call(
        pack_kernel,
        (message, message),
        [late_dy, late_saved],
        scratch=[pltpu.VMEM((tokens, width), BF)],
    )
    pair = from_partner(pair_message, "gy")
    core = from_partner(own, "gz")
    far = from_partner(pair, "gz")
    out_grad, delta, feat_t, out_term = call(
        early_kernel,
        (
            column,
            shape_of((2, block_tokens), F32),
            shape_of((half, block_tokens)),
            shape_of((half, half)),
        ),
        [*feats, own, core, pair, far, out_rows],
        scratch=[pltpu.VMEM((block_tokens, PART), BF), pltpu.VMEM((block_tokens, width), BF)],
        flops=4 * block_tokens * width * PART,
    )
    pixels = 2 * block_tokens * block_tokens
    groups = (2, count - 2)
    scored = []
    place = 0
    for blocks in groups:
        rows = -(-2 * blocks // 8) * 8
        scored += call(
            score_kernel,
            (
                shape_of((2 * blocks, block_tokens, block_tokens)),
                shape_of((2 * blocks, block_tokens, block_tokens)),
                shape_of((2 * rows, block_tokens), F32),
            ),
            [query, out_grad, delta, *near[place : place + blocks]],
            flops=4 * pixels * blocks * PART,
            moved=4 * pixels * blocks,
            exps=pixels * blocks,
        )
        place += blocks
    table = shape_of((-(-2 * count // 8) * 8, block_tokens), F32)
    parts, *partials = call(
        functools.partial(gradient_kernel, times, groups),
        (table, *[both] * (count - 1)),
        [query, out_grad, *scored],
        flops=4 * pixels * count * PART,
        moved=4 * pixels * count,
    )
    dq, own_partial = call(
        functools.partial(query_kernel, times, groups),
        (column, both),
        [parts, query, out_grad, scored[0], *scored[1::3], *near],
        scratch=[pltpu.VMEM((PART, block_tokens), F32)],
        flops=2 * pixels * count * PART,
        moved=2 * pixels * count,
    )
    back = []
    for partial, (axis, step) in reversed(list(zip(partials, routes))):
        back.append(shifted(partial, axis, -step))
    back.append(own_partial)
    grads, pair_out = call(
        functools.partial(collect_kernel, times[::-1]),
        (shape_of((block_tokens, 3 * PART)), shape_of((2 * tokens, 3 * PART))),
        [dq, *back],
    )
    pair_in = from_partner(pair_out, "gy")
    core_grads = from_partner(grads, "gz")
    planned = count_x == 4 and count_y == 4 and count_z == 2
    chunks = 4 if planned else 1
    piece = shape_of((half // chunks, 8 * PART))
    pieces = call(
        functools.partial(weight_kernel, chunks),
        tuple([piece] * chunks),
        [grads, core_grads, feat_t, out_term],
        scratch=[pltpu.VMEM((block_tokens, 6 * PART), BF), pltpu.VMEM((half, 8 * PART), BF)],
        flops=2 * block_tokens * half * 6 * PART,
    )
    def features_grad(far_in):
        return call(
            functools.partial(grad_x_kernel, own_half),
            shape_of(features.shape),
            [grads, core_grads, pair_in, far_in, *pairs],
            scratch=[pltpu.VMEM((tokens, 3 * width), BF), pltpu.VMEM((tokens, width), BF)],
            flops=2 * tokens * 3 * width * width,
        )

    if planned:
        terms = [pieces[0]] + [plane_swap(pieces[at], at, 0) for at in (1, 2, 3)]
        total = call(sum_kernel, piece, terms)
        total, pair_in = lax.optimization_barrier((total, pair_in))
        other = plane_swap(total, 0, 2)
        far_in = from_partner(pair_in, "gz")
        grad_x = features_grad(far_in)
        total, grad_x = lax.optimization_barrier((total, grad_x))
        total = call(sum_kernel, piece, [total, other])
        by_x, by_y, by_z = plane_swap(total, 1, 0), plane_swap(total, 2, 0), plane_swap(total, 0, 1)
        by_xy, by_xz = plane_swap(by_y, 1, 0), plane_swap(by_x, 0, 1)
        by_yz, by_xyz = plane_swap(by_z, 2, 0), plane_swap(by_xy, 0, 1)
        weights = call(
            spread_kernel,
            tuple([shape_of((half, width), F32)] * 4),
            [total, by_z, by_x, by_xz, by_y, by_yz, by_xy, by_xyz],
        )
    else:
        grad_x = features_grad(from_partner(pair_in, "gz"))
        terms = pieces[0].astype(F32)
        stacked = jnp.zeros((4, width, width), F32)
        for base, at in ((0, 0), (1, 1), (2, 2)):
            for side in range(2):
                tile = terms[:, (base * 2 + side) * PART : (base * 2 + side + 1) * PART]
                stacked = lax.dynamic_update_slice(
                    stacked, tile[None], (at, z_bit * half, side * half + y_bit * PART)
                )
        tile = terms[:, 6 * PART :].reshape(4, 2, 32, half)
        tile = tile.transpose(0, 2, 1, 3).reshape(PART, width)
        stacked = lax.dynamic_update_slice(
            stacked, tile[None], (3, z_bit * half + y_bit * PART, 0)
        )
        stacked = lax.psum(stacked, ("gx", "gy", "gz"))
        held_rows = w_query.shape[0]
        stacked = lax.dynamic_slice_in_dim(stacked, lax.axis_index("gz") * held_rows, held_rows, 1)
        weights = [stacked[at] for at in range(4)]
    return (grad_x, *weights)


def solution(mesh):
    return jax.shard_map(
        on_device,
        mesh=mesh,
        in_specs=(
            P("gx", "gy", "gz", None),
            P("gx", "gy", "gz", None),
            P("gx", "gy", "gz", None),
            P("gz", None),
            P("gz", None),
            P("gz", None),
            P("gz", None),
        ),
        out_specs=(
            P("gx", "gy", "gz", None),
            P("gz", None),
            P("gz", None),
            P("gz", None),
            P("gz", None),
        ),
        check_vma=False,
    )
```

```python
import functools
import math

import jax
import jax.numpy as jnp
from jax import lax
from jax.experimental import pallas as pl
from jax.experimental.pallas import tpu as pltpu
from jax.sharding import PartitionSpec as P

HEADS = 8
PART = 128
BF = jnp.bfloat16
F32 = jnp.float32
VMEM_BYTES = 32 * 1024 * 1024


def from_partner(block, axis):
    route = [(index, index ^ 1) for index in range(lax.axis_size(axis))]
    return lax.ppermute(block, axis, route)


def shifted(value, axis, steps):
    count = lax.axis_size(axis)
    return lax.ppermute(value, axis, [(source, (source + steps) % count) for source in range(count)])


def plane_swap(value, flip_x, flip_y):
    count_x, count_y = lax.axis_size("gx"), lax.axis_size("gy")
    route = []
    for at_x in range(count_x):
        for at_y in range(count_y):
            route.append((at_x * count_y + at_y, (at_x ^ flip_x) * count_y + (at_y ^ flip_y)))
    return lax.ppermute(value, ("gx", "gy"), route)


def dot_nn(left, right):
    return lax.dot_general(left, right, (((1,), (0,)), ((), ())), preferred_element_type=F32)


def dot_nt(left, right):
    return lax.dot_general(left, right, (((1,), (1,)), ((), ())), preferred_element_type=F32)


def dot_tn(left, right):
    return lax.dot_general(left, right, (((0,), (0,)), ((), ())), preferred_element_type=F32)


def columns(start):
    return pl.ds(pl.multiple_of(start, PART), PART)


def call(kernel, out_shape, args, scratch=(), flops=1e6, moved=1e6, exps=0, spaces=None):
    specs = [pl.BlockSpec(memory_space=space or pltpu.VMEM) for space in spaces or [None] * len(args)]
    return pl.pallas_call(
        kernel,
        out_shape=out_shape,
        in_specs=specs,
        scratch_shapes=list(scratch),
        compiler_params=pltpu.CompilerParams(vmem_limit_bytes=VMEM_BYTES),
        cost_estimate=pl.CostEstimate(
            flops=int(flops), bytes_accessed=int(moved), transcendentals=int(exps)
        ),
    )(*args)


def shape_of(dims, dtype=BF):
    return jax.ShapeDtypeStruct(dims, dtype)


def pack_kernel(dy_ref, saved_ref, pair_ref, own_ref, saved_s):
    y_bit = lax.axis_index("gy") % 2
    z_bit = lax.axis_index("gz") % 2
    tokens = pair_ref.shape[0]
    width = dy_ref.shape[-1]
    last = PART + width
    dys = dy_ref[...].reshape(tokens, width)
    saved_s[...] = saved_ref[...].reshape(tokens, width)
    for out in (pair_ref, own_ref):
        out[:, PART:last] = dys
    pair_ref[:, 0:PART] = saved_s[:, columns((z_bit * 2 + 1 - y_bit) * PART)]
    pair_ref[:, last:] = saved_s[:, columns(((1 - z_bit) * 2 + 1 - y_bit) * PART)]
    own_ref[:, 0:PART] = saved_s[:, columns(((1 - z_bit) * 2 + y_bit) * PART)]
    own_ref[:, last:] = saved_s[:, columns((z_bit * 2 + y_bit) * PART)]


def columns_kernel(own_half, wq0, wq1, wk0, wk1, wv0, wv1, w_cols):
    y_bit = lax.axis_index("gy") % 2
    z_bit = lax.axis_index("gz") % 2
    half = z_bit if own_half else z_bit * 0
    group = columns((z_bit * 2 + y_bit) * PART)
    half_rows = wq0.shape[0]
    for at, (first, second) in enumerate(((wq0, wq1), (wk0, wk1), (wv0, wv1))):
        spot = slice(at * PART, (at + 1) * PART)
        w_cols[pl.ds(pl.multiple_of(half * half_rows, half_rows), half_rows), spot] = first[:, group]
        w_cols[pl.ds(pl.multiple_of((1 - half) * half_rows, half_rows), half_rows), spot] = second[:, group]


def project_kernel(own, core, pair, far, w_cols, q_ref, kv_ref):
    width = own.shape[1]
    for at, source in enumerate((own, core, pair, far)):
        rows = slice(at * PART, (at + 1) * PART)
        made = dot_nn(source[...], w_cols[...])
        q_ref[rows, :] = made[:, 0:PART].astype(BF) * jnp.asarray(1.0 / math.sqrt(width // HEADS), BF)
        kv_ref[rows, :] = made[:, PART:].astype(BF)


def early_kernel(
    f_own, f_core, f_pair, f_far, own, core, pair, far, wout,
    do_ref, delta_ref, feat_t_ref, o_ref, saved, dys,
):
    y_bit = lax.axis_index("gy") % 2
    z_bit = lax.axis_index("gz") % 2
    width = f_own.shape[1]
    half = width // 2
    last = PART + width
    for at, (source, spot) in enumerate(((own, last), (core, 0), (pair, 0), (far, last))):
        rows = slice(at * PART, (at + 1) * PART)
        saved[rows, :] = source[:, spot : spot + PART]
        dys[rows, :] = source[:, PART:last]
    for at, source in enumerate((f_own, f_core, f_pair, f_far)):
        wanted = source[:, pl.ds(pl.multiple_of(z_bit * half, PART), half)]
        feat_t_ref[:, at * PART : (at + 1) * PART] = wanted.astype(F32).T.astype(BF)
    w_rows = wout[pl.ds(pl.multiple_of(y_bit * PART, PART), PART), :]
    out_grad = dot_nt(dys[...], w_rows).astype(BF)
    do_ref[...] = out_grad
    head_dim = width // HEADS
    products = (out_grad.astype(F32) * saved[...].astype(F32)).T
    delta_ref[0:1, :] = jnp.sum(products[0:head_dim], axis=0, keepdims=True)
    delta_ref[1:2, :] = jnp.sum(products[head_dim:PART], axis=0, keepdims=True)
    out = dot_nn(saved[...].astype(F32).T.astype(BF), dys[...]).astype(BF)
    for at in range(4):
        low = out[at * 32 : (at + 1) * 32, :]
        o_ref[at * 64 : at * 64 + 32, :] = low[:, 0:half]
        o_ref[at * 64 + 32 : at * 64 + 64, :] = low[:, half:]


def by_head(value):
    low = lax.broadcasted_iota(jnp.int32, value.shape, 1) < PART // 2
    none = jnp.zeros_like(value)
    return (jnp.where(low, value, none), jnp.where(low, none, value))


def row_scale(table, at, tokens):
    low = lax.broadcasted_iota(jnp.int32, (tokens, PART), 1) < PART // 2
    return jnp.where(low, table[:, 2 * at : 2 * at + 1], table[:, 2 * at + 1 : 2 * at + 2])


def score_kernel(q_ref, do_ref, delta_ref, *refs):
    count = len(refs) - 3
    e_ref, ds_ref, table_ref = refs[count:]
    half = table_ref.shape[0] // 2
    q_heads = by_head(q_ref[...])
    g_heads = by_head(do_ref[...])
    delta = delta_ref[...]
    if half > 2 * count:
        table_ref[...] = jnp.zeros_like(table_ref)
    for at in range(count):
        keys = refs[at][:, 0:PART]
        values = refs[at][:, PART:]
        for head in range(2):
            scores = dot_nt(keys, q_heads[head])
            top = jnp.max(scores, axis=0, keepdims=True)
            grown = jnp.exp(scores - top)
            row = 2 * at + head
            rounded = grown.astype(BF)
            e_ref[row] = rounded
            dprob = dot_nt(values, g_heads[head])
            ds_ref[row] = (rounded.astype(F32) * (dprob - delta[head : head + 1, :])).astype(BF)
            table_ref[row : row + 1, :] = top
            table_ref[half + row : half + row + 1, :] = jnp.sum(grown, axis=0, keepdims=True)


def gradient_kernel(times, groups, q_ref, do_ref, *refs):
    count = len(times)
    e_refs, ds_refs, tables = (refs[at : 3 * len(groups) : 3] for at in range(3))
    refs = refs[3 * len(groups) :]
    part_s, outs = refs[0], refs[1:]
    where = [(group, at) for group, blocks in enumerate(groups) for at in range(blocks)]
    if part_s.shape[0] > 2 * count:
        part_s[...] = jnp.zeros_like(part_s)
    for head in range(2):
        tops, totals = [], []
        for group, at in where:
            half = tables[group].shape[0] // 2
            row = 2 * at + head
            tops.append(tables[group][row : row + 1, :])
            totals.append(tables[group][half + row : half + row + 1, :])
        most = functools.reduce(jnp.maximum, tops)
        lifts = [jnp.exp(top - most) for top in tops]
        total = functools.reduce(
            jnp.add, [time * lift * part for time, lift, part in zip(times, lifts, totals)]
        )
        for at in range(count):
            part_s[2 * at + head : 2 * at + head + 1, :] = lifts[at] / total
    turned = part_s[...].T
    for at, (group, place) in enumerate(where):
        if at > 0:
            block_partials(turned, at, place, q_ref, do_ref, e_refs[group], ds_refs[group], outs[at - 1])


def block_partials(turned, at, place, q_ref, do_ref, e_ref, ds_ref, out_ref):
    scale = row_scale(turned, at, q_ref.shape[0])
    q_scaled = by_head((q_ref[...].astype(F32) * scale).astype(BF))
    g_scaled = by_head((do_ref[...].astype(F32) * scale).astype(BF))
    dks, dvs = [], []
    for head in range(2):
        dvs.append(dot_nn(e_ref[2 * place + head], g_scaled[head]))
        dks.append(dot_nn(ds_ref[2 * place + head], q_scaled[head]))
    out_ref[:, 0:PART] = (dks[0] + dks[1]).astype(BF)
    out_ref[:, PART:] = (dvs[0] + dvs[1]).astype(BF)


def query_kernel(times, groups, part_ref, q_ref, do_ref, e_ref, *refs):
    ds_refs, kvs = refs[: len(groups)], refs[len(groups) : -3]
    dq_ref, own_ref, dq_s = refs[-3:]
    block_partials(part_ref[...].T, 0, 0, q_ref, do_ref, e_ref, ds_refs[0], own_ref)
    head_dim = PART // 2
    where = [(group, at) for group, blocks in enumerate(groups) for at in range(blocks)]
    for at, (group, place) in enumerate(where):
        keys_t = kvs[at][:, 0:PART].astype(F32).T.astype(BF)
        for head in range(2):
            spot = slice(head * head_dim, (head + 1) * head_dim)
            part = part_ref[2 * at + head : 2 * at + head + 1, :] * times[at]
            added = dot_nn(keys_t[spot, :], ds_refs[group][2 * place + head]) * part
            dq_s[spot, :] = added if at == 0 else dq_s[spot, :] + added
    dq_ref[...] = (dq_s[...].T * (1.0 / math.sqrt(head_dim))).astype(BF)


def collect_kernel(times, dq_ref, *refs):
    total = times[0] * refs[0][...].astype(F32)
    for time, ref in zip(times[1:], refs[1:-1]):
        total = total + time * ref[...].astype(F32)
    refs[-1][:, 0:PART] = dq_ref[...]
    refs[-1][:, PART:] = total.astype(BF)


def place_grads(grads, own, core, count):
    z_bit = lax.axis_index("gz") % 2
    for at in range(count):
        source = slice(at * PART, (at + 1) * PART)
        grads[:, columns(at * 2 * PART + z_bit * PART)] = own[:, source]
        core_at = columns(at * 2 * PART + (1 - z_bit) * PART)
        for low in range(4):
            grads[low * PART : (low + 1) * PART, core_at] = core[
                (low ^ 1) * PART : ((low ^ 1) + 1) * PART, source
            ]


def weight_kernel(chunks, own, core, feat_t, o_ref, pair_ref, mine_ref, *refs):
    outs, (grads, made) = refs[:chunks], refs[chunks:]
    place_grads(grads, own, core, 3)
    mine_ref[...] = grads[0:PART, :]
    pair_ref[...] = grads[2 * PART : 3 * PART, :]
    wide = grads.shape[1]
    made[:, 0:wide] = dot_nn(feat_t[...], grads[...]).astype(BF)
    made[:, wide:] = o_ref[...]
    rows = made.shape[0] // chunks
    for at in range(chunks):
        spot = pl.ds(0, rows)
        if chunks > 1:
            spot = pl.ds(pl.multiple_of((lax.axis_index("gx") ^ at) * rows, rows), rows)
        outs[at][...] = made[spot, :]


def grad_x_kernel(own_half, mine, pair, wq0, wq1, wk0, wk1, wv0, wv1, out, full, made):
    y_bit = lax.axis_index("gy") % 2
    z_bit = lax.axis_index("gz") % 2
    half = z_bit if own_half else z_bit * 0
    width = wq0.shape[1]
    half_rows = wq0.shape[0]
    for at in range(3):
        for side in range(2):
            spot = slice((at * 2 + side) * PART, (at * 2 + side + 1) * PART)
            base = at * width + side * 2 * PART
            full[:, columns(base + y_bit * PART)] = mine[:, spot]
            full[:, columns(base + (1 - y_bit) * PART)] = pair[:, spot]
    for at, sources in ((half, (wq0, wk0, wv0)), (1 - half, (wq1, wk1, wv1))):
        total = functools.reduce(
            jnp.add,
            [dot_nt(full[:, n * width : (n + 1) * width], sources[n][...]) for n in range(3)],
        )
        made[:, pl.ds(pl.multiple_of(at * half_rows, PART), half_rows)] = total.astype(BF)
    out[...] = made[...].reshape(out.shape)


def sum_kernel(*refs):
    total = refs[0][...].astype(F32)
    for ref in refs[1:-1]:
        total = total + ref[...].astype(F32)
    refs[-1][...] = total.astype(BF)


def spread_kernel(*refs):
    pieces, outs = refs[:8], refs[8:]
    half = 2 * PART
    rows = pieces[0].shape[0]
    for at, piece in enumerate(pieces):
        place = lax.axis_index("gx") ^ (at // 2)
        bit = (lax.axis_index("gy") % 2) ^ (at % 2)
        spot = pl.ds(pl.multiple_of(place * rows, rows), rows)
        for base, out in enumerate(outs[:3]):
            for side in range(2):
                source = slice((base * 2 + side) * PART, (base * 2 + side + 1) * PART)
                out[spot, columns(side * half + bit * PART)] = piece[:, source].astype(F32)
        spot = pl.ds(pl.multiple_of(bit * PART + place * (rows // 2), rows // 2), rows // 2)
        outs[3][spot, 0:half] = piece[0 : rows // 2, 3 * half :].astype(F32)
        outs[3][spot, half:] = piece[rows // 2 :, 3 * half :].astype(F32)


def on_device(features, grad_y, attn_out, w_query, w_key, w_value, w_out):
    width = features.shape[-1]
    half = width // 2
    tokens = features.shape[0] * features.shape[1] * features.shape[2]
    block_tokens = 4 * tokens
    count_x, count_y, count_z = lax.axis_size("gx"), lax.axis_size("gy"), lax.axis_size("gz")
    z_bit = lax.axis_index("gz") % 2
    y_bit = lax.axis_index("gy") % 2

    own_half = count_z == 2
    if own_half:
        pairs = []
        for weight in (w_query, w_key, w_value):
            pairs += [weight, from_partner(weight, "gz")]
        out_rows = w_out
    else:
        pairs = []
        for weight in (w_query, w_key, w_value):
            whole = lax.all_gather(weight, "gz", axis=0, tiled=True)
            pairs += [whole[:half], whole[half:]]
        whole = lax.all_gather(w_out, "gz", axis=0, tiled=True)
        out_rows = lax.dynamic_slice_in_dim(whole, z_bit * half, half, 0)

    message = shape_of((tokens, width + 2 * PART))
    feat = features.reshape(tokens, width)
    feat_pair = from_partner(feat, "gy")
    feat_core = from_partner(feat, "gz")
    w_cols = call(
        functools.partial(columns_kernel, own_half),
        shape_of((width, 3 * PART)),
        pairs,
    )
    feat_pair, feat_core, w_cols = lax.optimization_barrier((feat_pair, feat_core, w_cols))
    feat_far = from_partner(feat_pair, "gz")
    feats = [feat, feat_core, feat_pair, feat_far]
    column = shape_of((block_tokens, PART))
    both = shape_of((block_tokens, 2 * PART))
    query, own_kv = call(
        project_kernel,
        (column, both),
        [*feats, w_cols],
        flops=2 * block_tokens * width * 3 * PART,
    )

    times = [1.0]
    routes = []
    for axis, step, blocks in (("gx", 1, count_x), ("gy", 2, count_y // 2), ("gz", 2, count_z // 2)):
        if blocks == 1:
            times[0] += 2.0
        elif blocks == 2:
            routes.append((axis, step))
            times.append(2.0)
        else:
            routes += [(axis, step), (axis, -step)]
            times += [1.0, 1.0]
    times = tuple(times)
    count = len(times)
    near = [own_kv] + [shifted(own_kv, axis, step) for axis, step in routes]
    late_dy, late_saved, query = lax.optimization_barrier((grad_y, attn_out, query))
    pair_message, own = call(
        pack_kernel,
        (message, message),
        [late_dy, late_saved],
        scratch=[pltpu.VMEM((tokens, width), BF)],
    )
    pair = from_partner(pair_message, "gy")
    core = from_partner(own, "gz")
    far = from_partner(pair, "gz")
    out_grad, delta, feat_t, out_term = call(
        early_kernel,
        (
            column,
            shape_of((2, block_tokens), F32),
            shape_of((half, block_tokens)),
            shape_of((half, half)),
        ),
        [*feats, own, core, pair, far, out_rows],
        scratch=[pltpu.VMEM((block_tokens, PART), BF), pltpu.VMEM((block_tokens, width), BF)],
        flops=4 * block_tokens * width * PART,
    )
    pixels = 2 * block_tokens * block_tokens
    groups = (2, count - 2)
    scored = []
    place = 0
    for blocks in groups:
        rows = -(-2 * blocks // 8) * 8
        scored += call(
            score_kernel,
            (
                shape_of((2 * blocks, block_tokens, block_tokens)),
                shape_of((2 * blocks, block_tokens, block_tokens)),
                shape_of((2 * rows, block_tokens), F32),
            ),
            [query, out_grad, delta, *near[place : place + blocks]],
            flops=4 * pixels * blocks * PART,
            moved=4 * pixels * blocks,
            exps=pixels * blocks,
        )
        place += blocks
    table = shape_of((-(-2 * count // 8) * 8, block_tokens), F32)
    parts, *partials = call(
        functools.partial(gradient_kernel, times, groups),
        (table, *[both] * (count - 1)),
        [query, out_grad, *scored],
        flops=4 * pixels * count * PART,
        moved=4 * pixels * count,
    )
    dq, own_partial = call(
        functools.partial(query_kernel, times, groups),
        (column, both),
        [parts, query, out_grad, scored[0], *scored[1::3], *near],
        scratch=[pltpu.VMEM((PART, block_tokens), F32)],
        flops=2 * pixels * count * PART,
        moved=2 * pixels * count,
    )
    back = []
    for partial, (axis, step) in reversed(list(zip(partials, routes))):
        back.append(shifted(partial, axis, -step))
    back.append(own_partial)
    grads = call(
        functools.partial(collect_kernel, times[::-1]), shape_of((block_tokens, 3 * PART)), [dq, *back]
    )
    core_grads = from_partner(grads, "gz")
    planned = count_x == 4 and count_y == 4 and count_z == 2
    chunks = 4 if planned else 1
    piece = shape_of((half // chunks, 8 * PART))
    pair_out, mine, *pieces = call(
        functools.partial(weight_kernel, chunks),
        (shape_of((tokens, 6 * PART)), shape_of((tokens, 6 * PART)), *[piece] * chunks),
        [grads, core_grads, feat_t, out_term],
        scratch=[pltpu.VMEM((block_tokens, 6 * PART), BF), pltpu.VMEM((half, 8 * PART), BF)],
        flops=2 * block_tokens * half * 6 * PART,
    )
    def features_grad(pair_rows):
        return call(
            functools.partial(grad_x_kernel, own_half),
            shape_of(features.shape),
            [mine, pair_rows, *pairs],
            scratch=[pltpu.VMEM((tokens, 3 * width), BF), pltpu.VMEM((tokens, width), BF)],
            flops=2 * tokens * 3 * width * width,
        )

    if planned:
        terms = [pieces[0]] + [plane_swap(pieces[at], at, 0) for at in (1, 2, 3)]
        total = call(sum_kernel, piece, terms)
        pair_in = from_partner(pair_out, "gy")
        total, pair_in = lax.optimization_barrier((total, pair_in))
        other = plane_swap(total, 0, 2)
        grad_x = features_grad(pair_in)
        total, grad_x = lax.optimization_barrier((total, grad_x))
        total = call(sum_kernel, piece, [total, other])
        by_x, by_y, by_z = plane_swap(total, 1, 0), plane_swap(total, 2, 0), plane_swap(total, 0, 1)
        by_xy, by_xz = plane_swap(by_y, 1, 0), plane_swap(by_z, 1, 0)
        by_yz, by_xyz = plane_swap(by_z, 2, 0), plane_swap(by_xy, 0, 1)
        weights = call(
            spread_kernel,
            tuple([shape_of((half, width), F32)] * 4),
            [total, by_z, by_x, by_xz, by_y, by_yz, by_xy, by_xyz],
        )
    else:
        grad_x = features_grad(from_partner(pair_out, "gy"))
        terms = pieces[0].astype(F32)
        stacked = jnp.zeros((4, width, width), F32)
        for base, at in ((0, 0), (1, 1), (2, 2)):
            for side in range(2):
                tile = terms[:, (base * 2 + side) * PART : (base * 2 + side + 1) * PART]
                stacked = lax.dynamic_update_slice(
                    stacked, tile[None], (at, z_bit * half, side * half + y_bit * PART)
                )
        tile = terms[:, 6 * PART :].reshape(4, 2, 32, half)
        tile = tile.transpose(0, 2, 1, 3).reshape(PART, width)
        stacked = lax.dynamic_update_slice(
            stacked, tile[None], (3, z_bit * half + y_bit * PART, 0)
        )
        stacked = lax.psum(stacked, ("gx", "gy", "gz"))
        held_rows = w_query.shape[0]
        stacked = lax.dynamic_slice_in_dim(stacked, lax.axis_index("gz") * held_rows, held_rows, 1)
        weights = [stacked[at] for at in range(4)]
    return (grad_x, *weights)


def solution(mesh):
    return jax.shard_map(
        on_device,
        mesh=mesh,
        in_specs=(
            P("gx", "gy", "gz", None),
            P("gx", "gy", "gz", None),
            P("gx", "gy", "gz", None),
            P("gz", None),
            P("gz", None),
            P("gz", None),
            P("gz", None),
        ),
        out_specs=(
            P("gx", "gy", "gz", None),
            P("gz", None),
            P("gz", None),
            P("gz", None),
            P("gz", None),
        ),
        check_vma=False,
    )
```
